128 devices in a mesh: fsdp: 16 (over x, y), replica: 8 (over z, core).
Axes of the slice: x: 4, y: 4, z: 4, core: 2. Of those that a mesh axis runs over, the one named last changes fastest.
Arguments:
- grads: bfloat16 [8, 6144, 6144], P('replica', 'fsdp'), may hold values from -80 to 80
- errors: bfloat16 [8, 6144, 6144], P('replica', 'fsdp'), may hold values from -1.25 to 1.25
- q_start: float32 [6144, 128], P('fsdp'), may hold values from -0.078125 to 0.078125
- clip_rms: float32 [], replicated, may hold values from 1.5 to 2.5
Outputs:
- new_errors: bfloat16 [8, 6144, 6144], P('replica', 'fsdp')
- p_basis: float32 [6144, 128], P('fsdp')
- q_out: float32 [6144, 128], P('fsdp')
The draws below stay inside these ranges and needn't reach their ends.
All inputs are finite; a program needn't handle non-finite values.
Results may differ from the reference program's by a relative error of at most 0.02.
Values may be sent and summed in bfloat16 or wider, within the bound.
A program may use at most 64 MiB of HBM per device.

```python
import math
import jax
import jax.numpy as jnp
from jax import lax

D = 6144
RANK = 128
N_REPLICA = 8


def draw_grads(key, part):
    key = jax.random.fold_in(key, 11)
    keys = jax.random.split(key, 4)
    positions = jnp.arange(D, dtype=jnp.float32) / D
    replicas = jnp.arange(N_REPLICA, dtype=jnp.float32) / max(N_REPLICA - 1, 1)
    values = jnp.clip(jax.random.normal(keys[0], (N_REPLICA, D, D), jnp.float32), -5.0, 5.0)
    lowest, highest, rise = (0.3, 3.0, 1.732)
    row_scale = jnp.exp(jax.random.uniform(keys[2], (N_REPLICA, D, 1), jnp.float32, math.log(lowest), math.log(highest)))
    row_scale = row_scale * jnp.power(rise, positions)[None, :, None] * jnp.power(rise, replicas)[:, None, None]
    col_scale = jnp.exp(jax.random.uniform(keys[3], (1, 1, D), jnp.float32, math.log(lowest), math.log(highest)))
    return jnp.clip(values * row_scale * col_scale, -80.0, 80.0).astype(jnp.bfloat16)


def draw_errors(key, part):
    key = jax.random.fold_in(key, 13)
    values = 0.3 * jnp.clip(jax.random.normal(key, (N_REPLICA, D, D), jnp.float32), -4.0, 4.0)
    return values.astype(jnp.bfloat16)


def level_of(stream_key, extent, cuts, low, top_value):
    def one(position, parts):
        heights = jax.random.uniform(jax.random.fold_in(jax.random.fold_in(stream_key, 6), position), (parts,), jnp.float32, low / len(cuts), top_value / len(cuts))
        return jnp.repeat(jnp.exp(heights), extent[position] // parts).reshape((-1,) + (1,) * (len(extent) - position - 1))

    gain = one(*cuts[0])
    for cut in cuts[1:]:
        gain = gain * one(*cut)
    return gain


def normal_values(stream_key, extent, spread, reach, shards=(), kind=jnp.bfloat16):
    level = level_of(stream_key, extent, shards, -0.22, 0.18) if shards else 1.0
    entries = jax.random.normal(stream_key, extent, jnp.float32) * spread * level
    return jnp.minimum(jnp.maximum(entries, -reach), reach).astype(kind)


def setup_inputs(seed: int = 0) -> dict:
    key_of = jax.random.split(jax.random.key(seed), 5)
    grads = draw_grads(jax.random.fold_in(key_of[4], 71), 0)
    errors = draw_errors(jax.random.fold_in(key_of[4], 71), 0)
    q_start = normal_values(key_of[2], (D, RANK), D ** -0.5, 0.078125, ((0, 16),), jnp.float32)
    clip_rms = jnp.clip(jax.random.uniform(key_of[3], (), jnp.float32, 1.5, 2.5), 1.5, 2.5)
    return dict(grads=grads, errors=errors, q_start=q_start, clip_rms=clip_rms)


def reference(grads, errors, q_start, clip_rms):
    q_warm = q_start.astype(jnp.bfloat16)
    squares = jnp.float32(0.0)
    p_sum = jnp.zeros((D, RANK), jnp.float32)
    lowered = []
    for index in range(N_REPLICA):
        merged = grads[index].astype(jnp.float32) + errors[index].astype(jnp.float32)
        squares = squares + jnp.sum(merged * merged)
        merged_b = merged.astype(jnp.bfloat16)
        lowered.append(merged_b)
        p_sum = p_sum + jnp.dot(merged_b.astype(jnp.float32), q_warm.astype(jnp.float32), preferred_element_type=jnp.float32)
    gram = jnp.dot(p_sum.T, p_sum, precision=lax.Precision.HIGHEST)
    factor = jnp.linalg.cholesky(gram)
    p_basis = jax.scipy.linalg.solve_triangular(factor, p_sum.T, lower=True).T
    p_low = p_basis.astype(jnp.bfloat16)
    q_total = jnp.zeros((D, RANK), jnp.float32)
    for index in range(N_REPLICA):
        q_total = q_total + lax.dot_general(lowered[index].astype(jnp.float32), p_low.astype(jnp.float32), (((0,), (0,)), ((), ())), preferred_element_type=jnp.float32)
    q_mean = q_total / N_REPLICA
    q_low = q_mean.astype(jnp.bfloat16)
    update = lax.dot_general(p_low.astype(jnp.float32), q_low.astype(jnp.float32), (((1,), (1,)), ((), ())), preferred_element_type=jnp.float32)
    new_errors = jnp.stack([(lowered[index].astype(jnp.float32) - update).astype(jnp.bfloat16) for index in range(N_REPLICA)])
    root_mean = jnp.sqrt(squares / (N_REPLICA * D * D) + 1e-06)
    clip_scale = jnp.minimum(jnp.float32(1.0), clip_rms / root_mean)
    return (new_errors, p_basis, clip_scale * q_mean)
```

```python
import jax
import jax.numpy as jnp
from jax import lax
from jax.experimental import pallas as pl
from jax.experimental.pallas import tpu as pltpu
from jax.sharding import PartitionSpec as P

MESH = pl.DeviceIdType.MESH
F32 = jnp.float32
BF16 = jnp.bfloat16

ROWS = 384
D = 6144
RANK = 128
CHUNKS = 8
CHUNK = ROWS // CHUNKS
HALF = ROWS // 2
PIECE = ROWS // 8


def mod4(v):
    return lax.rem(v, 4)


def split3(v):
    a = v.astype(BF16).astype(F32)
    b = (v - a).astype(BF16).astype(F32)
    return a, b, (v - a - b).astype(BF16).astype(F32)


def tile_of(part, x, y, z):
    return (z * 16 + x * 4 + y, x * 16 + y * 4 + z, y * 16 + z * 4 + x)[part]


def exchange(
    clip_ref,
    grads,
    errors,
    q_ref,
    merged_out,
    yt_out,
    bmat_ref,
    basis_ref,
    w_ref,
    gbuf,
    ebuf,
    qh,
    pacc,
    sq,
    psend,
    precv,
    pall,
    pt,
    gsend,
    gxr,
    gyr,
    gmat,
    aug,
    wbuf,
    yl,
    yr,
    yc,
    rs1,
    rs2,
    rs3,
    t1,
    t2,
    gy,
    load_sem,
    out_sem,
    yt_sem,
    q1s,
    q1r,
    q2s,
    q2r,
    q3s,
    q3r,
    p1s,
    p1r,
    p2s,
    p2r,
    gxs,
    gxq,
    gys,
    gyq,
    gas,
    gaq,
    cs,
    cr,
    r1s,
    r1r,
    r2s,
    r2r,
    r3s,
    r3r,
    a1s,
    a1r,
    a2s,
    a2r,
    a3s,
    a3r,
    ss,
    sr,
):
    f = lax.axis_index("fsdp")
    r = lax.axis_index("replica")
    x, y, z, c = f // 4, lax.rem(f, 4), r // 2, lax.rem(r, 2)
    sibling = (f, z * 2 + 1 - c)

    def on_x(d):
        return (mod4(x + d) * 4 + y, r)

    def on_y(d):
        return (x * 4 + mod4(y + d), r)

    def on_z(d):
        return (f, mod4(z + d) * 2 + c)

    def send(src, dst, ssem, rsem, device):
        copy = pltpu.make_async_remote_copy(
            src_ref=src, dst_ref=dst, send_sem=ssem, recv_sem=rsem, device_id=device, device_id_type=MESH
        )
        copy.start()
        return copy

    sent = []

    loads = []
    for k in range(CHUNKS):
        rows = pl.ds(k * CHUNK, CHUNK)
        a = pltpu.make_async_copy(grads.at[rows], gbuf.at[rows], load_sem.at[0, k])
        b = pltpu.make_async_copy(errors.at[rows], ebuf.at[rows], load_sem.at[1, k])
        a.start()
        b.start()
        loads.append((a, b))

    s_me, t_me = jnp.where(c == 0, y, x), jnp.where(c == 0, x, y)
    qh[c, s_me, t_me] = q_ref[pl.ds(pl.multiple_of(c * HALF, HALF), HALF), :].astype(BF16)

    barrier = pltpu.get_barrier_semaphore()
    peers = [sibling]
    for d in (1, 2, 3):
        peers += [on_x(d), on_y(d), on_z(d), (f, mod4(z + d) * 2 + 1 - c)]
    for device in peers:
        pl.semaphore_signal(barrier, inc=1, device_id=device, device_id_type=MESH)
    pl.semaphore_wait(barrier, len(peers))

    def along(first, d):
        if first:
            return (jnp.where(c == 0, mod4(x + d) * 4 + y, x * 4 + mod4(y + d)), r)
        return (jnp.where(c == 0, x * 4 + mod4(y + d), mod4(x + d) * 4 + y), r)

    q1 = []
    for d in (1, 2, 3):
        here = qh.at[c, s_me, t_me]
        q1.append(send(here, here, q1s.at[d - 1], q1r.at[d - 1], along(True, d)))

    sq[...] = jnp.zeros_like(sq)

    def merge(k):
        a, b = loads[k]
        a.wait()
        b.wait()

        def group(i, _):
            rows = pl.ds(pl.multiple_of(k * CHUNK + i * 16, 16), 16)
            total = jnp.zeros((16, 128), F32)
            for j in range(D // 768):
                cols = pl.ds(j * 768, 768)
                m = gbuf[rows, cols].astype(F32) + ebuf[rows, cols].astype(F32)
                gbuf[rows, cols] = m.astype(BF16)
                m2 = m * m
                for i2 in range(6):
                    total = total + m2[:, i2 * 128 : (i2 + 1) * 128]
            sq[...] += total[:8] + total[8:]
            return 0

        lax.fori_loop(0, CHUNK // 16, group, 0)
        rows = pl.ds(k * CHUNK, CHUNK)
        out = pltpu.make_async_copy(gbuf.at[rows], merged_out.at[rows], out_sem.at[k])
        out.start()
        return out

    outs = [merge(0), merge(1)]
    for copy in q1:
        copy.wait_recv()
    q2 = []
    for d in (1, 2, 3):
        here = qh.at[c, s_me]
        q2.append(send(here, here, q2s.at[d - 1], q2r.at[d - 1], along(False, d)))
    q3 = [send(qh.at[c, s_me], qh.at[c, s_me], q3s.at[0], q3r.at[0], sibling)]
    outs += [merge(k) for k in range(2, CHUNKS)]
    for d in (1, 2, 3):
        q2[d - 1].wait_recv()
        s = mod4(s_me + 4 - d)
        q3.append(send(qh.at[c, s], qh.at[c, s], q3s.at[d], q3r.at[d], sibling))
    for copy in q3:
        copy.wait_recv()
    sent += q1 + q2 + q3

    for j in range(8):
        parts = []
        for k in (2 * j, 2 * j + 1):
            parts += [qh[0, k % 4, k // 4], qh[1, k // 4, k % 4]]
        term = jnp.dot(
            gbuf[:, j * 768 : (j + 1) * 768], jnp.concatenate(parts, axis=0), preferred_element_type=F32
        )
        if j == 0:
            pacc[...] = term
        else:
            pacc[...] += term

    for k in range(8):
        psend[k, :PIECE] = pacc[k * PIECE : (k + 1) * PIECE]
        psend[k, PIECE:] = sq[...]
    p1 = []
    for e in range(1, 8):
        other = lax.rem(r + e, 8)
        p1.append(send(psend.at[other], precv.at[e - 1], p1s.at[e - 1], p1r.at[e - 1], (f, other)))
    total = psend[r]
    for e in range(1, 8):
        p1[e - 1].wait_recv()
        total = total + precv[e - 1]
    pall[r] = total[:PIECE].astype(BF16)
    p2 = []
    for e in range(1, 8):
        other = lax.rem(r + e, 8)
        p2.append(send(pall.at[r], pall.at[r], p2s.at[e - 1], p2r.at[e - 1], (f, other)))
    for copy in p2:
        copy.wait_recv()
    sent += p1 + p2

    p_full = pall[...].reshape(ROWS, RANK)
    pt[...] = p_full.T
    my_rows = pl.ds(pl.multiple_of(r * 16, 16), 16)
    gsend[0, :16] = jnp.dot(pt[my_rows, :], p_full, preferred_element_type=F32)
    gsend[0, 16:] = total[PIECE:]
    gx = [send(gsend.at[0], gxr.at[d - 1], gxs.at[d - 1], gxq.at[d - 1], on_x(d)) for d in (1, 2, 3)]

    def right(part):
        def pair(j, _):
            cols = [
                gbuf[:, pl.ds(pl.multiple_of(j * 768 + k * 384 + part * 128, 128), 128)] for k in (0, 1)
            ]
            block = jnp.dot(pt[...], jnp.concatenate(cols, axis=1), preferred_element_type=F32).astype(BF16)
            for k in (0, 1):
                for c2 in (0, 1):
                    for z2 in range(4):
                        yl[c2, part, tile_of(part, j // 2, lax.rem(j, 2) * 2 + k, z2)] = block[
                            c2 * 64 + z2 * 16 : c2 * 64 + z2 * 16 + 16, k * 128 : (k + 1) * 128
                        ]
            return 0

        lax.fori_loop(0, 8, pair, 0)
        return send(yl.at[1 - c, part], yr.at[part], cs.at[part], cr.at[part], sibling)

    order = ((z, x, y), (x, y, z), (y, z, x))
    ways = ((on_z, on_x, on_y), (on_x, on_y, on_z), (on_y, on_z, on_x))

    core = [right(0)]
    for copy in gx:
        copy.wait_recv()
    gsend[1] = gsend[0] + gxr[0] + gxr[1] + gxr[2]
    gyc = [send(gsend.at[1], gyr.at[d - 1], gys.at[d - 1], gyq.at[d - 1], on_y(d)) for d in (1, 2, 3)]
    core.append(right(1))
    for copy in gyc:
        copy.wait_recv()
    gsum = gsend[1] + gyr[0] + gyr[1] + gyr[2]
    gmat[r] = gsum[:16]
    ga = []
    for e in range(1, 8):
        other = lax.rem(r + e, 8)
        ga.append(send(gmat.at[r], gmat.at[r], gas.at[e - 1], gaq.at[e - 1], (f, other)))
    core.append(right(2))
    sent += gx + gyc + ga + core

    def add_core(part):
        core[part].wait_recv()

        def some(i, _):
            at = pl.ds(i * 8, 8)
            yc[part, at] = (yl[c, part, at].astype(F32) + yr[part, at].astype(F32)).astype(BF16)
            return 0

        lax.fori_loop(0, 8, some, 0)
        a0 = order[part][0]
        return [
            send(
                yc.at[part, pl.ds(mod4(a0 + d) * 16, 16)],
                rs1.at[part, d - 1],
                r1s.at[part, d - 1],
                r1r.at[part, d - 1],
                ways[part][0](d),
            )
            for d in (1, 2, 3)
        ]

    s1 = [add_core(part) for part in range(3)]

    for copy in ga:
        copy.wait_recv()
    aug[:, :RANK] = gmat[...].reshape(RANK, RANK)
    rows_i = lax.broadcasted_iota(jnp.int32, (RANK, RANK), 0)
    cols_i = lax.broadcasted_iota(jnp.int32, (RANK, RANK), 1)
    aug[:, RANK:] = jnp.where(rows_i == cols_i, 1.0, 0.0).astype(F32)
    sub = lax.broadcasted_iota(jnp.int32, (8, 128), 0)

    def panel(k, _):
        base = pl.multiple_of(k * 8, 8)
        rowp = aug[pl.ds(base, 8), :RANK]
        ext = aug[pl.ds(base, 8), RANK:]
        turned = pltpu.roll(rowp, lax.rem(128 - base, 128), 1)
        col = [jnp.broadcast_to(turned[:, j : j + 1], (8, 128)) for j in range(8)]
        for j in range(8):
            pivot = jnp.broadcast_to(col[j][j : j + 1, :], (8, 128))
            inv = lax.rsqrt(pivot)
            inv = inv * (1.5 - 0.5 * pivot * inv * inv)
            low = jnp.where(sub > j, col[j] * inv, 0.0)
            for m in range(j + 1, 8):
                col[m] = col[m] - low * jnp.broadcast_to(low[m : m + 1, :], (8, 128))
            row_r = jnp.broadcast_to(rowp[j : j + 1, :], (8, 128)) * inv
            row_e = jnp.broadcast_to(ext[j : j + 1, :], (8, 128)) * inv
            rowp = jnp.where(sub == j, row_r, rowp - low * row_r)
            ext = jnp.where(sub == j, row_e, ext - low * row_e)
        wbuf[pl.ds(base, 8), :] = ext
        v1, v2, v3 = split3(rowp)
        e1, e2, e3 = split3(ext)
        left = jnp.concatenate([v1, v1, v2, v2, v1, v3], axis=0).T.astype(BF16)
        top = jnp.concatenate([v1, v2, v1, v2, v3, v1], axis=0)
        more = jnp.concatenate([e1, e2, e1, e2, e3, e1], axis=0)
        both = jnp.concatenate([top, more], axis=1).astype(BF16)
        aug[...] -= jnp.dot(left, both, preferred_element_type=F32)
        return 0

    lax.fori_loop(0, 8, panel, 0)

    def add(part, own, came, out, waits, n):
        for copy in waits[part]:
            copy.wait_recv()
        value = own.astype(F32)
        for d in (0, 1, 2):
            value = value + came[part, d].astype(F32)
        out[part] = value.astype(BF16)

    s2, s3, g1, g2, g3, sib = [], [], [], [], [], []
    for part in range(3):
        a0, a1, _ = order[part]
        add(part, yc[part, pl.ds(a0 * 16, 16)], rs1, t1, s1, 16)
        s2.append([
            send(
                t1.at[part, pl.ds(mod4(a1 + d) * 4, 4)],
                rs2.at[part, d - 1],
                r2s.at[part, d - 1],
                r2r.at[part, d - 1],
                ways[part][1](d),
            )
            for d in (1, 2, 3)
        ])
    for part in range(3):
        _, a1, a2 = order[part]
        add(part, t1[part, pl.ds(a1 * 4, 4)], rs2, t2, s2, 4)
        s3.append([
            send(
                t2.at[part, pl.ds(mod4(a2 + d), 1)],
                rs3.at[part, d - 1],
                r3s.at[part, d - 1],
                r3r.at[part, d - 1],
                ways[part][2](d),
            )
            for d in (1, 2, 3)
        ])
    for part in range(3):
        a0, a1, a2 = order[part]
        for copy in s3[part]:
            copy.wait_recv()
        value = t2[part, pl.ds(a2, 1)].astype(F32)
        for d in (0, 1, 2):
            value = value + rs3[part, d].astype(F32)
        mine = pl.ds(a0 * 16 + a1 * 4 + a2, 1)
        gy[c, part, mine] = value.astype(BF16)
        here = gy.at[c, part, mine]
        g1.append([
            send(here, here, a1s.at[part, d - 1], a1r.at[part, d - 1], ways[part][2](d)) for d in (1, 2, 3)
        ])
    for part in range(3):
        a0, a1, _ = order[part]
        for copy in g1[part]:
            copy.wait_recv()
        here = gy.at[c, part, pl.ds(a0 * 16 + a1 * 4, 4)]
        g2.append([
            send(here, here, a2s.at[part, d - 1], a2r.at[part, d - 1], ways[part][1](d)) for d in (1, 2, 3)
        ])
    for part in range(3):
        a0 = order[part][0]
        for copy in g2[part]:
            copy.wait_recv()
        here = gy.at[c, part, pl.ds(a0 * 16, 16)]
        g3.append([
            send(here, here, a3s.at[part, d - 1], a3r.at[part, d - 1], ways[part][0](d)) for d in (1, 2, 3)
        ])
        sib.append([send(here, here, ss.at[part, 0], sr.at[part, 0], sibling)])

    lax.fori_loop(8, 16, panel, 0)

    w = wbuf[...]
    pb = jnp.zeros((ROWS, RANK), F32)
    p_again = pall[...].reshape(ROWS, RANK)
    for piece in split3(w)[::-1]:
        pb = pb + lax.dot_general(
            p_again, piece.astype(BF16), (((1,), (1,)), ((), ())), preferred_element_type=F32
        )
    basis_ref[...] = pb
    bmat_ref[...] = (
        jnp.dot(pb, w, preferred_element_type=F32, precision=lax.Precision.HIGHEST) * 0.125
    ).astype(BF16)
    squares = jnp.sum(gsum[16:])
    root_mean = jnp.sqrt(jnp.full((1, RANK), squares) / (8 * D * D) + 1e-06)
    scale = jnp.minimum(1.0, clip_ref[0, 0] / root_mean) * 0.125
    w_ref[...] = w * scale

    for d in (1, 2, 3):
        for part in range(3):
            g3[part][d - 1].wait_recv()
            here = gy.at[c, part, pl.ds(mod4(order[part][0] + 4 - d) * 16, 16)]
            sib[part].append(send(here, here, ss.at[part, d], sr.at[part, d], sibling))
    ytc = []
    for part in range(3):
        ytc.append(pltpu.make_async_copy(gy.at[c, part], yt_out.at[c, part], yt_sem.at[0, part]))
        ytc[-1].start()
    for part in range(3):
        for copy in sib[part]:
            copy.wait_recv()
        ytc.append(pltpu.make_async_copy(gy.at[1 - c, part], yt_out.at[1 - c, part], yt_sem.at[1, part]))
        ytc[-1].start()
    for group in (s1, s2, s3, g1, g2, g3, sib):
        for copies in group:
            sent += copies
    for copy in sent:
        copy.wait_send()
    for copy in outs + ytc:
        copy.wait()


def update(merged_ref, yt_ref, bmat_ref, basis_ref, w_ref, new_ref, basis_out, q_out):
    f = lax.axis_index("fsdp")
    j = pl.program_id(0)

    def columns(part, x, y):
        tiles = [yt_ref[c, part, tile_of(part, x, y, z)] for c in (0, 1) for z in range(4)]
        return jnp.concatenate(tiles, axis=0)

    x, y = j // 2, lax.rem(j, 2) * 2
    right = jnp.concatenate([columns(part, x, y + k) for k in (0, 1) for part in range(3)], axis=1)
    for i in range(3):
        rows = slice(i * 128, (i + 1) * 128)
        low = jnp.dot(bmat_ref[rows], right, preferred_element_type=F32)
        new_ref[rows] = (merged_ref[rows].astype(F32) - low).astype(BF16)

    @pl.when(j == 7)
    def _():
        basis_out[...] = basis_ref[...]
        for part in range(3):
            own = columns(part, f // 4, lax.rem(f, 4))
            value = jnp.zeros((RANK, RANK), F32)
            for piece in split3(w_ref[...])[::-1]:
                value = value + jnp.dot(piece.astype(BF16), own, preferred_element_type=F32)
            q_out[part * 128 : (part + 1) * 128] = value.T


def body(grads, errors, q_start, clip_rms):
    dma = pltpu.SemaphoreType.DMA
    vmem = pltpu.VMEM
    hbm = pl.BlockSpec(memory_space=pl.ANY)
    inside = pl.BlockSpec(memory_space=pltpu.VMEM)
    merged, yt, bmat, basis, w = pl.pallas_call(
        exchange,
        out_shape=(
            jax.ShapeDtypeStruct((ROWS, D), BF16),
            jax.ShapeDtypeStruct((2, 3, 64, 16, 128), BF16),
            jax.ShapeDtypeStruct((ROWS, RANK), BF16),
            jax.ShapeDtypeStruct((ROWS, RANK), F32),
            jax.ShapeDtypeStruct((RANK, RANK), F32),
        ),
        in_specs=[pl.BlockSpec(memory_space=pltpu.SMEM), hbm, hbm, inside],
        out_specs=(hbm, hbm, inside, inside, inside),
        scratch_shapes=[
            vmem((ROWS, D), BF16),
            vmem((ROWS, D), BF16),
            vmem((2, 4, 4, HALF, RANK), BF16),
            vmem((ROWS, RANK), F32),
            vmem((8, 128), F32),
            vmem((8, PIECE + 8, RANK), F32),
            vmem((7, PIECE + 8, RANK), F32),
            vmem((8, PIECE, RANK), BF16),
            vmem((RANK, ROWS), BF16),
            vmem((2, 24, RANK), F32),
            vmem((3, 24, RANK), F32),
            vmem((3, 24, RANK), F32),
            vmem((8, 16, RANK), F32),
            vmem((RANK, 2 * RANK), F32),
            vmem((RANK, RANK), F32),
            vmem((2, 3, 64, 16, 128), BF16),
            vmem((3, 64, 16, 128), BF16),
            vmem((3, 64, 16, 128), BF16),
            vmem((3, 3, 16, 16, 128), BF16),
            vmem((3, 3, 4, 16, 128), BF16),
            vmem((3, 3, 1, 16, 128), BF16),
            vmem((3, 16, 16, 128), BF16),
            vmem((3, 4, 16, 128), BF16),
            vmem((2, 3, 64, 16, 128), BF16),
            dma((2, CHUNKS)),
            dma((CHUNKS,)),
            dma((2, 3)),
            dma((3,)),
            dma((3,)),
            dma((3,)),
            dma((3,)),
            dma((4,)),
            dma((4,)),
            dma((7,)),
            dma((7,)),
            dma((7,)),
            dma((7,)),
            dma((3,)),
            dma((3,)),
            dma((3,)),
            dma((3,)),
            dma((7,)),
            dma((7,)),
            dma((3,)),
            dma((3,)),
        ]
        + [dma((3, 3))] * 12
        + [dma((3, 4))] * 2,
        compiler_params=pltpu.CompilerParams(
            collective_id=0, has_side_effects=True, vmem_limit_bytes=48 * 1024 * 1024
        ),
        name="exchange",
    )(clip_rms.reshape(1, 1), grads[0], errors[0], q_start)

    def whole(shape):
        return pl.BlockSpec(shape, lambda j: (0,) * len(shape))

    new_errors, basis, q_out = pl.pallas_call(
        update,
        grid=(8,),
        out_shape=(
            jax.ShapeDtypeStruct((ROWS, D), BF16),
            jax.ShapeDtypeStruct((ROWS, RANK), F32),
            jax.ShapeDtypeStruct((ROWS, RANK), F32),
        ),
        in_specs=[
            pl.BlockSpec((ROWS, 768), lambda j: (0, j)),
            whole((2, 3, 64, 16, 128)),
            whole((ROWS, RANK)),
            whole((ROWS, RANK)),
            whole((RANK, RANK)),
        ],
        out_specs=(
            pl.BlockSpec((ROWS, 768), lambda j: (0, j)),
            whole((ROWS, RANK)),
            whole((ROWS, RANK)),
        ),
        compiler_params=pltpu.CompilerParams(vmem_limit_bytes=48 * 1024 * 1024),
        name="update",
    )(merged, yt, bmat, basis, w)
    return new_errors[None], basis, q_out


def solution(mesh):
    return jax.shard_map(
        body,
        mesh=mesh,
        in_specs=(P("replica", "fsdp", None), P("replica", "fsdp", None), P("fsdp", None), P()),
        out_specs=(P("replica", "fsdp", None), P("fsdp", None), P("fsdp", None)),
        check_vma=False,
    )
```

```python
import jax
import jax.numpy as jnp
from jax import lax
from jax.experimental import pallas as pl
from jax.experimental.pallas import tpu as pltpu
from jax.sharding import PartitionSpec as P

MESH = pl.DeviceIdType.MESH
F32 = jnp.float32
BF16 = jnp.bfloat16

ROWS = 384
D = 6144
RANK = 128
CHUNKS = 8
CHUNK = ROWS // CHUNKS
HALF = ROWS // 2
PIECE = ROWS // 8
FAR = (2, 1, 3, 0)
OFFSETS = [(dx, dy) for dx in FAR for dy in FAR]


def mod4(v):
    return lax.rem(v + 4, 4)


def split3(v):
    a = v.astype(BF16).astype(F32)
    b = (v - a).astype(BF16).astype(F32)
    return a, b, (v - a - b).astype(BF16).astype(F32)


def exchange(
    clip_ref,
    grads,
    errors,
    q_ref,
    new_ref,
    basis_ref,
    qout_ref,
    gbuf,
    ebuf,
    qin,
    qh,
    pacc,
    sq,
    psend,
    precv,
    pall,
    pt,
    gsend,
    grecv,
    gmat,
    aug,
    wbuf,
    bmat,
    yl,
    yr,
    yc,
    rs,
    gy,
    load_sem,
    qin_sem,
    q1s,
    q1r,
    q2s,
    q2r,
    q3s,
    q3r,
    p1s,
    p1r,
    p2s,
    p2r,
    g1s,
    g1r,
    g2s,
    g2r,
    g3s,
    g3r,
    cs,
    cr,
    rss,
    rsr,
    ags,
    agr,
    fs,
    fr,
):
    f = lax.axis_index("fsdp")
    r = lax.axis_index("replica")
    x, y, z, c = f // 4, lax.rem(f, 4), r // 2, lax.rem(r, 2)
    sibling = (f, z * 2 + 1 - c)

    def at_xy(dx, dy):
        return mod4(x + dx) * 4 + mod4(y + dy)

    def at_z(dz):
        return mod4(z + dz) * 2 + c

    def describe(src, dst, ssem, rsem, device):
        return pltpu.make_async_remote_copy(
            src_ref=src, dst_ref=dst, send_sem=ssem, recv_sem=rsem, device_id=device, device_id_type=MESH
        )

    def send(src, dst, ssem, rsem, device):
        copy = describe(src, dst, ssem, rsem, device)
        copy.start()
        return copy

    sent = []

    qload = pltpu.make_async_copy(q_ref.at[pl.ds(pl.multiple_of(c * HALF, HALF), HALF)], qin, qin_sem)
    qload.start()

    barrier = pltpu.get_barrier_semaphore()
    peers = [sibling]
    for d in (1, 2, 3):
        peers += [(at_xy(d, 0), r), (at_xy(0, d), r), (f, at_z(d)), (f, mod4(z + d) * 2 + 1 - c)]
    for device in peers:
        pl.semaphore_signal(barrier, inc=1, device_id=device, device_id_type=MESH)

    loads = []
    for k in range(CHUNKS):
        rows = pl.ds(k * CHUNK, CHUNK)
        a = pltpu.make_async_copy(grads.at[rows], gbuf.at[rows], load_sem.at[0, k])
        b = pltpu.make_async_copy(errors.at[rows], ebuf.at[rows], load_sem.at[1, k])
        a.start()
        b.start()
        loads.append((a, b))

    s_me, t_me = jnp.where(c == 0, y, x), jnp.where(c == 0, x, y)
    qload.wait()
    qh[c, s_me, t_me] = qin[...].astype(BF16)
    sq[...] = jnp.zeros_like(sq)
    pl.semaphore_wait(barrier, len(peers))

    def along_t(d):
        return (jnp.where(c == 0, at_xy(d, 0), at_xy(0, d)), r)

    def along_s(d):
        return (jnp.where(c == 0, at_xy(0, d), at_xy(d, 0)), r)

    own = qh.at[c, s_me, t_me]
    q1 = [send(own, own, q1s.at[d - 1], q1r.at[d - 1], along_t(d)) for d in (1, 2, 3)]
    q2 = [send(own, own, q2s.at[0, d - 1], q2r.at[d - 1], along_s(d)) for d in (1, 2, 3)]
    q3 = [send(own, own, q3s.at[0], q3r.at[0], sibling)]

    def merge(k):
        a, b = loads[k]
        a.wait()
        b.wait()

        def group(i, _):
            rows = pl.ds(pl.multiple_of(k * CHUNK + i * 16, 16), 16)
            total = jnp.zeros((16, 128), F32)
            for j in range(D // 768):
                cols = pl.ds(j * 768, 768)
                m = gbuf[rows, cols].astype(F32) + ebuf[rows, cols].astype(F32)
                gbuf[rows, cols] = m.astype(BF16)
                m2 = m * m
                for i2 in range(6):
                    total = total + m2[:, i2 * 128 : (i2 + 1) * 128]
            sq[...] += total[:8] + total[8:]
            return 0

        lax.fori_loop(0, CHUNK // 16, group, 0)

    for k in range(3):
        merge(k)
    for d in (1, 3, 2):
        q1[d - 1].wait_recv()
        here = qh.at[c, s_me, mod4(t_me - d)]
        for e in (2, 1, 3):
            q2.append(send(here, here, q2s.at[d, e - 1], q2r.at[e - 1], along_s(e)))
        q3.append(send(here, here, q3s.at[d], q3r.at[d], sibling))
    for k in range(3, CHUNKS):
        merge(k)
    for d in (1, 3, 2):
        here = qh.at[c, mod4(s_me - d)]
        describe(here, here, q2s.at[0, 0], q2r.at[d - 1], sibling).wait_recv()
        q3.append(send(here, here, q3s.at[3 + d], q3r.at[3 + d], sibling))
    for copy in q3:
        copy.wait_recv()
    sent += q1 + q2 + q3

    for j in range(8):
        parts = []
        for k in (2 * j, 2 * j + 1):
            parts += [qh[0, k % 4, k // 4], qh[1, k // 4, k % 4]]
        term = jnp.dot(
            gbuf[:, j * 768 : (j + 1) * 768], jnp.concatenate(parts, axis=0), preferred_element_type=F32
        )
        if j == 0:
            pacc[...] = term
        else:
            pacc[...] += term

    for k in range(8):
        psend[k, :PIECE] = pacc[k * PIECE : (k + 1) * PIECE]
        psend[k, PIECE:] = sq[...]
    p1 = []
    for e in (4, 3, 5, 2, 6, 1, 7):
        other = lax.rem(r + e, 8)
        p1.append(send(psend.at[other], precv.at[r], p1s.at[e - 1], p1r.at[e - 1], (f, other)))
    precv[r] = psend[r]
    for copy in p1:
        copy.wait_recv()
    total = precv[0]
    for k in range(1, 8):
        total = total + precv[k]
    pall[r] = total[:PIECE].astype(BF16)
    p2 = []
    for e in (4, 3, 5, 2, 6, 1, 7):
        other = lax.rem(r + e, 8)
        p2.append(send(pall.at[r], pall.at[r], p2s.at[e - 1], p2r.at[e - 1], (f, other)))
    for copy in p2:
        copy.wait_recv()
    sent += p1 + p2

    p_full = pall[...].reshape(ROWS, RANK)
    pt[...] = p_full.T
    slot = c * 4 + z
    my_rows = pl.ds(pl.multiple_of(slot * 16, 16), 16)
    gsend[:16] = jnp.dot(pt[my_rows, :], p_full, preferred_element_type=F32)
    gsend[16:] = total[PIECE:]
    g1 = [
        send(gsend, grecv.at[k], g1s.at[k], g1r.at[k], (at_xy(dx, dy), r))
        for k, (dx, dy) in enumerate(OFFSETS[:-1])
    ]

    core, rsends = [], []

    def multiply(k):
        g = at_xy(*OFFSETS[k])
        cols = gbuf[:, pl.ds(pl.multiple_of(g * ROWS, 128), ROWS)]
        yl[g] = jnp.dot(pt[...], cols, preferred_element_type=F32).astype(BF16)
        theirs = yl.at[g, pl.ds(pl.multiple_of((1 - c) * 64, 64), 64)]
        core.append(send(theirs, yr.at[g], cs.at[k], cr.at[k], sibling))

    def scatter(k):
        g = at_xy(*OFFSETS[k])
        core[k].wait_recv()
        mine = yl[g, pl.ds(pl.multiple_of(c * 64, 64), 64), :]
        yc[g] = (mine.astype(F32) + yr[g].astype(F32)).astype(BF16)
        here = pl.ds(pl.multiple_of(z * 16, 16), 16)
        for dz in FAR:
            if (dz, k) != (0, 15):
                src = yc.at[g, pl.ds(pl.multiple_of(mod4(z + dz) * 16, 16), 16)]
                rsends.append(send(src, rs.at[f, here], rss.at[k], rsr.at[k], (g, at_z(dz))))
        if k == 15:
            rs[f, here] = yc[f, here, :]

    for k in range(16):
        multiply(k)
        if k >= 2:
            scatter(k - 2)
    scatter(14)
    scatter(15)

    gsum = gsend[...]
    for k in range(15):
        g1[k].wait_recv()
        gsum = gsum + grecv[k]
    gmat[slot] = gsum[:16]
    g2 = [send(gmat.at[slot], gmat.at[slot], g2s.at[d - 1], g2r.at[d - 1], (f, at_z(d))) for d in (1, 2, 3)]

    def came(k, sems, ref):
        dx, dy = OFFSETS[k]
        g = at_xy(-dx, -dy)
        region = ref.at[g, pl.ds(0, 64)] if k < 15 else ref.at[g, pl.ds(0, 48)]
        describe(region, region, sems[0].at[k], sems[1].at[k], sibling).wait_recv()
        return g

    value = jnp.zeros((16, ROWS), F32)
    for k in range(16):
        g = came(k, (rss, rsr), rs)
        for i in range(4):
            value = value + rs[g, i * 16 : (i + 1) * 16, :].astype(F32)
        if k == 8:
            for copy in g2:
                copy.wait_recv()
            side = gmat.at[pl.ds(c * 4, 4)]
            g3 = send(side, side, g3s.at[0], g3r.at[0], sibling)
    mine = pl.ds(pl.multiple_of(c * 64 + z * 16, 16), 16)
    gy[f, mine] = value.astype(BF16)
    asends = []
    for k in range(16):
        g = at_xy(*OFFSETS[k])
        for dz in FAR:
            if (dz, k) != (0, 15):
                here = gy.at[f, mine]
                asends.append(send(here, here, ags.at[k], agr.at[k], (g, at_z(dz))))

    g3.wait_recv()
    aug[:, :RANK] = gmat[...].reshape(RANK, RANK)
    rows_i = lax.broadcasted_iota(jnp.int32, (RANK, RANK), 0)
    cols_i = lax.broadcasted_iota(jnp.int32, (RANK, RANK), 1)
    aug[:, RANK:] = jnp.where(rows_i == cols_i, 1.0, 0.0).astype(F32)
    sub = lax.broadcasted_iota(jnp.int32, (8, 128), 0)

    def panel(k, _):
        base = pl.multiple_of(k * 8, 8)
        rowp = aug[pl.ds(base, 8), :RANK]
        ext = aug[pl.ds(base, 8), RANK:]
        turned = pltpu.roll(rowp, lax.rem(128 - base, 128), 1)
        col = [jnp.broadcast_to(turned[:, j : j + 1], (8, 128)) for j in range(8)]
        for j in range(8):
            pivot = jnp.broadcast_to(col[j][j : j + 1, :], (8, 128))
            inv = lax.rsqrt(pivot)
            inv = inv * (1.5 - 0.5 * pivot * inv * inv)
            low = jnp.where(sub > j, col[j] * inv, 0.0)
            for m in range(j + 1, 8):
                col[m] = col[m] - low * jnp.broadcast_to(low[m : m + 1, :], (8, 128))
            row_r = jnp.broadcast_to(rowp[j : j + 1, :], (8, 128)) * inv
            row_e = jnp.broadcast_to(ext[j : j + 1, :], (8, 128)) * inv
            rowp = jnp.where(sub == j, row_r, rowp - low * row_r)
            ext = jnp.where(sub == j, row_e, ext - low * row_e)
        wbuf[pl.ds(base, 8), :] = ext
        v1, v2, v3 = split3(rowp)
        e1, e2, e3 = split3(ext)
        left = jnp.concatenate([v1, v1, v2, v2, v1, v3], axis=0).T.astype(BF16)
        top = jnp.concatenate([v1, v2, v1, v2, v3, v1], axis=0)
        more = jnp.concatenate([e1, e2, e1, e2, e3, e1], axis=0)
        both = jnp.concatenate([top, more], axis=1).astype(BF16)
        aug[...] -= jnp.dot(left, both, preferred_element_type=F32)
        return 0

    lax.fori_loop(0, 16, panel, 0)

    w = wbuf[...]
    pb = jnp.zeros((ROWS, RANK), F32)
    p_again = pall[...].reshape(ROWS, RANK)
    for piece in split3(w)[::-1]:
        pb = pb + lax.dot_general(
            p_again, piece.astype(BF16), (((1,), (1,)), ((), ())), preferred_element_type=F32
        )
    basis_ref[...] = pb
    bmat[...] = (
        jnp.dot(pb, w, preferred_element_type=F32, precision=lax.Precision.HIGHEST) * 0.125
    ).astype(BF16)

    passed = []

    def forward(k):
        g = came(k, (ags, agr), gy)
        here = gy.at[g, pl.ds(pl.multiple_of(c * 64, 64), 64)]
        passed.append(send(here, here, fs.at[k], fr.at[k], sibling))

    def update(k):
        dx, dy = OFFSETS[k]
        g = at_xy(-dx, -dy)
        passed[k].wait_recv()
        cols = pl.ds(pl.multiple_of(g * ROWS, 128), ROWS)
        low = jnp.dot(bmat[...], gy[g], preferred_element_type=F32)
        new_ref[:, cols] = (gbuf[:, cols].astype(F32) - low).astype(BF16)

    for k in range(16):
        forward(k)
        if k >= 3:
            update(k - 3)
    for k in (13, 14, 15):
        update(k)

    squares = jnp.sum(gsum[16:])
    root_mean = jnp.sqrt(jnp.full((1, RANK), squares) / (8 * D * D) + 1e-06)
    scale = jnp.minimum(1.0, clip_ref[0, 0] / root_mean) * 0.125
    block = gy[f]
    value = jnp.zeros((RANK, ROWS), F32)
    for piece in split3(wbuf[...])[::-1]:
        value = value + jnp.dot(piece.astype(BF16), block, preferred_element_type=F32)
    qout_ref[...] = value.T * scale

    for copy in sent + g1 + g2 + [g3] + core + passed:
        copy.wait_send()
    for sems, ref in ((rss, yc), (ags, gy)):
        for k in range(16):
            region = ref.at[0, pl.ds(0, 64)] if k < 15 else ref.at[0, pl.ds(0, 48)]
            describe(region, region, sems.at[k], rsr.at[k], sibling).wait_send()


def body(grads, errors, q_start, clip_rms):
    dma = pltpu.SemaphoreType.DMA
    vmem = pltpu.VMEM
    hbm = pl.BlockSpec(memory_space=pltpu.HBM)
    inside = pl.BlockSpec(memory_space=pltpu.VMEM)
    new_errors, basis, q_out = pl.pallas_call(
        exchange,
        out_shape=(
            jax.ShapeDtypeStruct((ROWS, D), BF16),
            jax.ShapeDtypeStruct((ROWS, RANK), F32),
            jax.ShapeDtypeStruct((ROWS, RANK), F32),
        ),
        in_specs=[pl.BlockSpec(memory_space=pltpu.SMEM), hbm, hbm, hbm],
        out_specs=(inside, inside, inside),
        scratch_shapes=[
            vmem((ROWS, D), BF16),
            vmem((ROWS, D), BF16),
            vmem((HALF, RANK), F32),
            vmem((2, 4, 4, HALF, RANK), BF16),
            vmem((ROWS, RANK), F32),
            vmem((8, 128), F32),
            vmem((8, PIECE + 8, RANK), F32),
            vmem((8, PIECE + 8, RANK), F32),
            vmem((8, PIECE, RANK), BF16),
            vmem((RANK, ROWS), BF16),
            vmem((24, RANK), F32),
            vmem((15, 24, RANK), F32),
            vmem((8, 16, RANK), F32),
            vmem((RANK, 2 * RANK), F32),
            vmem((RANK, RANK), F32),
            vmem((ROWS, RANK), BF16),
            vmem((16, RANK, ROWS), BF16),
            vmem((16, 64, ROWS), BF16),
            vmem((16, 64, ROWS), BF16),
            vmem((16, 64, ROWS), BF16),
            vmem((16, RANK, ROWS), BF16),
            dma((2, CHUNKS)),
            dma(()),
            dma((3,)),
            dma((3,)),
            dma((4, 3)),
            dma((3,)),
            dma((7,)),
            dma((7,)),
            dma((7,)),
            dma((7,)),
            dma((7,)),
            dma((7,)),
            dma((15,)),
            dma((15,)),
            dma((3,)),
            dma((3,)),
            dma((1,)),
            dma((1,)),
        ]
        + [dma((16,))] * 8,
        compiler_params=pltpu.CompilerParams(
            collective_id=0, has_side_effects=True, vmem_limit_bytes=47 * 1024 * 1024
        ),
        name="exchange",
    )(clip_rms.reshape(1, 1), grads[0], errors[0], q_start)
    return new_errors[None], basis, q_out


def solution(mesh):
    return jax.shard_map(
        body,
        mesh=mesh,
        in_specs=(P("replica", "fsdp", None), P("replica", "fsdp", None), P("fsdp", None), P()),
        out_specs=(P("replica", "fsdp", None), P("fsdp", None), P("fsdp", None)),
        check_vma=False,
    )
```

```python
import jax
import jax.numpy as jnp
from jax import lax
from jax.experimental import pallas as pl
from jax.experimental.pallas import tpu as pltpu
from jax.sharding import PartitionSpec as P

MESH = pl.DeviceIdType.MESH
F32 = jnp.float32
BF16 = jnp.bfloat16

ROWS = 384
D = 6144
RANK = 128
CHUNKS = 8
CHUNK = ROWS // CHUNKS
HALF = ROWS // 2
PIECE = ROWS // 8
FAR = (2, 1, 3, 0)
PLANE = [(d, e) for d in FAR for e in FAR][:-1]


def mod4(v):
    return lax.rem(v + 4, 4)


def split3(v):
    a = v.astype(BF16).astype(F32)
    b = (v - a).astype(BF16).astype(F32)
    return a, b, (v - a - b).astype(BF16).astype(F32)


def tile_of(part, x, y, z):
    return (z * 16 + x * 4 + y, x * 16 + y * 4 + z, y * 16 + z * 4 + x)[part]


def exchange(
    clip_ref,
    grads,
    errors,
    q_ref,
    new_ref,
    basis_ref,
    qout_ref,
    gbuf,
    ebuf,
    qin,
    qh,
    pacc,
    sq,
    psend,
    precv,
    pall,
    pt,
    gsend,
    gxr,
    gyr,
    gmat,
    aug,
    wbuf,
    bmat,
    yl,
    yr,
    yc,
    rs1,
    t1,
    rs2,
    gy,
    load_sem,
    qin_sem,
    q1s,
    q1r,
    q2s,
    q2r,
    q3s,
    q3r,
    p1s,
    p1r,
    p2s,
    p2r,
    gxs,
    gxq,
    gys,
    gyq,
    g2s,
    g2r,
    g3s,
    g3r,
    cs,
    cr,
    r1s,
    r1r,
    a2s,
    a2r,
    r2s,
    r2r,
    a1s,
    a1r,
    fs,
    fr,
):
    f = lax.axis_index("fsdp")
    r = lax.axis_index("replica")
    x, y, z, c = f // 4, lax.rem(f, 4), r // 2, lax.rem(r, 2)
    sibling = (f, z * 2 + 1 - c)

    def at_xy(dx, dy):
        return mod4(x + dx) * 4 + mod4(y + dy)

    def at_z(dz):
        return mod4(z + dz) * 2 + c

    def describe(src, dst, ssem, rsem, device):
        return pltpu.make_async_remote_copy(
            src_ref=src, dst_ref=dst, send_sem=ssem, recv_sem=rsem, device_id=device, device_id_type=MESH
        )

    def send(src, dst, ssem, rsem, device):
        copy = describe(src, dst, ssem, rsem, device)
        copy.start()
        return copy

    sent = []

    qload = pltpu.make_async_copy(q_ref.at[pl.ds(pl.multiple_of(c * HALF, HALF), HALF)], qin, qin_sem)
    qload.start()

    barrier = pltpu.get_barrier_semaphore()
    peers = [sibling]
    for d in (1, 2, 3):
        peers += [(at_xy(d, 0), r), (at_xy(0, d), r), (f, at_z(d)), (f, mod4(z + d) * 2 + 1 - c)]
    for device in peers:
        pl.semaphore_signal(barrier, inc=1, device_id=device, device_id_type=MESH)

    loads = []
    for k in range(CHUNKS):
        rows = pl.ds(k * CHUNK, CHUNK)
        a = pltpu.make_async_copy(grads.at[rows], gbuf.at[rows], load_sem.at[0, k])
        b = pltpu.make_async_copy(errors.at[rows], ebuf.at[rows], load_sem.at[1, k])
        a.start()
        b.start()
        loads.append((a, b))

    s_me, t_me = jnp.where(c == 0, y, x), jnp.where(c == 0, x, y)
    qload.wait()
    qh[c, s_me, t_me] = qin[...].astype(BF16)
    sq[...] = jnp.zeros_like(sq)
    pl.semaphore_wait(barrier, len(peers))

    def along_t(d):
        return (jnp.where(c == 0, at_xy(d, 0), at_xy(0, d)), r)

    def along_s(d):
        return (jnp.where(c == 0, at_xy(0, d), at_xy(d, 0)), r)

    own = qh.at[c, s_me, t_me]
    q1 = [send(own, own, q1s.at[d - 1], q1r.at[d - 1], along_t(d)) for d in (1, 2, 3)]
    q2 = [send(own, own, q2s.at[0, d - 1], q2r.at[d - 1], along_s(d)) for d in (1, 2, 3)]
    q3 = [send(own, own, q3s.at[0], q3r.at[0], sibling)]

    def merge(k):
        a, b = loads[k]
        a.wait()
        b.wait()

        def group(i, _):
            rows = pl.ds(pl.multiple_of(k * CHUNK + i * 16, 16), 16)
            total = jnp.zeros((16, 128), F32)
            for j in range(D // 768):
                cols = pl.ds(j * 768, 768)
                m = gbuf[rows, cols].astype(F32) + ebuf[rows, cols].astype(F32)
                gbuf[rows, cols] = m.astype(BF16)
                m2 = m * m
                for i2 in range(6):
                    total = total + m2[:, i2 * 128 : (i2 + 1) * 128]
            sq[...] += total[:8] + total[8:]
            return 0

        lax.fori_loop(0, CHUNK // 16, group, 0)

    for k in range(3):
        merge(k)
    for d in (1, 3, 2):
        q1[d - 1].wait_recv()
        here = qh.at[c, s_me, mod4(t_me - d)]
        for e in (2, 1, 3):
            q2.append(send(here, here, q2s.at[d, e - 1], q2r.at[e - 1], along_s(e)))
        q3.append(send(here, here, q3s.at[d], q3r.at[d], sibling))
    for k in range(3, CHUNKS):
        merge(k)
    for d in (1, 3, 2):
        here = qh.at[c, mod4(s_me - d)]
        describe(here, here, q2s.at[0, 0], q2r.at[d - 1], sibling).wait_recv()
        q3.append(send(here, here, q3s.at[3 + d], q3r.at[3 + d], sibling))
    for copy in q3:
        copy.wait_recv()
    sent += q1 + q2 + q3

    for j in range(8):
        parts = []
        for k in (2 * j, 2 * j + 1):
            parts += [qh[0, k % 4, k // 4], qh[1, k // 4, k % 4]]
        term = jnp.dot(
            gbuf[:, j * 768 : (j + 1) * 768], jnp.concatenate(parts, axis=0), preferred_element_type=F32
        )
        if j == 0:
            pacc[...] = term
        else:
            pacc[...] += term

    for k in range(8):
        psend[k] = pacc[k * PIECE : (k + 1) * PIECE].astype(BF16)
    p1 = []
    for e in (4, 3, 5, 2, 6, 1, 7):
        other = lax.rem(r + e, 8)
        p1.append(send(psend.at[other], precv.at[r], p1s.at[e - 1], p1r.at[e - 1], (f, other)))
    precv[r] = psend[r]
    for copy in p1:
        copy.wait_recv()
    total = precv[0].astype(F32)
    for k in range(1, 8):
        total = total + precv[k].astype(F32)
    pall[r] = total.astype(BF16)
    p2 = []
    for e in (4, 3, 5, 2, 6, 1, 7):
        other = lax.rem(r + e, 8)
        p2.append(send(pall.at[r], pall.at[r], p2s.at[e - 1], p2r.at[e - 1], (f, other)))
    for copy in p2:
        copy.wait_recv()
    sent += p1 + p2

    p_full = pall[...].reshape(ROWS, RANK)
    pt[...] = p_full.T
    slot = c * 4 + z
    my_rows = pl.ds(pl.multiple_of(slot * 16, 16), 16)
    gsend[0, :16] = jnp.dot(pt[my_rows, :], p_full, preferred_element_type=F32)
    gsend[0, 16:] = sq[...]
    gx = [send(gsend.at[0], gxr.at[d - 1], gxs.at[d - 1], gxq.at[d - 1], (at_xy(d, 0), r)) for d in (1, 2, 3)]

    core = []
    order = ((z, x, y), (x, y, z), (y, z, x))

    def way(part, steps):
        dx, dy, dz = ((steps[1], steps[2], steps[0]), (steps[0], steps[1], steps[2]), (steps[2], steps[0], steps[1]))[
            part
        ]
        return (at_xy(dx, dy), at_z(dz))

    def multiply(part):
        for j in range(4):
            cols = [gbuf[:, pl.ds((4 * j + k) * ROWS + part * 128, 128)] for k in range(4)]
            block = jnp.dot(pt[...], jnp.concatenate(cols, axis=1), preferred_element_type=F32).astype(BF16)
            for k in range(4):
                for c2 in (0, 1):
                    for z2 in range(4):
                        at = c2 * 64 + z2 * 16
                        yl[c2, part, tile_of(part, j, k, z2)] = block[at : at + 16, k * 128 : (k + 1) * 128]
        core.append(send(yl.at[1 - c, part], yr.at[part], cs.at[part], cr.at[part], sibling))

    def add_core(part):
        core[part].wait_recv()
        for k in range(8):
            at = pl.ds(k * 8, 8)
            yc[part, at] = (yl[c, part, at].astype(F32) + yr[part, at].astype(F32)).astype(BF16)
        a0 = order[part][0]
        return [
            send(
                yc.at[part, pl.ds(mod4(a0 + d) * 16, 16)],
                rs1.at[part, d - 1],
                r1s.at[part, d - 1],
                r1r.at[part, d - 1],
                way(part, (d, 0, 0)),
            )
            for d in (2, 1, 3)
        ]

    def add_line(part):
        a0, a1, a2 = order[part]
        for copy in s1[part]:
            copy.wait_recv()
        value = yc[part, pl.ds(a0 * 16, 16)].astype(F32)
        for d in range(3):
            value = value + rs1[part, d].astype(F32)
        t1[part] = value.astype(BF16)
        return [
            send(
                t1.at[part, mod4(a1 + d) * 4 + mod4(a2 + e)],
                rs2.at[part, k],
                r2s.at[part],
                r2r.at[part],
                way(part, (0, d, e)),
            )
            for k, (d, e) in enumerate(PLANE)
        ]

    def add_plane(part):
        a0, a1, a2 = order[part]
        describe(rs2.at[part], rs2.at[part], r2s.at[part], r2r.at[part], sibling).wait_recv()
        value = t1[part, a1 * 4 + a2].astype(F32)
        for k in range(15):
            value = value + rs2[part, k].astype(F32)
        mine = a0 * 16 + a1 * 4 + a2
        gy[c, part, mine] = value.astype(BF16)
        here = gy.at[c, part, mine]
        for d, e in PLANE:
            send(here, here, a1s.at[part], a1r.at[part], way(part, (0, d, e)))

    multiply(0)
    multiply(1)
    s1 = [add_core(0)]
    multiply(2)
    s1 += [add_core(1), add_core(2)]
    for copy in gx:
        copy.wait_recv()
    gsend[1] = gsend[0] + gxr[0] + gxr[1] + gxr[2]
    gy1 = [send(gsend.at[1], gyr.at[d - 1], gys.at[d - 1], gyq.at[d - 1], (at_xy(0, d), r)) for d in (1, 2, 3)]
    add_line(0)
    for copy in gy1:
        copy.wait_recv()
    gmat[slot] = gsend[1] + gyr[0] + gyr[1] + gyr[2]
    g2 = [send(gmat.at[slot], gmat.at[slot], g2s.at[d - 1], g2r.at[d - 1], (f, at_z(d))) for d in (1, 2, 3)]
    add_line(1)
    add_line(2)
    for copy in g2:
        copy.wait_recv()
    side = gmat.at[pl.ds(c * 4, 4)]
    g3 = send(side, side, g3s.at[0], g3r.at[0], sibling)
    for part in range(3):
        add_plane(part)

    g3.wait_recv()
    for k in range(8):
        aug[k * 16 : (k + 1) * 16, :RANK] = gmat[k, :16]
    rows_i = lax.broadcasted_iota(jnp.int32, (RANK, RANK), 0)
    cols_i = lax.broadcasted_iota(jnp.int32, (RANK, RANK), 1)
    aug[:, RANK:] = jnp.where(rows_i == cols_i, 1.0, 0.0).astype(F32)
    sub = lax.broadcasted_iota(jnp.int32, (8, 128), 0)

    def panel(k, _):
        base = pl.multiple_of(k * 8, 8)
        rowp = aug[pl.ds(base, 8), :RANK]
        ext = aug[pl.ds(base, 8), RANK:]
        turned = pltpu.roll(rowp, lax.rem(128 - base, 128), 1)
        col = [jnp.broadcast_to(turned[:, j : j + 1], (8, 128)) for j in range(8)]
        for j in range(8):
            pivot = jnp.broadcast_to(col[j][j : j + 1, :], (8, 128))
            inv = lax.rsqrt(pivot)
            inv = inv * (1.5 - 0.5 * pivot * inv * inv)
            low = jnp.where(sub > j, col[j] * inv, 0.0)
            for m in range(j + 1, 8):
                col[m] = col[m] - low * jnp.broadcast_to(low[m : m + 1, :], (8, 128))
            row_r = jnp.broadcast_to(rowp[j : j + 1, :], (8, 128)) * inv
            row_e = jnp.broadcast_to(ext[j : j + 1, :], (8, 128)) * inv
            rowp = jnp.where(sub == j, row_r, rowp - low * row_r)
            ext = jnp.where(sub == j, row_e, ext - low * row_e)
        wbuf[pl.ds(base, 8), :] = ext
        v1, v2, v3 = split3(rowp)
        e1, e2, e3 = split3(ext)
        left = jnp.concatenate([v1, v1, v2, v2, v1, v3], axis=0).T.astype(BF16)
        top = jnp.concatenate([v1, v2, v1, v2, v3, v1], axis=0)
        more = jnp.concatenate([e1, e2, e1, e2, e3, e1], axis=0)
        both = jnp.concatenate([top, more], axis=1).astype(BF16)
        aug[...] -= jnp.dot(left, both, preferred_element_type=F32)
        return 0

    lines, passed = [], []

    def spread(part):
        a0 = order[part][0]
        here = gy.at[c, part, pl.ds(a0 * 16, 16)]
        region = rs2.at[part]
        describe(region, region, a1s.at[part], a1r.at[part], sibling).wait_recv()
        lines.append([
            send(here, here, a2s.at[part, d - 1], a2r.at[part, d - 1], way(part, (d, 0, 0))) for d in (1, 2, 3)
        ])
        passed.append([send(here, here, fs.at[part, 0], fr.at[part, 0], sibling)])

    lax.fori_loop(0, 9, panel, 0)
    for part in range(3):
        spread(part)
    lax.fori_loop(9, 16, panel, 0)

    w = wbuf[...]
    pb = jnp.zeros((ROWS, RANK), F32)
    p_again = pall[...].reshape(ROWS, RANK)
    for piece in split3(w)[::-1]:
        pb = pb + lax.dot_general(
            p_again, piece.astype(BF16), (((1,), (1,)), ((), ())), preferred_element_type=F32
        )
    basis_ref[...] = pb
    bmat[...] = (
        jnp.dot(pb, w, preferred_element_type=F32, precision=lax.Precision.HIGHEST) * 0.125
    ).astype(BF16)

    def right(part, x2, y2):
        tiles = [gy[c2, part, tile_of(part, x2, y2, z2)] for c2 in (0, 1) for z2 in range(4)]
        return jnp.concatenate(tiles, axis=0)

    def update(part, places):
        low = jnp.dot(
            bmat[...],
            jnp.concatenate([right(part, x2, y2) for x2, y2 in places], axis=1),
            preferred_element_type=F32,
        )
        for k, (x2, y2) in enumerate(places):
            cols = pl.ds(pl.multiple_of((x2 * 4 + y2) * ROWS + part * 128, 128), 128)
            new_ref[:, cols] = (gbuf[:, cols].astype(F32) - low[:, k * 128 : (k + 1) * 128]).astype(BF16)

    def group(part, a0):
        passed[part][-1].wait_recv()
        if part == 1:
            update(part, [(a0, k) for k in range(4)])
        if part == 2:
            update(part, [(k, a0) for k in range(4)])

    for part in range(3):
        group(part, order[part][0])
    for d in (1, 3, 2):
        for part in range(3):
            lines[part][d - 1].wait_recv()
            here = gy.at[c, part, pl.ds(mod4(order[part][0] - d) * 16, 16)]
            passed[part].append(send(here, here, fs.at[part, d], fr.at[part, d], sibling))
        for part in range(3):
            group(part, mod4(order[part][0] - d))
    for j in range(4):
        update(0, [(j, k) for k in range(4)])

    squares = jnp.sum(jnp.sum(gmat[:, 16:], axis=0))
    root_mean = jnp.sqrt(jnp.full((1, RANK), squares) / (8 * D * D) + 1e-06)
    scale = jnp.minimum(1.0, clip_ref[0, 0] / root_mean) * 0.125
    block = jnp.concatenate([right(part, x, y) for part in range(3)], axis=1)
    value = jnp.zeros((RANK, ROWS), F32)
    for piece in split3(wbuf[...])[::-1]:
        value = value + jnp.dot(piece.astype(BF16), block, preferred_element_type=F32)
    qout_ref[...] = value.T * scale

    for group_of in s1 + lines + passed:
        sent += group_of
    for copy in sent + gx + gy1 + g2 + [g3] + core:
        copy.wait_send()
    for part in range(3):
        region = rs2.at[part]
        for sems in (r2s, a1s):
            describe(region, region, sems.at[part], r2r.at[part], sibling).wait_send()


def hand_over(new_ref, basis_ref, q_ref, new_out, basis_out, q_out, sems):
    copies = [
        pltpu.make_async_copy(basis_ref, basis_out, sems.at[CHUNKS]),
        pltpu.make_async_copy(q_ref, q_out, sems.at[CHUNKS + 1]),
    ]
    for k in range(CHUNKS):
        rows = pl.ds(k * CHUNK, CHUNK)
        copies.append(pltpu.make_async_copy(new_ref.at[rows], new_out.at[rows], sems.at[k]))
    for copy in copies:
        copy.start()
    for copy in copies:
        copy.wait()


def body(grads, errors, q_start, clip_rms):
    dma = pltpu.SemaphoreType.DMA
    vmem = pltpu.VMEM
    hbm = pl.BlockSpec(memory_space=pltpu.HBM)
    inside = pl.BlockSpec(memory_space=pltpu.VMEM)
    new_errors, basis, q_out = pl.pallas_call(
        exchange,
        out_shape=(
            jax.ShapeDtypeStruct((ROWS, D), BF16),
            jax.ShapeDtypeStruct((ROWS, RANK), F32),
            jax.ShapeDtypeStruct((ROWS, RANK), F32),
        ),
        in_specs=[pl.BlockSpec(memory_space=pltpu.SMEM), hbm, hbm, hbm],
        out_specs=(inside, inside, inside),
        scratch_shapes=[
            vmem((ROWS, D), BF16),
            vmem((ROWS, D), BF16),
            vmem((HALF, RANK), F32),
            vmem((2, 4, 4, HALF, RANK), BF16),
            vmem((ROWS, RANK), F32),
            vmem((8, 128), F32),
            vmem((8, PIECE, RANK), BF16),
            vmem((8, PIECE, RANK), BF16),
            vmem((8, PIECE, RANK), BF16),
            vmem((RANK, ROWS), BF16),
            vmem((2, 24, RANK), F32),
            vmem((3, 24, RANK), F32),
            vmem((3, 24, RANK), F32),
            vmem((8, 24, RANK), F32),
            vmem((RANK, 2 * RANK), F32),
            vmem((RANK, RANK), F32),
            vmem((ROWS, RANK), BF16),
            vmem((2, 3, 64, 16, 128), BF16),
            vmem((3, 64, 16, 128), BF16),
            vmem((3, 64, 16, 128), BF16),
            vmem((3, 3, 16, 16, 128), BF16),
            vmem((3, 16, 16, 128), BF16),
            vmem((3, 15, 16, 128), BF16),
            vmem((2, 3, 64, 16, 128), BF16),
            dma((2, CHUNKS)),
            dma(()),
            dma((3,)),
            dma((3,)),
            dma((4, 3)),
            dma((3,)),
            dma((7,)),
            dma((7,)),
            dma((7,)),
            dma((7,)),
            dma((7,)),
            dma((7,)),
            dma((3,)),
            dma((3,)),
            dma((3,)),
            dma((3,)),
            dma((3,)),
            dma((3,)),
            dma((1,)),
            dma((1,)),
            dma((3,)),
            dma((3,)),
            dma((3, 3)),
            dma((3, 3)),
            dma((3, 3)),
            dma((3, 3)),
            dma((3,)),
            dma((3,)),
            dma((3,)),
            dma((3,)),
            dma((3, 4)),
            dma((3, 4)),
        ],
        compiler_params=pltpu.CompilerParams(
            collective_id=0, has_side_effects=True, vmem_limit_bytes=47 * 1024 * 1024
        ),
        name="exchange",
    )(clip_rms.reshape(1, 1), grads[0], errors[0], q_start)
    anywhere = pl.BlockSpec(memory_space=pl.ANY)
    new_errors, basis, q_out = pl.pallas_call(
        hand_over,
        out_shape=(
            jax.ShapeDtypeStruct((ROWS, D), BF16),
            jax.ShapeDtypeStruct((ROWS, RANK), F32),
            jax.ShapeDtypeStruct((ROWS, RANK), F32),
        ),
        in_specs=[anywhere] * 3,
        out_specs=(anywhere,) * 3,
        scratch_shapes=[dma((CHUNKS + 2,))],
        compiler_params=pltpu.CompilerParams(vmem_limit_bytes=1024 * 1024),
        name="hand_over",
    )(new_errors, basis, q_out)
    return new_errors[None], basis, q_out


def solution(mesh):
    return jax.shard_map(
        body,
        mesh=mesh,
        in_specs=(P("replica", "fsdp", None), P("replica", "fsdp", None), P("fsdp", None), P()),
        out_specs=(P("replica", "fsdp", None), P("fsdp", None), P("fsdp", None)),
        check_vma=False,
    )
```

```python
import jax
import jax.numpy as jnp
from jax import lax
from jax.experimental import pallas as pl
from jax.experimental.pallas import tpu as pltpu
from jax.sharding import PartitionSpec as P

MESH = pl.DeviceIdType.MESH
F32 = jnp.float32
BF16 = jnp.bfloat16

ROWS = 384
D = 6144
RANK = 128
CHUNKS = 8
CHUNK = ROWS // CHUNKS
HALF = ROWS // 2
PIECE = ROWS // 8
FAR = (2, 1, 3, 0)
PLANE = [(d, e) for d in FAR for e in FAR][:-1]


def mod4(v):
    return lax.rem(v + 4, 4)


def split3(v):
    a = v.astype(BF16).astype(F32)
    b = (v - a).astype(BF16).astype(F32)
    return a, b, (v - a - b).astype(BF16).astype(F32)


def tile_of(part, x, y, z):
    return (z * 16 + x * 4 + y, x * 16 + y * 4 + z, y * 16 + z * 4 + x)[part]


def exchange(
    clip_ref,
    grads,
    errors,
    q_ref,
    new_ref,
    basis_ref,
    qout_ref,
    gbuf,
    ebuf,
    qin,
    qh,
    pacc,
    sq,
    psend,
    precv,
    pall,
    pt,
    gsend,
    gxr,
    gyr,
    gmat,
    aug,
    wbuf,
    bmat,
    yl,
    yr,
    yc,
    rs1,
    t1,
    rs2,
    gy,
    load_sem,
    qin_sem,
    q1s,
    q1r,
    q2s,
    q2r,
    q3s,
    q3r,
    p1s,
    p1r,
    p2s,
    p2r,
    gxs,
    gxq,
    gys,
    gyq,
    g2s,
    g2r,
    g3s,
    g3r,
    cs,
    cr,
    r1s,
    r1r,
    a2s,
    a2r,
    r2s,
    r2r,
    a1s,
    a1r,
    fs,
    fr,
):
    f = lax.axis_index("fsdp")
    r = lax.axis_index("replica")
    x, y, z, c = f // 4, lax.rem(f, 4), r // 2, lax.rem(r, 2)
    sibling = (f, z * 2 + 1 - c)

    def at_xy(dx, dy):
        return mod4(x + dx) * 4 + mod4(y + dy)

    def at_z(dz):
        return mod4(z + dz) * 2 + c

    def describe(src, dst, ssem, rsem, device):
        return pltpu.make_async_remote_copy(
            src_ref=src, dst_ref=dst, send_sem=ssem, recv_sem=rsem, device_id=device, device_id_type=MESH
        )

    def send(src, dst, ssem, rsem, device):
        copy = describe(src, dst, ssem, rsem, device)
        copy.start()
        return copy

    sent = []

    qload = pltpu.make_async_copy(q_ref.at[pl.ds(pl.multiple_of(c * HALF, HALF), HALF)], qin, qin_sem)
    qload.start()

    barrier = pltpu.get_barrier_semaphore()
    peers = [sibling]
    for d in (1, 2, 3):
        peers += [(at_xy(d, 0), r), (at_xy(0, d), r), (f, at_z(d)), (f, mod4(z + d) * 2 + 1 - c)]
    for device in peers:
        pl.semaphore_signal(barrier, inc=1, device_id=device, device_id_type=MESH)

    loads = []
    for k in range(CHUNKS):
        rows = pl.ds(k * CHUNK, CHUNK)
        a = pltpu.make_async_copy(grads.at[rows], gbuf.at[rows], load_sem.at[0, k])
        b = pltpu.make_async_copy(errors.at[rows], ebuf.at[rows], load_sem.at[1, k])
        a.start()
        b.start()
        loads.append((a, b))

    s_me, t_me = jnp.where(c == 0, y, x), jnp.where(c == 0, x, y)
    qload.wait()
    filled = pl.ds(pl.multiple_of(c * 64, 64), HALF)
    for s in range(4):
        for t in range(4):
            qh[0, s, t, HALF:] = jnp.zeros((64, RANK), BF16)
            qh[1, s, t, :64] = jnp.zeros((64, RANK), BF16)
    qh[c, s_me, t_me, filled] = qin[...].astype(BF16)
    sq[...] = jnp.zeros_like(sq)
    pl.semaphore_wait(barrier, len(peers))

    def along_t(d):
        return (jnp.where(c == 0, at_xy(d, 0), at_xy(0, d)), r)

    def along_s(d):
        return (jnp.where(c == 0, at_xy(0, d), at_xy(d, 0)), r)

    own = qh.at[c, s_me, t_me, filled]
    q1 = [send(own, own, q1s.at[d - 1], q1r.at[d - 1], along_t(d)) for d in (1, 2, 3)]
    q2 = [send(own, own, q2s.at[0, d - 1], q2r.at[d - 1], along_s(d)) for d in (1, 2, 3)]
    q3 = [send(own, own, q3s.at[0], q3r.at[0], sibling)]

    def merge(k):
        a, b = loads[k]
        a.wait()
        b.wait()

        def group(i, _):
            rows = pl.ds(pl.multiple_of(k * CHUNK + i * 16, 16), 16)
            total = jnp.zeros((16, 128), F32)
            for j in range(D // 768):
                cols = pl.ds(j * 768, 768)
                m = gbuf[rows, cols].astype(F32) + ebuf[rows, cols].astype(F32)
                gbuf[rows, cols] = m.astype(BF16)
                m2 = m * m
                for i2 in range(6):
                    total = total + m2[:, i2 * 128 : (i2 + 1) * 128]
            sq[...] += total[:8] + total[8:]
            return 0

        lax.fori_loop(0, CHUNK // 16, group, 0)

    for k in range(3):
        merge(k)
    for d in (1, 3, 2):
        q1[d - 1].wait_recv()
        here = qh.at[c, s_me, mod4(t_me - d), filled]
        for e in (2, 1, 3):
            q2.append(send(here, here, q2s.at[d, e - 1], q2r.at[e - 1], along_s(e)))
        q3.append(send(here, here, q3s.at[d], q3r.at[d], sibling))
    for k in range(3, CHUNKS):
        merge(k)
    def add_p(half, s, first=False):
        cols = []
        for t in range(4):
            g = jnp.where(half == 0, t * 4 + s, s * 4 + t)
            cols.append(gbuf[:, pl.ds(pl.multiple_of(g * ROWS + half * 128, 128), 256)])
        term = jnp.dot(
            jnp.concatenate(cols, axis=1), qh[half, s].reshape(1024, RANK), preferred_element_type=F32
        )
        if first:
            pacc[...] = term
        else:
            pacc[...] += term

    def pass_q(d):
        here = qh.at[c, mod4(s_me - d), :, filled]
        describe(here, here, q2s.at[0, 0], q2r.at[d - 1], sibling).wait_recv()
        q3.append(send(here, here, q3s.at[3 + d], q3r.at[3 + d], sibling))
        add_p(c, mod4(s_me - d))

    add_p(c, s_me, True)
    pass_q(1)
    for copy in q3[:4]:
        copy.wait_recv()
    add_p(1 - c, t_me)
    pass_q(3)
    q3[4].wait_recv()
    add_p(1 - c, mod4(t_me - 1))
    pass_q(2)
    q3[5].wait_recv()
    add_p(1 - c, mod4(t_me - 3))
    q3[6].wait_recv()
    add_p(1 - c, mod4(t_me - 2))
    sent += q1 + q2 + q3

    for k in range(8):
        psend[k] = pacc[k * PIECE : (k + 1) * PIECE].astype(BF16)
    p1 = []
    for e in (4, 3, 5, 2, 6, 1, 7):
        other = lax.rem(r + e, 8)
        p1.append(send(psend.at[other], precv.at[r], p1s.at[e - 1], p1r.at[e - 1], (f, other)))
    precv[r] = psend[r]
    for copy in p1:
        copy.wait_recv()
    total = precv[0].astype(F32)
    for k in range(1, 8):
        total = total + precv[k].astype(F32)
    pall[r] = total.astype(BF16)
    p2 = []
    for e in (4, 3, 5, 2, 6, 1, 7):
        other = lax.rem(r + e, 8)
        p2.append(send(pall.at[r], pall.at[r], p2s.at[e - 1], p2r.at[e - 1], (f, other)))
    for copy in p2:
        copy.wait_recv()
    sent += p1 + p2

    p_full = pall[...].reshape(ROWS, RANK)
    pt[...] = p_full.T

    core = []
    order = ((z, x, y), (x, y, z), (y, z, x))

    def way(part, steps):
        dx, dy, dz = ((steps[1], steps[2], steps[0]), (steps[0], steps[1], steps[2]), (steps[2], steps[0], steps[1]))[
            part
        ]
        return (at_xy(dx, dy), at_z(dz))

    def multiply(part):
        for j in range(4):
            cols = [gbuf[:, pl.ds((4 * j + k) * ROWS + part * 128, 128)] for k in range(4)]
            block = jnp.dot(pt[...], jnp.concatenate(cols, axis=1), preferred_element_type=F32).astype(BF16)
            for k in range(4):
                for c2 in (0, 1):
                    for z2 in range(4):
                        at = c2 * 64 + z2 * 16
                        yl[c2, part, tile_of(part, j, k, z2)] = block[at : at + 16, k * 128 : (k + 1) * 128]
        core.append(send(yl.at[1 - c, part], yr.at[part], cs.at[part], cr.at[part], sibling))

    def add_core(part):
        core[part].wait_recv()
        for k in range(8):
            at = pl.ds(k * 8, 8)
            yc[part, at] = (yl[c, part, at].astype(F32) + yr[part, at].astype(F32)).astype(BF16)
        a0 = order[part][0]
        return [
            send(
                yc.at[part, pl.ds(mod4(a0 + d) * 16, 16)],
                rs1.at[part, d - 1],
                r1s.at[part, d - 1],
                r1r.at[part, d - 1],
                way(part, (d, 0, 0)),
            )
            for d in (2, 1, 3)
        ]

    def add_line(part):
        a0, a1, a2 = order[part]
        for copy in s1[part]:
            copy.wait_recv()
        value = yc[part, pl.ds(a0 * 16, 16)].astype(F32)
        for d in range(3):
            value = value + rs1[part, d].astype(F32)
        t1[part] = value.astype(BF16)
        return [
            send(
                t1.at[part, mod4(a1 + d) * 4 + mod4(a2 + e)],
                rs2.at[part, k],
                r2s.at[part],
                r2r.at[part],
                way(part, (0, d, e)),
            )
            for k, (d, e) in enumerate(PLANE)
        ]

    def add_plane(part):
        a0, a1, a2 = order[part]
        describe(rs2.at[part], rs2.at[part], r2s.at[part], r2r.at[part], sibling).wait_recv()
        value = t1[part, a1 * 4 + a2].astype(F32)
        for k in range(15):
            value = value + rs2[part, k].astype(F32)
        mine = a0 * 16 + a1 * 4 + a2
        gy[c, part, mine] = value.astype(BF16)
        here = gy.at[c, part, mine]
        for d, e in PLANE:
            send(here, here, a1s.at[part], a1r.at[part], way(part, (0, d, e)))

    multiply(0)
    multiply(1)

    slot = c * 4 + z
    my_rows = pl.ds(pl.multiple_of(slot * 16, 16), 16)
    gsend[0, :16] = jnp.dot(pt[my_rows, :], p_full, preferred_element_type=F32)
    gsend[0, 16:] = sq[...]
    gx = [send(gsend.at[0], gxr.at[d - 1], gxs.at[d - 1], gxq.at[d - 1], (at_xy(d, 0), r)) for d in (1, 2, 3)]

    s1 = [add_core(0)]
    multiply(2)
    s1 += [add_core(1), add_core(2)]
    for copy in gx:
        copy.wait_recv()
    gsend[1] = gsend[0] + gxr[0] + gxr[1] + gxr[2]
    gy1 = [send(gsend.at[1], gyr.at[d - 1], gys.at[d - 1], gyq.at[d - 1], (at_xy(0, d), r)) for d in (1, 2, 3)]
    add_line(0)
    for copy in gy1:
        copy.wait_recv()
    gmat[slot] = gsend[1] + gyr[0] + gyr[1] + gyr[2]
    g2 = [send(gmat.at[slot], gmat.at[slot], g2s.at[d - 1], g2r.at[d - 1], (f, at_z(d))) for d in (1, 2, 3)]
    add_line(1)
    add_line(2)
    for copy in g2:
        copy.wait_recv()
    side = gmat.at[pl.ds(c * 4, 4)]
    g3 = send(side, side, g3s.at[0], g3r.at[0], sibling)
    for part in range(3):
        add_plane(part)

    g3.wait_recv()
    for k in range(8):
        aug[k * 16 : (k + 1) * 16, :RANK] = gmat[k, :16]
    rows_i = lax.broadcasted_iota(jnp.int32, (RANK, RANK), 0)
    cols_i = lax.broadcasted_iota(jnp.int32, (RANK, RANK), 1)
    aug[:, RANK:] = jnp.where(rows_i == cols_i, 1.0, 0.0).astype(F32)
    sub = lax.broadcasted_iota(jnp.int32, (8, 128), 0)

    def panel(k, _):
        base = pl.multiple_of(k * 8, 8)
        rowp = aug[pl.ds(base, 8), :RANK]
        ext = aug[pl.ds(base, 8), RANK:]
        turned = pltpu.roll(rowp, lax.rem(128 - base, 128), 1)
        col = [jnp.broadcast_to(turned[:, j : j + 1], (8, 128)) for j in range(8)]
        for j in range(8):
            pivot = jnp.broadcast_to(col[j][j : j + 1, :], (8, 128))
            inv = lax.rsqrt(pivot)
            inv = inv * (1.5 - 0.5 * pivot * inv * inv)
            low = jnp.where(sub > j, col[j] * inv, 0.0)
            for m in range(j + 1, 8):
                col[m] = col[m] - low * jnp.broadcast_to(low[m : m + 1, :], (8, 128))
            row_r = jnp.broadcast_to(rowp[j : j + 1, :], (8, 128)) * inv
            row_e = jnp.broadcast_to(ext[j : j + 1, :], (8, 128)) * inv
            rowp = jnp.where(sub == j, row_r, rowp - low * row_r)
            ext = jnp.where(sub == j, row_e, ext - low * row_e)
        wbuf[pl.ds(base, 8), :] = ext
        v1, v2, v3 = split3(rowp)
        e1, e2, e3 = split3(ext)
        left = jnp.concatenate([v1, v1, v2, v2, v1, v3], axis=0).T.astype(BF16)
        top = jnp.concatenate([v1, v2, v1, v2, v3, v1], axis=0)
        more = jnp.concatenate([e1, e2, e1, e2, e3, e1], axis=0)
        both = jnp.concatenate([top, more], axis=1).astype(BF16)
        aug[...] -= jnp.dot(left, both, preferred_element_type=F32)
        return 0

    lines, passed = [], []

    def spread(part):
        a0 = order[part][0]
        here = gy.at[c, part, pl.ds(a0 * 16, 16)]
        region = rs2.at[part]
        describe(region, region, a1s.at[part], a1r.at[part], sibling).wait_recv()
        lines.append([
            send(here, here, a2s.at[part, d - 1], a2r.at[part, d - 1], way(part, (d, 0, 0))) for d in (1, 2, 3)
        ])
        passed.append([send(here, here, fs.at[part, 0], fr.at[part, 0], sibling)])

    lax.fori_loop(0, 9, panel, 0)
    for part in range(3):
        spread(part)
    for group_of in s1:
        sent += group_of
    for copy in sent + gx + gy1 + g2 + [g3] + core:
        copy.wait_send()
    for part in range(3):
        region = rs2.at[part]
        for sems in (r2s, a1s):
            describe(region, region, sems.at[part], r2r.at[part], sibling).wait_send()
    lax.fori_loop(9, 16, panel, 0)

    w = wbuf[...]
    pb = jnp.zeros((ROWS, RANK), F32)
    p_again = pall[...].reshape(ROWS, RANK)
    for piece in split3(w)[::-1]:
        pb = pb + lax.dot_general(
            p_again, piece.astype(BF16), (((1,), (1,)), ((), ())), preferred_element_type=F32
        )
    basis_ref[...] = pb
    bmat[...] = (
        jnp.dot(pb, w, preferred_element_type=F32, precision=lax.Precision.HIGHEST) * 0.125
    ).astype(BF16)

    def right(part, x2, y2):
        tiles = [gy[c2, part, tile_of(part, x2, y2, z2)] for c2 in (0, 1) for z2 in range(4)]
        return jnp.concatenate(tiles, axis=0)

    def update(part, places):
        low = jnp.dot(
            bmat[...],
            jnp.concatenate([right(part, x2, y2) for x2, y2 in places], axis=1),
            preferred_element_type=F32,
        )
        for k, (x2, y2) in enumerate(places):
            cols = pl.ds(pl.multiple_of((x2 * 4 + y2) * ROWS + part * 128, 128), 128)
            new_ref[:, cols] = (gbuf[:, cols].astype(F32) - low[:, k * 128 : (k + 1) * 128]).astype(BF16)

    def pass_line(d):
        for part in range(3):
            lines[part][d - 1].wait_recv()
            here = gy.at[c, part, pl.ds(mod4(order[part][0] - d) * 16, 16)]
            passed[part].append(send(here, here, fs.at[part, d], fr.at[part, d], sibling))

    def groups(d):
        for part in range(3):
            passed[part][(0, 1, 3, 2)[d]].wait_recv()
            a0 = mod4(order[part][0] - d)
            if part == 1:
                update(part, [(a0, k) for k in range(4)])
            if part == 2:
                update(part, [(k, a0) for k in range(4)])

    groups(0)
    pass_line(1)
    pass_line(3)
    groups(1)
    pass_line(2)
    groups(3)
    groups(2)
    for j in range(4):
        update(0, [(j, k) for k in range(4)])

    squares = jnp.sum(jnp.sum(gmat[:, 16:], axis=0))
    root_mean = jnp.sqrt(jnp.full((1, RANK), squares) / (8 * D * D) + 1e-06)
    scale = jnp.minimum(1.0, clip_ref[0, 0] / root_mean) * 0.125
    block = jnp.concatenate([right(part, x, y) for part in range(3)], axis=1)
    value = jnp.zeros((RANK, ROWS), F32)
    for piece in split3(wbuf[...])[::-1]:
        value = value + jnp.dot(piece.astype(BF16), block, preferred_element_type=F32)
    qout_ref[...] = value.T * scale

    for group_of in lines + passed:
        for copy in group_of:
            copy.wait_send()


def hand_over(new_ref, basis_ref, q_ref, new_out, basis_out, q_out, sems):
    copies = [
        pltpu.make_async_copy(basis_ref, basis_out, sems.at[CHUNKS]),
        pltpu.make_async_copy(q_ref, q_out, sems.at[CHUNKS + 1]),
    ]
    for k in range(CHUNKS):
        rows = pl.ds(k * CHUNK, CHUNK)
        copies.append(pltpu.make_async_copy(new_ref.at[rows], new_out.at[rows], sems.at[k]))
    for copy in copies:
        copy.start()
    for copy in copies:
        copy.wait()


def body(grads, errors, q_start, clip_rms):
    dma = pltpu.SemaphoreType.DMA
    vmem = pltpu.VMEM
    hbm = pl.BlockSpec(memory_space=pltpu.HBM)
    inside = pl.BlockSpec(memory_space=pltpu.VMEM)
    new_errors, basis, q_out = pl.pallas_call(
        exchange,
        out_shape=(
            jax.ShapeDtypeStruct((ROWS, D), BF16),
            jax.ShapeDtypeStruct((ROWS, RANK), F32),
            jax.ShapeDtypeStruct((ROWS, RANK), F32),
        ),
        in_specs=[pl.BlockSpec(memory_space=pltpu.SMEM), hbm, hbm, hbm],
        out_specs=(inside, inside, inside),
        scratch_shapes=[
            vmem((ROWS, D), BF16),
            vmem((ROWS, D), BF16),
            vmem((HALF, RANK), F32),
            vmem((2, 4, 4, 256, RANK), BF16),
            vmem((ROWS, RANK), F32),
            vmem((8, 128), F32),
            vmem((8, PIECE, RANK), BF16),
            vmem((8, PIECE, RANK), BF16),
            vmem((8, PIECE, RANK), BF16),
            vmem((RANK, ROWS), BF16),
            vmem((2, 24, RANK), F32),
            vmem((3, 24, RANK), F32),
            vmem((3, 24, RANK), F32),
            vmem((8, 24, RANK), F32),
            vmem((RANK, 2 * RANK), F32),
            vmem((RANK, RANK), F32),
            vmem((ROWS, RANK), BF16),
            vmem((2, 3, 64, 16, 128), BF16),
            vmem((3, 64, 16, 128), BF16),
            vmem((3, 64, 16, 128), BF16),
            vmem((3, 3, 16, 16, 128), BF16),
            vmem((3, 16, 16, 128), BF16),
            vmem((3, 15, 16, 128), BF16),
            vmem((2, 3, 64, 16, 128), BF16),
            dma((2, CHUNKS)),
            dma(()),
            dma((3,)),
            dma((3,)),
            dma((4, 3)),
            dma((3,)),
            dma((7,)),
            dma((7,)),
            dma((7,)),
            dma((7,)),
            dma((7,)),
            dma((7,)),
            dma((3,)),
            dma((3,)),
            dma((3,)),
            dma((3,)),
            dma((3,)),
            dma((3,)),
            dma((1,)),
            dma((1,)),
            dma((3,)),
            dma((3,)),
            dma((3, 3)),
            dma((3, 3)),
            dma((3, 3)),
            dma((3, 3)),
            dma((3,)),
            dma((3,)),
            dma((3,)),
            dma((3,)),
            dma((3, 4)),
            dma((3, 4)),
        ],
        compiler_params=pltpu.CompilerParams(
            collective_id=0, has_side_effects=True, vmem_limit_bytes=47 * 1024 * 1024
        ),
        name="exchange",
    )(clip_rms.reshape(1, 1), grads[0], errors[0], q_start)
    anywhere = pl.BlockSpec(memory_space=pl.ANY)
    new_errors, basis, q_out = pl.pallas_call(
        hand_over,
        out_shape=(
            jax.ShapeDtypeStruct((ROWS, D), BF16),
            jax.ShapeDtypeStruct((ROWS, RANK), F32),
            jax.ShapeDtypeStruct((ROWS, RANK), F32),
        ),
        in_specs=[anywhere] * 3,
        out_specs=(anywhere,) * 3,
        scratch_shapes=[dma((CHUNKS + 2,))],
        compiler_params=pltpu.CompilerParams(vmem_limit_bytes=1024 * 1024),
        name="hand_over",
    )(new_errors, basis, q_out)
    return new_errors[None], basis, q_out


def solution(mesh):
    return jax.shard_map(
        body,
        mesh=mesh,
        in_specs=(P("replica", "fsdp", None), P("replica", "fsdp", None), P("fsdp", None), P()),
        out_specs=(P("replica", "fsdp", None), P("fsdp", None), P("fsdp", None)),
        check_vma=False,
    )
```

```python
import jax
import jax.numpy as jnp
from jax import lax
from jax.experimental import pallas as pl
from jax.experimental.pallas import tpu as pltpu
from jax.sharding import PartitionSpec as P

MESH = pl.DeviceIdType.MESH
F32 = jnp.float32
BF16 = jnp.bfloat16

ROWS = 384
D = 6144
RANK = 128
CHUNKS = 8
CHUNK = ROWS // CHUNKS
HALF = ROWS // 2
PIECE = ROWS // 8
FAR = (2, 1, 3, 0)
PLANE = [(d, e) for d in FAR for e in FAR][:-1]


def mod4(v):
    return lax.rem(v + 4, 4)


def split3(v):
    a = v.astype(BF16).astype(F32)
    b = (v - a).astype(BF16).astype(F32)
    return a, b, (v - a - b).astype(BF16).astype(F32)


def tile_of(part, x, y, z):
    return (z * 16 + x * 4 + y, x * 16 + y * 4 + z, y * 16 + z * 4 + x)[part]


def exchange(
    clip_ref,
    grads,
    errors,
    q_ref,
    new_ref,
    basis_ref,
    qout_ref,
    gbuf,
    ebuf,
    qin,
    qh,
    pacc,
    sq,
    psend,
    precv,
    pall,
    pt,
    gsend,
    gxr,
    gyr,
    gmat,
    aug,
    wbuf,
    bmat,
    yl,
    yr,
    yc,
    rs1,
    t1,
    rs2,
    gy,
    load_sem,
    qin_sem,
    q1s,
    q1r,
    q2s,
    q2r,
    q3s,
    q3r,
    p1s,
    p1r,
    p2s,
    p2r,
    gxs,
    gxq,
    gys,
    gyq,
    g2s,
    g2r,
    g3s,
    g3r,
    cs,
    cr,
    r1s,
    r1r,
    a2s,
    a2r,
    r2s,
    r2r,
    a1s,
    a1r,
    fs,
    fr,
):
    f = lax.axis_index("fsdp")
    r = lax.axis_index("replica")
    x, y, z, c = f // 4, lax.rem(f, 4), r // 2, lax.rem(r, 2)
    sibling = (f, z * 2 + 1 - c)

    def at_xy(dx, dy):
        return mod4(x + dx) * 4 + mod4(y + dy)

    def at_z(dz):
        return mod4(z + dz) * 2 + c

    def describe(src, dst, ssem, rsem, device):
        return pltpu.make_async_remote_copy(
            src_ref=src, dst_ref=dst, send_sem=ssem, recv_sem=rsem, device_id=device, device_id_type=MESH
        )

    def send(src, dst, ssem, rsem, device):
        copy = describe(src, dst, ssem, rsem, device)
        copy.start()
        return copy

    sent = []

    qload = pltpu.make_async_copy(q_ref.at[pl.ds(pl.multiple_of(c * HALF, HALF), HALF)], qin, qin_sem)
    qload.start()

    barrier = pltpu.get_barrier_semaphore()
    peers = [sibling]
    for d in (1, 2, 3):
        peers += [(at_xy(d, 0), r), (at_xy(0, d), r), (f, at_z(d)), (f, mod4(z + d) * 2 + 1 - c)]
    for device in peers:
        pl.semaphore_signal(barrier, inc=1, device_id=device, device_id_type=MESH)

    loads = []
    for k in range(CHUNKS):
        rows = pl.ds(k * CHUNK, CHUNK)
        a = pltpu.make_async_copy(grads.at[rows], gbuf.at[rows], load_sem.at[0, k])
        b = pltpu.make_async_copy(errors.at[rows], ebuf.at[rows], load_sem.at[1, k])
        a.start()
        b.start()
        loads.append((a, b))

    s_me, t_me = jnp.where(c == 0, y, x), jnp.where(c == 0, x, y)
    qload.wait()
    filled = pl.ds(pl.multiple_of(c * 64, 64), HALF)
    for s in range(4):
        for t in range(4):
            qh[0, s, t, HALF:] = jnp.zeros((64, RANK), BF16)
            qh[1, s, t, :64] = jnp.zeros((64, RANK), BF16)
    qh[c, s_me, t_me, filled] = qin[...].astype(BF16)
    sq[...] = jnp.zeros_like(sq)
    pl.semaphore_wait(barrier, len(peers))

    def along_t(d):
        return (jnp.where(c == 0, at_xy(d, 0), at_xy(0, d)), r)

    def along_s(d):
        return (jnp.where(c == 0, at_xy(0, d), at_xy(d, 0)), r)

    own = qh.at[c, s_me, t_me, filled]
    q1 = [send(own, own, q1s.at[d - 1], q1r.at[d - 1], along_t(d)) for d in (1, 2, 3)]
    q2 = [send(own, own, q2s.at[0, d - 1], q2r.at[d - 1], along_s(d)) for d in (1, 2, 3)]
    q3 = [send(own, own, q3s.at[0], q3r.at[0], sibling)]

    def merge(k):
        a, b = loads[k]
        a.wait()
        b.wait()

        def group(i, _):
            rows = pl.ds(pl.multiple_of(k * CHUNK + i * 16, 16), 16)
            total = jnp.zeros((16, 128), F32)
            for j in range(D // 768):
                cols = pl.ds(j * 768, 768)
                m = gbuf[rows, cols].astype(F32) + ebuf[rows, cols].astype(F32)
                gbuf[rows, cols] = m.astype(BF16)
                m2 = m * m
                for i2 in range(6):
                    total = total + m2[:, i2 * 128 : (i2 + 1) * 128]
            sq[...] += total[:8] + total[8:]
            return 0

        lax.fori_loop(0, CHUNK // 16, group, 0)

    for k in range(3):
        merge(k)
    for d in (1, 3, 2):
        q1[d - 1].wait_recv()
        here = qh.at[c, s_me, mod4(t_me - d), filled]
        for e in (2, 1, 3):
            q2.append(send(here, here, q2s.at[d, e - 1], q2r.at[e - 1], along_s(e)))
        q3.append(send(here, here, q3s.at[d], q3r.at[d], sibling))
    for k in range(3, CHUNKS):
        merge(k)
    def add_p(half, s, first=False):
        cols = []
        for t in range(4):
            g = jnp.where(half == 0, t * 4 + s, s * 4 + t)
            cols.append(gbuf[:, pl.ds(pl.multiple_of(g * ROWS + half * 128, 128), 256)])
        term = jnp.dot(
            jnp.concatenate(cols, axis=1), qh[half, s].reshape(1024, RANK), preferred_element_type=F32
        )
        if first:
            pacc[...] = term
        else:
            pacc[...] += term

    def pass_q(d):
        here = qh.at[c, mod4(s_me - d), :, filled]
        describe(here, here, q2s.at[0, 0], q2r.at[d - 1], sibling).wait_recv()
        q3.append(send(here, here, q3s.at[3 + d], q3r.at[3 + d], sibling))
        add_p(c, mod4(s_me - d))

    add_p(c, s_me, True)
    pass_q(1)
    for copy in q3[:4]:
        copy.wait_recv()
    add_p(1 - c, t_me)
    pass_q(3)
    q3[4].wait_recv()
    add_p(1 - c, mod4(t_me - 1))
    pass_q(2)
    q3[5].wait_recv()
    add_p(1 - c, mod4(t_me - 3))
    q3[6].wait_recv()
    add_p(1 - c, mod4(t_me - 2))
    sent += q1 + q2 + q3

    for k in range(8):
        psend[k] = pacc[k * PIECE : (k + 1) * PIECE].astype(BF16)
    p1 = []
    for e in (4, 3, 5, 2, 6, 1, 7):
        other = lax.rem(r + e, 8)
        p1.append(send(psend.at[other], precv.at[r], p1s.at[e - 1], p1r.at[e - 1], (f, other)))
    precv[r] = psend[r]
    for copy in p1:
        copy.wait_recv()
    total = precv[0].astype(F32)
    for k in range(1, 8):
        total = total + precv[k].astype(F32)
    pall[r] = total.astype(BF16)
    p2 = []
    for e in (4, 3, 5, 2, 6, 1, 7):
        other = lax.rem(r + e, 8)
        p2.append(send(pall.at[r], pall.at[r], p2s.at[e - 1], p2r.at[e - 1], (f, other)))
    for copy in p2:
        copy.wait_recv()
    sent += p1 + p2

    p_full = pall[...].reshape(ROWS, RANK)
    pt[...] = p_full.T

    slot = c * 4 + z
    my_rows = pl.ds(pl.multiple_of(slot * 16, 16), 16)
    gsend[0, :16] = jnp.dot(pt[my_rows, :], p_full, preferred_element_type=F32)
    gsend[0, 16:] = sq[...]
    gx = [
        send(gsend.at[0], gxr.at[k], gxs.at[k], gxq.at[k], (at_xy(dx, dy), r)) for k, (dx, dy) in enumerate(PLANE)
    ]

    core, s1 = {}, ([], [], [])
    order = ((z, x, y), (x, y, z), (y, z, x))

    def way(part, steps):
        dx, dy, dz = ((steps[1], steps[2], steps[0]), (steps[0], steps[1], steps[2]), (steps[2], steps[0], steps[1]))[
            part
        ]
        return (at_xy(dx, dy), at_z(dz))

    def multiply(part, places):
        cols = [
            gbuf[:, pl.ds(pl.multiple_of((x2 * 4 + y2) * ROWS + part * 128, 128), 128)] for x2, y2 in places
        ]
        block = jnp.dot(pt[...], jnp.concatenate(cols, axis=1), preferred_element_type=F32).astype(BF16)
        for k, (x2, y2) in enumerate(places):
            for c2 in (0, 1):
                for z2 in range(4):
                    at = c2 * 64 + z2 * 16
                    yl[c2, part, tile_of(part, x2, y2, z2)] = block[at : at + 16, k * 128 : (k + 1) * 128]

    def line(part, d):
        return pl.ds(pl.multiple_of(mod4(order[part][0] + d) * 16, 16), 16)

    def swap(part, d):
        at = line(part, d)
        core[part, d] = send(yl.at[1 - c, part, at], yr.at[part, at], cs.at[part, d], cr.at[part, d], sibling)

    def add_core(part, d):
        at = line(part, d)
        core[part, d].wait_recv()
        yc[part, at] = (yl[c, part, at].astype(F32) + yr[part, at].astype(F32)).astype(BF16)
        if d:
            s1[part].append(
                send(
                    yc.at[part, at],
                    rs1.at[part, d - 1],
                    r1s.at[part, d - 1],
                    r1r.at[part, d - 1],
                    way(part, (d, 0, 0)),
                )
            )

    def add_line(part):
        a0, a1, a2 = order[part]
        for copy in s1[part]:
            copy.wait_recv()
        value = yc[part, pl.ds(a0 * 16, 16)].astype(F32)
        for d in range(3):
            value = value + rs1[part, d].astype(F32)
        t1[part] = value.astype(BF16)
        return [
            send(
                t1.at[part, mod4(a1 + d) * 4 + mod4(a2 + e)],
                rs2.at[part, k],
                r2s.at[part],
                r2r.at[part],
                way(part, (0, d, e)),
            )
            for k, (d, e) in enumerate(PLANE)
        ]

    def add_plane(part):
        a0, a1, a2 = order[part]
        describe(rs2.at[part], rs2.at[part], r2s.at[part], r2r.at[part], sibling).wait_recv()
        value = t1[part, a1 * 4 + a2].astype(F32)
        for k in range(15):
            value = value + rs2[part, k].astype(F32)
        mine = a0 * 16 + a1 * 4 + a2
        gy[c, part, mine] = value.astype(BF16)
        here = gy.at[c, part, mine]
        for d, e in PLANE:
            send(here, here, a1s.at[part], a1r.at[part], way(part, (0, d, e)))

    for j in range(4):
        multiply(0, [(j, k) for k in range(4)])
    for d in FAR:
        swap(0, d)
    for d in FAR:
        multiply(1, [(mod4(x + d), k) for k in range(4)])
        swap(1, d)
    for d in FAR:
        multiply(2, [(k, mod4(y + d)) for k in range(4)])
        swap(2, d)
        add_core(0, d)

    for part in (1, 2):
        for d in FAR:
            add_core(part, d)
    add_line(0)
    for copy in gx:
        copy.wait_recv()
    gsum = gsend[0]
    for k in range(15):
        gsum = gsum + gxr[k]
    gmat[slot] = gsum
    g2 = [send(gmat.at[slot], gmat.at[slot], g2s.at[d - 1], g2r.at[d - 1], (f, at_z(d))) for d in (1, 2, 3)]
    add_line(1)
    add_line(2)
    for copy in g2:
        copy.wait_recv()
    side = gmat.at[pl.ds(c * 4, 4)]
    g3 = send(side, side, g3s.at[0], g3r.at[0], sibling)
    for part in range(3):
        add_plane(part)

    g3.wait_recv()
    for k in range(8):
        aug[k * 16 : (k + 1) * 16, :RANK] = gmat[k, :16]
    rows_i = lax.broadcasted_iota(jnp.int32, (RANK, RANK), 0)
    cols_i = lax.broadcasted_iota(jnp.int32, (RANK, RANK), 1)
    aug[:, RANK:] = jnp.where(rows_i == cols_i, 1.0, 0.0).astype(F32)
    sub = lax.broadcasted_iota(jnp.int32, (8, 128), 0)

    def spread_row(v, i):
        return jnp.broadcast_to(v[i : i + 1, :], (8, 128))

    def panel(k, _):
        base = pl.multiple_of(k * 16, 16)
        halves = (pl.ds(base, 8), pl.ds(base + 8, 8))
        rowp = [aug[at, :RANK] for at in halves]
        ext = [aug[at, RANK:] for at in halves]
        turned = [pltpu.roll(v, lax.rem(128 - base, 128), 1) for v in rowp]
        col = [[jnp.broadcast_to(v[:, j : j + 1], (8, 128)) for v in turned] for j in range(16)]
        diag = [jnp.ones((8, 128), F32)] * 2
        for j in range(16):
            top, i = j // 8, j % 8
            pivot = spread_row(col[j][top], i)
            inv = 1.0 / pivot
            low = [None, None]
            for h in range(top, 2):
                low[h] = col[j][h] * inv
            low[top] = jnp.where(sub > i, low[top], 0.0)
            pivots = [spread_row(col[m][top], i) for m in range(j + 1, 16)]
            row_r, row_e = spread_row(rowp[top], i), spread_row(ext[top], i)
            for h in range(top, 2):
                for m in range(j + 1, 16):
                    col[m][h] = col[m][h] - low[h] * pivots[m - j - 1]
                rowp[h] = rowp[h] - low[h] * row_r
                ext[h] = ext[h] - low[h] * row_e
            diag[top] = jnp.where(sub == i, pivot, diag[top])
        for h in (0, 1):
            inv = lax.rsqrt(diag[h])
            inv = inv * (1.5 - 0.5 * diag[h] * inv * inv)
            rowp[h] = rowp[h] * inv
            ext[h] = ext[h] * inv
            wbuf[halves[h], :] = ext[h]
        v1, v2, v3 = split3(jnp.concatenate(rowp, axis=0))
        e1, e2, e3 = split3(jnp.concatenate(ext, axis=0))
        left = jnp.concatenate([v1, v1, v2, v2, v1, v3], axis=0).T.astype(BF16)
        top = jnp.concatenate([v1, v2, v1, v2, v3, v1], axis=0)
        more = jnp.concatenate([e1, e2, e1, e2, e3, e1], axis=0)
        both = jnp.concatenate([top, more], axis=1).astype(BF16)
        aug[...] -= jnp.dot(left, both, preferred_element_type=F32)
        return 0

    lines, passed = [], []

    def spread(part):
        a0 = order[part][0]
        here = gy.at[c, part, pl.ds(a0 * 16, 16)]
        region = rs2.at[part]
        describe(region, region, a1s.at[part], a1r.at[part], sibling).wait_recv()
        lines.append([
            send(here, here, a2s.at[part, d - 1], a2r.at[part, d - 1], way(part, (d, 0, 0))) for d in (1, 2, 3)
        ])
        passed.append([send(here, here, fs.at[part, 0], fr.at[part, 0], sibling)])

    lax.fori_loop(0, 5, panel, 0)
    spread(0)
    lax.fori_loop(5, 6, panel, 0)
    spread(1)
    lax.fori_loop(6, 7, panel, 0)
    spread(2)
    for group_of in s1:
        sent += group_of
    for copy in sent + gx + g2 + [g3] + list(core.values()):
        copy.wait_send()
    for part in range(3):
        region = rs2.at[part]
        for sems in (r2s, a1s):
            describe(region, region, sems.at[part], r2r.at[part], sibling).wait_send()
    lax.fori_loop(7, 8, panel, 0)

    w = wbuf[...]
    pb = jnp.zeros((ROWS, RANK), F32)
    p_again = pall[...].reshape(ROWS, RANK)
    for piece in split3(w)[::-1]:
        pb = pb + lax.dot_general(
            p_again, piece.astype(BF16), (((1,), (1,)), ((), ())), preferred_element_type=F32
        )
    basis_ref[...] = pb
    bmat[...] = (
        jnp.dot(pb, w, preferred_element_type=F32, precision=lax.Precision.HIGHEST) * 0.125
    ).astype(BF16)

    def right(part, x2, y2):
        tiles = [gy[c2, part, tile_of(part, x2, y2, z2)] for c2 in (0, 1) for z2 in range(4)]
        return jnp.concatenate(tiles, axis=0)

    def update(part, places):
        low = jnp.dot(
            bmat[...],
            jnp.concatenate([right(part, x2, y2) for x2, y2 in places], axis=1),
            preferred_element_type=F32,
        )
        for k, (x2, y2) in enumerate(places):
            cols = pl.ds(pl.multiple_of((x2 * 4 + y2) * ROWS + part * 128, 128), 128)
            new_ref[:, cols] = (gbuf[:, cols].astype(F32) - low[:, k * 128 : (k + 1) * 128]).astype(BF16)

    def pass_line(d):
        for part in range(3):
            lines[part][d - 1].wait_recv()
            here = gy.at[c, part, pl.ds(mod4(order[part][0] - d) * 16, 16)]
            passed[part].append(send(here, here, fs.at[part, d], fr.at[part, d], sibling))

    def groups(d):
        for part in range(3):
            passed[part][(0, 1, 3, 2)[d]].wait_recv()
            a0 = mod4(order[part][0] - d)
            if part == 1:
                update(part, [(a0, k) for k in range(4)])
            if part == 2:
                update(part, [(k, a0) for k in range(4)])

    groups(0)
    pass_line(1)
    pass_line(3)
    groups(1)
    pass_line(2)
    groups(3)
    groups(2)
    for j in range(4):
        update(0, [(j, k) for k in range(4)])

    squares = jnp.sum(jnp.sum(gmat[:, 16:], axis=0))
    root_mean = jnp.sqrt(jnp.full((1, RANK), squares) / (8 * D * D) + 1e-06)
    scale = jnp.minimum(1.0, clip_ref[0, 0] / root_mean) * 0.125
    block = jnp.concatenate([right(part, x, y) for part in range(3)], axis=1)
    value = jnp.zeros((RANK, ROWS), F32)
    for piece in split3(wbuf[...])[::-1]:
        value = value + jnp.dot(piece.astype(BF16), block, preferred_element_type=F32)
    qout_ref[...] = value.T * scale

    for group_of in lines + passed:
        for copy in group_of:
            copy.wait_send()


def hand_over(new_ref, basis_ref, q_ref, new_out, basis_out, q_out, sems):
    copies = [
        pltpu.make_async_copy(basis_ref, basis_out, sems.at[CHUNKS]),
        pltpu.make_async_copy(q_ref, q_out, sems.at[CHUNKS + 1]),
    ]
    for k in range(CHUNKS):
        rows = pl.ds(k * CHUNK, CHUNK)
        copies.append(pltpu.make_async_copy(new_ref.at[rows], new_out.at[rows], sems.at[k]))
    for copy in copies:
        copy.start()
    for copy in copies:
        copy.wait()


def body(grads, errors, q_start, clip_rms):
    dma = pltpu.SemaphoreType.DMA
    vmem = pltpu.VMEM
    hbm = pl.BlockSpec(memory_space=pltpu.HBM)
    inside = pl.BlockSpec(memory_space=pltpu.VMEM)
    new_errors, basis, q_out = pl.pallas_call(
        exchange,
        out_shape=(
            jax.ShapeDtypeStruct((ROWS, D), BF16),
            jax.ShapeDtypeStruct((ROWS, RANK), F32),
            jax.ShapeDtypeStruct((ROWS, RANK), F32),
        ),
        in_specs=[pl.BlockSpec(memory_space=pltpu.SMEM), hbm, hbm, hbm],
        out_specs=(inside, inside, inside),
        scratch_shapes=[
            vmem((ROWS, D), BF16),
            vmem((ROWS, D), BF16),
            vmem((HALF, RANK), F32),
            vmem((2, 4, 4, 256, RANK), BF16),
            vmem((ROWS, RANK), F32),
            vmem((8, 128), F32),
            vmem((8, PIECE, RANK), BF16),
            vmem((8, PIECE, RANK), BF16),
            vmem((8, PIECE, RANK), BF16),
            vmem((RANK, ROWS), BF16),
            vmem((2, 24, RANK), F32),
            vmem((15, 24, RANK), F32),
            vmem((3, 24, RANK), F32),
            vmem((8, 24, RANK), F32),
            vmem((RANK, 2 * RANK), F32),
            vmem((RANK, RANK), F32),
            vmem((ROWS, RANK), BF16),
            vmem((2, 3, 64, 16, 128), BF16),
            vmem((3, 64, 16, 128), BF16),
            vmem((3, 64, 16, 128), BF16),
            vmem((3, 3, 16, 16, 128), BF16),
            vmem((3, 16, 16, 128), BF16),
            vmem((3, 15, 16, 128), BF16),
            vmem((2, 3, 64, 16, 128), BF16),
            dma((2, CHUNKS)),
            dma(()),
            dma((3,)),
            dma((3,)),
            dma((4, 3)),
            dma((3,)),
            dma((7,)),
            dma((7,)),
            dma((7,)),
            dma((7,)),
            dma((7,)),
            dma((7,)),
            dma((15,)),
            dma((15,)),
            dma((3,)),
            dma((3,)),
            dma((3,)),
            dma((3,)),
            dma((1,)),
            dma((1,)),
            dma((3, 4)),
            dma((3, 4)),
            dma((3, 3)),
            dma((3, 3)),
            dma((3, 3)),
            dma((3, 3)),
            dma((3,)),
            dma((3,)),
            dma((3,)),
            dma((3,)),
            dma((3, 4)),
            dma((3, 4)),
        ],
        compiler_params=pltpu.CompilerParams(
            collective_id=0, has_side_effects=True, vmem_limit_bytes=47 * 1024 * 1024
        ),
        name="exchange",
    )(clip_rms.reshape(1, 1), grads[0], errors[0], q_start)
    anywhere = pl.BlockSpec(memory_space=pl.ANY)
    new_errors, basis, q_out = pl.pallas_call(
        hand_over,
        out_shape=(
            jax.ShapeDtypeStruct((ROWS, D), BF16),
            jax.ShapeDtypeStruct((ROWS, RANK), F32),
            jax.ShapeDtypeStruct((ROWS, RANK), F32),
        ),
        in_specs=[anywhere] * 3,
        out_specs=(anywhere,) * 3,
        scratch_shapes=[dma((CHUNKS + 2,))],
        compiler_params=pltpu.CompilerParams(vmem_limit_bytes=1024 * 1024),
        name="hand_over",
    )(new_errors, basis, q_out)
    return new_errors[None], basis, q_out


def solution(mesh):
    return jax.shard_map(
        body,
        mesh=mesh,
        in_specs=(P("replica", "fsdp", None), P("replica", "fsdp", None), P("fsdp", None), P()),
        out_specs=(P("replica", "fsdp", None), P("fsdp", None), P("fsdp", None)),
        check_vma=False,
    )
```

```python
import jax
import jax.numpy as jnp
from jax import lax
from jax.experimental import pallas as pl
from jax.experimental.pallas import tpu as pltpu
from jax.sharding import PartitionSpec as P

MESH = pl.DeviceIdType.MESH
F32 = jnp.float32
BF16 = jnp.bfloat16

ROWS = 384
D = 6144
RANK = 128
CHUNKS = 8
CHUNK = ROWS // CHUNKS
HALF = ROWS // 2
FAR = (2, 1, 3, 0)
PLANE = [(d, e) for d in FAR for e in FAR][:-1]


def mod4(v):
    return lax.rem(v + 4, 4)


def split3(v):
    a = v.astype(BF16).astype(F32)
    b = (v - a).astype(BF16).astype(F32)
    return a, b, (v - a - b).astype(BF16).astype(F32)


def tile_of(part, x, y, z):
    return (z * 16 + x * 4 + y, x * 16 + y * 4 + z, y * 16 + z * 4 + x)[part]


def exchange(
    clip_ref,
    grads,
    errors,
    q_ref,
    new_ref,
    basis_ref,
    qout_ref,
    gbuf,
    ebuf,
    qin,
    qh,
    pacc,
    sq,
    phalf,
    pz,
    pall,
    pt,
    gsend,
    gxr,
    gyr,
    gmat,
    aug,
    wbuf,
    bmat,
    yl,
    yr,
    yc,
    rs1,
    t1,
    rs2,
    gy,
    load_sem,
    qin_sem,
    q1s,
    q1r,
    q2s,
    q2r,
    q3s,
    q3r,
    p1s,
    p1r,
    p2s,
    p2r,
    p3s,
    p3r,
    gxs,
    gxq,
    gys,
    gyq,
    g2s,
    g2r,
    g3s,
    g3r,
    cs,
    cr,
    r1s,
    r1r,
    a2s,
    a2r,
    r2s,
    r2r,
    a1s,
    a1r,
    fs,
    fr,
):
    f = lax.axis_index("fsdp")
    r = lax.axis_index("replica")
    x, y, z, c = f // 4, lax.rem(f, 4), r // 2, lax.rem(r, 2)
    sibling = (f, z * 2 + 1 - c)

    xs = [mod4(x + d) * 4 for d in range(4)]
    ys = [mod4(y + d) for d in range(4)]
    zs = [mod4(z + d) * 2 + c for d in range(4)]

    def at_xy(dx, dy):
        return xs[dx] + ys[dy]

    def at_z(dz):
        return zs[dz]

    def describe(src, dst, ssem, rsem, device):
        return pltpu.make_async_remote_copy(
            src_ref=src, dst_ref=dst, send_sem=ssem, recv_sem=rsem, device_id=device, device_id_type=MESH
        )

    def send(src, dst, ssem, rsem, device):
        copy = describe(src, dst, ssem, rsem, device)
        copy.start()
        return copy

    sent = []

    qload = pltpu.make_async_copy(q_ref.at[pl.ds(pl.multiple_of(c * HALF, HALF), HALF)], qin, qin_sem)
    qload.start()

    barrier = pltpu.get_barrier_semaphore()
    peers = []
    for d in (2, 1, 3):
        peers += [(at_xy(d, 0), r), (at_xy(0, d), r)]
    peers.append(sibling)
    for d in (2, 1, 3):
        peers.append((f, at_z(d)))
    for device in peers:
        pl.semaphore_signal(barrier, inc=1, device_id=device, device_id_type=MESH)

    for k in range(CHUNKS):
        rows = pl.ds(k * CHUNK, CHUNK)
        pltpu.make_async_copy(grads.at[rows], gbuf.at[rows], load_sem.at[0, k]).start()
        pltpu.make_async_copy(errors.at[rows], ebuf.at[rows], load_sem.at[1, k]).start()

    s_me, t_me = jnp.where(c == 0, y, x), jnp.where(c == 0, x, y)
    qload.wait()
    filled = pl.ds(pl.multiple_of(c * 64, 64), HALF)
    for s in range(4):
        for t in range(4):
            qh[0, s, t, HALF:] = jnp.zeros((64, RANK), BF16)
            qh[1, s, t, :64] = jnp.zeros((64, RANK), BF16)
    qh[c, s_me, t_me, filled] = qin[...].astype(BF16)
    sq[...] = jnp.zeros_like(sq)
    pl.semaphore_wait(barrier, len(peers))

    def along_t(d):
        return (jnp.where(c == 0, at_xy(d, 0), at_xy(0, d)), r)

    def along_s(d):
        return (jnp.where(c == 0, at_xy(0, d), at_xy(d, 0)), r)

    own = qh.at[c, s_me, t_me, filled]
    q1 = [send(own, own, q1s.at[d - 1], q1r.at[d - 1], along_t(d)) for d in (1, 2, 3)]
    q2 = [send(own, own, q2s.at[0, d - 1], q2r.at[d - 1], along_s(d)) for d in (1, 2, 3)]
    q3 = [send(own, own, q3s.at[0], q3r.at[0], sibling)]

    def merge(k, _):
        rows = pl.ds(pl.multiple_of(k * CHUNK, CHUNK), CHUNK)
        pltpu.make_async_copy(grads.at[rows], gbuf.at[rows], load_sem.at[0, k]).wait()
        pltpu.make_async_copy(errors.at[rows], ebuf.at[rows], load_sem.at[1, k]).wait()

        def group(i, _):
            rows = pl.ds(pl.multiple_of(k * CHUNK + i * 16, 16), 16)
            total = jnp.zeros((16, 128), F32)
            for j in range(D // 768):
                cols = pl.ds(j * 768, 768)
                m = gbuf[rows, cols].astype(F32) + ebuf[rows, cols].astype(F32)
                gbuf[rows, cols] = m.astype(BF16)
                m2 = m * m
                for i2 in range(6):
                    total = total + m2[:, i2 * 128 : (i2 + 1) * 128]
            sq[...] += total[:8] + total[8:]
            return 0

        lax.fori_loop(0, CHUNK // 16, group, 0)
        return 0

    lax.fori_loop(0, 3, merge, 0)
    for d in (1, 3, 2):
        q1[d - 1].wait_recv()
        here = qh.at[c, s_me, mod4(t_me - d), filled]
        for e in (2, 1, 3):
            q2.append(send(here, here, q2s.at[d, e - 1], q2r.at[e - 1], along_s(e)))
        q3.append(send(here, here, q3s.at[d], q3r.at[d], sibling))
    lax.fori_loop(3, CHUNKS, merge, 0)
    def add_p(half, places, first=False):
        cols, right = [], []
        for s in places:
            right.append(qh[half, s].reshape(1024, RANK))
            for t in range(4):
                g = jnp.where(half == 0, t * 4 + s, s * 4 + t)
                cols.append(gbuf[:, pl.ds(pl.multiple_of(g * ROWS + half * 128, 128), 256)])
        term = jnp.dot(
            jnp.concatenate(cols, axis=1), jnp.concatenate(right, axis=0), preferred_element_type=F32
        )
        if first:
            pacc[...] = term
        else:
            pacc[...] += term

    add_p(c, [s_me], True)
    for copy in q3[:4]:
        copy.wait_recv()
    add_p(1 - c, [t_me])
    for d in (1, 3, 2):
        here = qh.at[c, mod4(s_me - d), :, filled]
        describe(here, here, q2s.at[0, 0], q2r.at[d - 1], sibling).wait_recv()
        q3.append(send(here, here, q3s.at[3 + d], q3r.at[3 + d], sibling))
    add_p(c, [mod4(s_me - d) for d in (1, 3, 2)])
    for copy in q3[4:]:
        copy.wait_recv()
    add_p(1 - c, [mod4(t_me - d) for d in (1, 3, 2)])
    sent += q1 + q2 + q3

    half_c = pl.ds(pl.multiple_of(c * HALF, HALF), HALF)
    other_half = pl.ds(pl.multiple_of((1 - c) * HALF, HALF), HALF)
    p1 = send(pacc.at[other_half], phalf, p1s, p1r, sibling)
    p1.wait_recv()
    pz[z] = (pacc[half_c, :] + phalf[...]).astype(BF16)
    p2 = [send(pz.at[z], pz.at[z], p2s.at[d - 1], p2r.at[d - 1], (f, at_z(d))) for d in (2, 1, 3)]
    for copy in p2:
        copy.wait_recv()
    total = pz[0].astype(F32)
    for k in range(1, 4):
        total = total + pz[k].astype(F32)
    pall[c] = total.astype(BF16)
    p3 = send(pall.at[c], pall.at[c], p3s, p3r, sibling)
    p3.wait_recv()
    sent += [p1, p3] + p2

    p_full = pall[...].reshape(ROWS, RANK)
    pt[...] = p_full.T

    core, s1 = {}, ([], [], [])
    order = ((z, x, y), (x, y, z), (y, z, x))

    def way(part, steps):
        dx, dy, dz = ((steps[1], steps[2], steps[0]), (steps[0], steps[1], steps[2]), (steps[2], steps[0], steps[1]))[
            part
        ]
        return (at_xy(dx, dy), at_z(dz))

    def multiply(part, places):
        cols = [
            gbuf[:, pl.ds(pl.multiple_of((x2 * 4 + y2) * ROWS + part * 128, 128), 128)] for x2, y2 in places
        ]
        block = jnp.dot(pt[...], jnp.concatenate(cols, axis=1), preferred_element_type=F32).astype(BF16)
        for k, (x2, y2) in enumerate(places):
            for c2 in (0, 1):
                for z2 in range(4):
                    at = c2 * 64 + z2 * 16
                    yl[c2, part, tile_of(part, x2, y2, z2)] = block[at : at + 16, k * 128 : (k + 1) * 128]

    def line(part, d):
        return pl.ds(pl.multiple_of(mod4(order[part][0] + d) * 16, 16), 16)

    def swap(part, d):
        at = line(part, d)
        core[part, d] = send(yl.at[1 - c, part, at], yr.at[part, at], cs.at[part, d], cr.at[part, d], sibling)

    def add_core(part, d):
        at = line(part, d)
        core[part, d].wait_recv()
        yc[part, at] = (yl[c, part, at].astype(F32) + yr[part, at].astype(F32)).astype(BF16)
        if d:
            s1[part].append(
                send(
                    yc.at[part, at],
                    rs1.at[part, d - 1],
                    r1s.at[part, d - 1],
                    r1r.at[part, d - 1],
                    way(part, (d, 0, 0)),
                )
            )

    def add_line(part):
        a0, a1, a2 = order[part]
        for copy in s1[part]:
            copy.wait_recv()
        value = yc[part, pl.ds(a0 * 16, 16)].astype(F32)
        for d in range(3):
            value = value + rs1[part, d].astype(F32)
        t1[part] = value.astype(BF16)
        return [
            send(
                t1.at[part, mod4(a1 + d) * 4 + mod4(a2 + e)],
                rs2.at[part, k],
                r2s.at[part],
                r2r.at[part],
                way(part, (0, d, e)),
            )
            for k, (d, e) in enumerate(PLANE)
        ]

    def add_plane(part):
        a0, a1, a2 = order[part]
        describe(rs2.at[part], rs2.at[part], r2s.at[part], r2r.at[part], sibling).wait_recv()
        value = t1[part, a1 * 4 + a2].astype(F32)
        for k in range(15):
            value = value + rs2[part, k].astype(F32)
        mine = a0 * 16 + a1 * 4 + a2
        gy[c, part, mine] = value.astype(BF16)
        here = gy.at[c, part, mine]
        for d, e in PLANE:
            send(here, here, a1s.at[part], a1r.at[part], way(part, (0, d, e)))

    for j in range(4):
        multiply(0, [(j, k) for k in range(4)])
    for d in FAR:
        swap(0, d)

    slot = c * 4 + z
    my_rows = pl.ds(pl.multiple_of(slot * 16, 16), 16)
    gsend[0, :16] = jnp.dot(pt[my_rows, :], p_full, preferred_element_type=F32)
    gsend[0, 16:] = sq[...]
    gx = [
        send(gsend.at[0], gxr.at[k], gxs.at[k], gxq.at[k], (at_xy(dx, dy), r)) for k, (dx, dy) in enumerate(PLANE)
    ]

    for d in FAR:
        multiply(1, [(mod4(x + d), k) for k in range(4)])
        swap(1, d)
        add_core(0, d)
    for d in FAR:
        multiply(2, [(k, mod4(y + d)) for k in range(4)])
        swap(2, d)
        add_core(1, d)
    for d in FAR:
        add_core(2, d)

    add_line(0)
    for copy in gx:
        copy.wait_recv()
    gsum = gsend[0]
    for k in range(15):
        gsum = gsum + gxr[k]
    gmat[slot] = gsum
    g2 = [send(gmat.at[slot], gmat.at[slot], g2s.at[d - 1], g2r.at[d - 1], (f, at_z(d))) for d in (1, 2, 3)]
    add_line(1)
    add_line(2)
    for copy in g2:
        copy.wait_recv()
    side = gmat.at[pl.ds(c * 4, 4)]
    g3 = send(side, side, g3s.at[0], g3r.at[0], sibling)
    for part in range(3):
        add_plane(part)

    g3.wait_recv()
    for k in range(8):
        aug[k * 16 : (k + 1) * 16, :RANK] = gmat[k, :16]
    rows_i = lax.broadcasted_iota(jnp.int32, (RANK, RANK), 0)
    cols_i = lax.broadcasted_iota(jnp.int32, (RANK, RANK), 1)
    aug[:, RANK:] = jnp.where(rows_i == cols_i, 1.0, 0.0).astype(F32)
    sub = lax.broadcasted_iota(jnp.int32, (8, 128), 0)

    def spread_row(v, i):
        return jnp.broadcast_to(v[i : i + 1, :], (8, 128))

    def panel(k, _):
        base = pl.multiple_of(k * 16, 16)
        halves = (pl.ds(base, 8), pl.ds(base + 8, 8))
        rowp = [aug[at, :RANK] for at in halves]
        ext = [aug[at, RANK:] for at in halves]
        turned = [pltpu.roll(v, lax.rem(128 - base, 128), 1) for v in rowp]
        col = [[jnp.broadcast_to(v[:, j : j + 1], (8, 128)) for v in turned] for j in range(16)]
        diag = [jnp.ones((8, 128), F32)] * 2
        for j in range(16):
            top, i = j // 8, j % 8
            pivot = spread_row(col[j][top], i)
            inv = 1.0 / pivot
            low = [None, None]
            for h in range(top, 2):
                low[h] = col[j][h] * inv
            low[top] = jnp.where(sub > i, low[top], 0.0)
            pivots = [spread_row(col[m][top], i) for m in range(j + 1, 16)]
            row_r, row_e = spread_row(rowp[top], i), spread_row(ext[top], i)
            for h in range(top, 2):
                for m in range(j + 1, 16):
                    col[m][h] = col[m][h] - low[h] * pivots[m - j - 1]
                rowp[h] = rowp[h] - low[h] * row_r
                ext[h] = ext[h] - low[h] * row_e
            diag[top] = jnp.where(sub == i, pivot, diag[top])
        for h in (0, 1):
            inv = lax.rsqrt(diag[h])
            inv = inv * (1.5 - 0.5 * diag[h] * inv * inv)
            rowp[h] = rowp[h] * inv
            ext[h] = ext[h] * inv
            wbuf[halves[h], :] = ext[h]
        v1, v2, v3 = split3(jnp.concatenate(rowp, axis=0))
        e1, e2, e3 = split3(jnp.concatenate(ext, axis=0))
        left = jnp.concatenate([v1, v1, v2, v2, v1, v3], axis=0).T.astype(BF16)
        top = jnp.concatenate([v1, v2, v1, v2, v3, v1], axis=0)
        more = jnp.concatenate([e1, e2, e1, e2, e3, e1], axis=0)
        both = jnp.concatenate([top, more], axis=1).astype(BF16)
        aug[...] -= jnp.dot(left, both, preferred_element_type=F32)
        return 0

    lines, passed = [], []

    def spread(part):
        a0 = order[part][0]
        here = gy.at[c, part, pl.ds(a0 * 16, 16)]
        region = rs2.at[part]
        describe(region, region, a1s.at[part], a1r.at[part], sibling).wait_recv()
        lines.append([
            send(here, here, a2s.at[part, d - 1], a2r.at[part, d - 1], way(part, (d, 0, 0))) for d in (1, 2, 3)
        ])
        passed.append([send(here, here, fs.at[part, 0], fr.at[part, 0], sibling)])

    lax.fori_loop(0, 3, panel, 0)
    spread(0)
    lax.fori_loop(3, 4, panel, 0)
    spread(1)
    lax.fori_loop(4, 5, panel, 0)
    spread(2)
    for group_of in s1:
        sent += group_of
    for copy in sent + gx + g2 + [g3] + list(core.values()):
        copy.wait_send()
    for part in range(3):
        region = rs2.at[part]
        for sems in (r2s, a1s):
            describe(region, region, sems.at[part], r2r.at[part], sibling).wait_send()

    lax.fori_loop(5, 8, panel, 0)

    w = wbuf[...]
    pb = jnp.zeros((ROWS, RANK), F32)
    p_again = pall[...].reshape(ROWS, RANK)
    for piece in split3(w)[::-1]:
        pb = pb + lax.dot_general(
            p_again, piece.astype(BF16), (((1,), (1,)), ((), ())), preferred_element_type=F32
        )
    basis_ref[...] = pb
    bmat[...] = (
        jnp.dot(pb, w, preferred_element_type=F32, precision=lax.Precision.HIGHEST) * 0.125
    ).astype(BF16)

    def right(part, x2, y2):
        tiles = [gy[c2, part, tile_of(part, x2, y2, z2)] for c2 in (0, 1) for z2 in range(4)]
        return jnp.concatenate(tiles, axis=0)

    def update(part, places):
        low = jnp.dot(
            bmat[...],
            jnp.concatenate([right(part, x2, y2) for x2, y2 in places], axis=1),
            preferred_element_type=F32,
        )
        for k, (x2, y2) in enumerate(places):
            cols = pl.ds(pl.multiple_of((x2 * 4 + y2) * ROWS + part * 128, 128), 128)
            new_ref[:, cols] = (gbuf[:, cols].astype(F32) - low[:, k * 128 : (k + 1) * 128]).astype(BF16)

    def pass_line(d):
        for part in range(3):
            lines[part][d - 1].wait_recv()
            here = gy.at[c, part, pl.ds(mod4(order[part][0] - d) * 16, 16)]
            passed[part].append(send(here, here, fs.at[part, d], fr.at[part, d], sibling))

    def groups(d):
        for part in range(3):
            passed[part][(0, 1, 3, 2)[d]].wait_recv()
            a0 = mod4(order[part][0] - d)
            if part == 1:
                update(part, [(a0, k) for k in range(4)])
            if part == 2:
                update(part, [(k, a0) for k in range(4)])

    groups(0)
    pass_line(1)
    pass_line(3)
    groups(1)
    pass_line(2)
    groups(3)
    groups(2)
    for j in range(4):
        update(0, [(j, k) for k in range(4)])

    squares = jnp.sum(jnp.sum(gmat[:, 16:], axis=0))
    root_mean = jnp.sqrt(jnp.full((1, RANK), squares) / (8 * D * D) + 1e-06)
    scale = jnp.minimum(1.0, clip_ref[0, 0] / root_mean) * 0.125
    block = jnp.concatenate([right(part, x, y) for part in range(3)], axis=1)
    value = jnp.zeros((RANK, ROWS), F32)
    for piece in split3(wbuf[...])[::-1]:
        value = value + jnp.dot(piece.astype(BF16), block, preferred_element_type=F32)
    qout_ref[...] = value.T * scale

    for group_of in lines + passed:
        for copy in group_of:
            copy.wait_send()


def hand_over(new_ref, basis_ref, q_ref, new_out, basis_out, q_out, sems):
    copies = [
        pltpu.make_async_copy(basis_ref, basis_out, sems.at[CHUNKS]),
        pltpu.make_async_copy(q_ref, q_out, sems.at[CHUNKS + 1]),
    ]
    for k in range(CHUNKS):
        rows = pl.ds(k * CHUNK, CHUNK)
        copies.append(pltpu.make_async_copy(new_ref.at[rows], new_out.at[rows], sems.at[k]))
    for copy in copies:
        copy.start()
    for copy in copies:
        copy.wait()


def body(grads, errors, q_start, clip_rms):
    dma = pltpu.SemaphoreType.DMA
    vmem = pltpu.VMEM
    hbm = pl.BlockSpec(memory_space=pltpu.HBM)
    inside = pl.BlockSpec(memory_space=pltpu.VMEM)
    new_errors, basis, q_out = pl.pallas_call(
        exchange,
        out_shape=(
            vmem((ROWS, D), BF16),
            vmem((ROWS, RANK), F32),
            vmem((ROWS, RANK), F32),
        ),
        in_specs=[pl.BlockSpec(memory_space=pltpu.SMEM), hbm, hbm, hbm],
        out_specs=(inside, inside, inside),
        scratch_shapes=[
            vmem((ROWS, D), BF16),
            vmem((ROWS, D), BF16),
            vmem((HALF, RANK), F32),
            vmem((2, 4, 4, 256, RANK), BF16),
            vmem((ROWS, RANK), F32),
            vmem((8, 128), F32),
            vmem((HALF, RANK), F32),
            vmem((4, HALF, RANK), BF16),
            vmem((2, HALF, RANK), BF16),
            vmem((RANK, ROWS), BF16),
            vmem((2, 24, RANK), F32),
            vmem((15, 24, RANK), F32),
            vmem((3, 24, RANK), F32),
            vmem((8, 24, RANK), F32),
            vmem((RANK, 2 * RANK), F32),
            vmem((RANK, RANK), F32),
            vmem((ROWS, RANK), BF16),
            vmem((2, 3, 64, 16, 128), BF16),
            vmem((3, 64, 16, 128), BF16),
            vmem((3, 64, 16, 128), BF16),
            vmem((3, 3, 16, 16, 128), BF16),
            vmem((3, 16, 16, 128), BF16),
            vmem((3, 15, 16, 128), BF16),
            vmem((2, 3, 64, 16, 128), BF16),
            dma((2, CHUNKS)),
            dma(()),
            dma((3,)),
            dma((3,)),
            dma((4, 3)),
            dma((3,)),
            dma((7,)),
            dma((7,)),
            dma(()),
            dma(()),
            dma((3,)),
            dma((3,)),
            dma(()),
            dma(()),
            dma((15,)),
            dma((15,)),
            dma((3,)),
            dma((3,)),
            dma((3,)),
            dma((3,)),
            dma((1,)),
            dma((1,)),
            dma((3, 4)),
            dma((3, 4)),
            dma((3, 3)),
            dma((3, 3)),
            dma((3, 3)),
            dma((3, 3)),
            dma((3,)),
            dma((3,)),
            dma((3,)),
            dma((3,)),
            dma((3, 4)),
            dma((3, 4)),
        ],
        compiler_params=pltpu.CompilerParams(
            collective_id=0, has_side_effects=True, vmem_limit_bytes=40 * 1024 * 1024
        ),
        name="exchange",
    )(clip_rms.reshape(1, 1), *[pltpu.with_memory_space_constraint(v, pltpu.HBM) for v in (grads[0], errors[0], q_start)])
    anywhere = pl.BlockSpec(memory_space=pl.ANY)
    new_errors, basis, q_out = pl.pallas_call(
        hand_over,
        out_shape=(
            jax.ShapeDtypeStruct((ROWS, D), BF16),
            jax.ShapeDtypeStruct((ROWS, RANK), F32),
            jax.ShapeDtypeStruct((ROWS, RANK), F32),
        ),
        in_specs=[anywhere] * 3,
        out_specs=(anywhere,) * 3,
        scratch_shapes=[dma((CHUNKS + 2,))],
        compiler_params=pltpu.CompilerParams(vmem_limit_bytes=1024 * 1024),
        name="hand_over",
    )(new_errors, basis, q_out)
    return new_errors[None], basis, q_out


def solution(mesh):
    return jax.shard_map(
        body,
        mesh=mesh,
        in_specs=(P("replica", "fsdp", None), P("replica", "fsdp", None), P("fsdp", None), P()),
        out_specs=(P("replica", "fsdp", None), P("fsdp", None), P("fsdp", None)),
        check_vma=False,
    )
```

```python
import jax
import jax.numpy as jnp
from jax import lax
from jax.experimental import pallas as pl
from jax.experimental.pallas import tpu as pltpu
from jax.sharding import PartitionSpec as P

MESH = pl.DeviceIdType.MESH
F32 = jnp.float32
BF16 = jnp.bfloat16

ROWS = 384
D = 6144
RANK = 128
CHUNKS = 8
CHUNK = ROWS // CHUNKS
HALF = ROWS // 2
FAR = (2, 1, 3, 0)
PLANE = [(d, e) for d in FAR for e in FAR][:-1]


def mod4(v):
    return lax.rem(v + 4, 4)


def split3(v):
    a = v.astype(BF16).astype(F32)
    b = (v - a).astype(BF16).astype(F32)
    return a, b, (v - a - b).astype(BF16).astype(F32)


def tile_of(part, x, y, z):
    return (z * 16 + x * 4 + y, x * 16 + y * 4 + z, y * 16 + z * 4 + x)[part]


def exchange(
    clip_ref,
    grads,
    errors,
    q_ref,
    gbuf,
    gy,
    bmat,
    basis_ref,
    w_ref,
    ebuf,
    qin,
    qh,
    pacc,
    sq,
    phalf,
    pz,
    pall,
    pt,
    gsend,
    gxr,
    gyr,
    gmat,
    aug,
    wbuf,
    yl,
    yr,
    yc,
    rs1,
    t1,
    rs2,
    load_sem,
    qin_sem,
    q1s,
    q1r,
    q2s,
    q2r,
    q3s,
    q3r,
    p1s,
    p1r,
    p2s,
    p2r,
    p3s,
    p3r,
    gxs,
    gxq,
    gys,
    gyq,
    g2s,
    g2r,
    g3s,
    g3r,
    cs,
    cr,
    r1s,
    r1r,
    a2s,
    a2r,
    r2s,
    r2r,
    a1s,
    a1r,
    fs,
    fr,
):
    f = lax.axis_index("fsdp")
    r = lax.axis_index("replica")
    x, y, z, c = f // 4, lax.rem(f, 4), r // 2, lax.rem(r, 2)
    sibling = (f, z * 2 + 1 - c)

    xs = [mod4(x + d) * 4 for d in range(4)]
    ys = [mod4(y + d) for d in range(4)]
    zs = [mod4(z + d) * 2 + c for d in range(4)]

    def at_xy(dx, dy):
        return xs[dx] + ys[dy]

    def at_z(dz):
        return zs[dz]

    def describe(src, dst, ssem, rsem, device):
        return pltpu.make_async_remote_copy(
            src_ref=src, dst_ref=dst, send_sem=ssem, recv_sem=rsem, device_id=device, device_id_type=MESH
        )

    def send(src, dst, ssem, rsem, device):
        copy = describe(src, dst, ssem, rsem, device)
        copy.start()
        return copy

    sent = []

    qload = pltpu.make_async_copy(q_ref.at[pl.ds(pl.multiple_of(c * HALF, HALF), HALF)], qin, qin_sem)
    qload.start()

    barrier = pltpu.get_barrier_semaphore()
    peers = []
    for d in (2, 1, 3):
        peers += [(at_xy(d, 0), r), (at_xy(0, d), r)]
    peers.append(sibling)
    for d in (2, 1, 3):
        peers.append((f, at_z(d)))
    for device in peers:
        pl.semaphore_signal(barrier, inc=1, device_id=device, device_id_type=MESH)

    for k in range(CHUNKS):
        rows = pl.ds(k * CHUNK, CHUNK)
        pltpu.make_async_copy(grads.at[rows], gbuf.at[rows], load_sem.at[0, k]).start()
        pltpu.make_async_copy(errors.at[rows], ebuf.at[rows], load_sem.at[1, k]).start()

    s_me, t_me = jnp.where(c == 0, y, x), jnp.where(c == 0, x, y)
    qload.wait()
    filled = pl.ds(pl.multiple_of(c * 64, 64), HALF)
    for s in range(4):
        for t in range(4):
            qh[0, s, t, HALF:] = jnp.zeros((64, RANK), BF16)
            qh[1, s, t, :64] = jnp.zeros((64, RANK), BF16)
    qh[c, s_me, t_me, filled] = qin[...].astype(BF16)
    sq[...] = jnp.zeros_like(sq)
    pl.semaphore_wait(barrier, len(peers))

    def along_t(d):
        return (jnp.where(c == 0, at_xy(d, 0), at_xy(0, d)), r)

    def along_s(d):
        return (jnp.where(c == 0, at_xy(0, d), at_xy(d, 0)), r)

    own = qh.at[c, s_me, t_me, filled]
    q1 = [send(own, own, q1s.at[d - 1], q1r.at[d - 1], along_t(d)) for d in (1, 2, 3)]
    q2 = [send(own, own, q2s.at[0, d - 1], q2r.at[d - 1], along_s(d)) for d in (1, 2, 3)]
    q3 = [send(own, own, q3s.at[0], q3r.at[0], sibling)]

    def merge(k, _):
        rows = pl.ds(pl.multiple_of(k * CHUNK, CHUNK), CHUNK)
        pltpu.make_async_copy(grads.at[rows], gbuf.at[rows], load_sem.at[0, k]).wait()
        pltpu.make_async_copy(errors.at[rows], ebuf.at[rows], load_sem.at[1, k]).wait()

        def group(i, _):
            rows = pl.ds(pl.multiple_of(k * CHUNK + i * 16, 16), 16)
            total = jnp.zeros((16, 128), F32)
            for j in range(D // 768):
                cols = pl.ds(j * 768, 768)
                m = gbuf[rows, cols].astype(F32) + ebuf[rows, cols].astype(F32)
                gbuf[rows, cols] = m.astype(BF16)
                m2 = m * m
                for i2 in range(6):
                    total = total + m2[:, i2 * 128 : (i2 + 1) * 128]
            sq[...] += total[:8] + total[8:]
            return 0

        lax.fori_loop(0, CHUNK // 16, group, 0)
        return 0

    lax.fori_loop(0, 3, merge, 0)
    for d in (1, 3, 2):
        q1[d - 1].wait_recv()
        here = qh.at[c, s_me, mod4(t_me - d), filled]
        for e in (2, 1, 3):
            q2.append(send(here, here, q2s.at[d, e - 1], q2r.at[e - 1], along_s(e)))
        q3.append(send(here, here, q3s.at[d], q3r.at[d], sibling))
    lax.fori_loop(3, CHUNKS, merge, 0)
    def add_p(half, places, first=False):
        cols, right = [], []
        for s in places:
            right.append(qh[half, s].reshape(1024, RANK))
            for t in range(4):
                g = jnp.where(half == 0, t * 4 + s, s * 4 + t)
                cols.append(gbuf[:, pl.ds(pl.multiple_of(g * ROWS + half * 128, 128), 256)])
        term = jnp.dot(
            jnp.concatenate(cols, axis=1), jnp.concatenate(right, axis=0), preferred_element_type=F32
        )
        if first:
            pacc[...] = term
        else:
            pacc[...] += term

    add_p(c, [s_me], True)
    for copy in q3[:4]:
        copy.wait_recv()
    add_p(1 - c, [t_me])
    for d in (1, 3, 2):
        here = qh.at[c, mod4(s_me - d), :, filled]
        describe(here, here, q2s.at[0, 0], q2r.at[d - 1], sibling).wait_recv()
        q3.append(send(here, here, q3s.at[3 + d], q3r.at[3 + d], sibling))
    add_p(c, [mod4(s_me - d) for d in (1, 3, 2)])
    for copy in q3[4:]:
        copy.wait_recv()
    add_p(1 - c, [mod4(t_me - d) for d in (1, 3, 2)])
    sent += q1 + q2 + q3

    half_c = pl.ds(pl.multiple_of(c * HALF, HALF), HALF)
    other_half = pl.ds(pl.multiple_of((1 - c) * HALF, HALF), HALF)
    p1 = send(pacc.at[other_half], phalf, p1s, p1r, sibling)
    p1.wait_recv()
    pz[z] = (pacc[half_c, :] + phalf[...]).astype(BF16)
    p2 = [send(pz.at[z], pz.at[z], p2s.at[d - 1], p2r.at[d - 1], (f, at_z(d))) for d in (2, 1, 3)]
    for copy in p2:
        copy.wait_recv()
    total = pz[0].astype(F32)
    for k in range(1, 4):
        total = total + pz[k].astype(F32)
    pall[c] = total.astype(BF16)
    p3 = send(pall.at[c], pall.at[c], p3s, p3r, sibling)
    p3.wait_recv()
    sent += [p1, p3] + p2

    p_full = pall[...].reshape(ROWS, RANK)
    pt[...] = p_full.T

    core, s1 = {}, ([], [], [])
    order = ((z, x, y), (x, y, z), (y, z, x))

    def way(part, steps):
        dx, dy, dz = ((steps[1], steps[2], steps[0]), (steps[0], steps[1], steps[2]), (steps[2], steps[0], steps[1]))[
            part
        ]
        return (at_xy(dx, dy), at_z(dz))

    def multiply(part, places):
        cols = [
            gbuf[:, pl.ds(pl.multiple_of((x2 * 4 + y2) * ROWS + part * 128, 128), 128)] for x2, y2 in places
        ]
        block = jnp.dot(pt[...], jnp.concatenate(cols, axis=1), preferred_element_type=F32).astype(BF16)
        for k, (x2, y2) in enumerate(places):
            for c2 in (0, 1):
                for z2 in range(4):
                    at = c2 * 64 + z2 * 16
                    yl[c2, part, tile_of(part, x2, y2, z2)] = block[at : at + 16, k * 128 : (k + 1) * 128]

    def line(part, d):
        return pl.ds(pl.multiple_of(mod4(order[part][0] + d) * 16, 16), 16)

    def swap(part, d):
        at = line(part, d)
        core[part, d] = send(yl.at[1 - c, part, at], yr.at[part, at], cs.at[part, d], cr.at[part, d], sibling)

    def add_core(part, d):
        at = line(part, d)
        core[part, d].wait_recv()
        yc[part, at] = (yl[c, part, at].astype(F32) + yr[part, at].astype(F32)).astype(BF16)
        if d:
            s1[part].append(
                send(
                    yc.at[part, at],
                    rs1.at[part, d - 1],
                    r1s.at[part, d - 1],
                    r1r.at[part, d - 1],
                    way(part, (d, 0, 0)),
                )
            )

    def add_line(part):
        a0, a1, a2 = order[part]
        for copy in s1[part]:
            copy.wait_recv()
        value = yc[part, pl.ds(a0 * 16, 16)].astype(F32)
        for d in range(3):
            value = value + rs1[part, d].astype(F32)
        t1[part] = value.astype(BF16)
        return [
            send(
                t1.at[part, mod4(a1 + d) * 4 + mod4(a2 + e)],
                rs2.at[part, k],
                r2s.at[part],
                r2r.at[part],
                way(part, (0, d, e)),
            )
            for k, (d, e) in enumerate(PLANE)
        ]

    def add_plane(part):
        a0, a1, a2 = order[part]
        describe(rs2.at[part], rs2.at[part], r2s.at[part], r2r.at[part], sibling).wait_recv()
        value = t1[part, a1 * 4 + a2].astype(F32)
        for k in range(15):
            value = value + rs2[part, k].astype(F32)
        mine = a0 * 16 + a1 * 4 + a2
        gy[c, part, mine] = value.astype(BF16)
        here = gy.at[c, part, mine]
        for d, e in PLANE:
            send(here, here, a1s.at[part], a1r.at[part, d], way(part, (0, d, e)))

    for j in range(4):
        multiply(0, [(j, k) for k in range(4)])
    for d in FAR:
        swap(0, d)

    slot = c * 4 + z
    my_rows = pl.ds(pl.multiple_of(slot * 16, 16), 16)
    gsend[0, :16] = jnp.dot(pt[my_rows, :], p_full, preferred_element_type=F32)
    gsend[0, 16:] = sq[...]
    gx = [
        send(gsend.at[0], gxr.at[k], gxs.at[k], gxq.at[k], (at_xy(dx, dy), r)) for k, (dx, dy) in enumerate(PLANE)
    ]

    for d in FAR:
        multiply(1, [(mod4(x + d), k) for k in range(4)])
        swap(1, d)
        add_core(0, d)
    for d in FAR:
        multiply(2, [(k, mod4(y + d)) for k in range(4)])
        swap(2, d)
        add_core(1, d)
    for d in FAR:
        add_core(2, d)

    add_line(0)
    for copy in gx:
        copy.wait_recv()
    gsum = gsend[0]
    for k in range(15):
        gsum = gsum + gxr[k]
    gmat[slot] = gsum
    g2 = [send(gmat.at[slot], gmat.at[slot], g2s.at[d - 1], g2r.at[d - 1], (f, at_z(d))) for d in (1, 2, 3)]
    add_line(1)
    add_line(2)
    for copy in g2:
        copy.wait_recv()
    side = gmat.at[pl.ds(c * 4, 4)]
    g3 = send(side, side, g3s.at[0], g3r.at[0], sibling)
    for part in range(3):
        add_plane(part)

    g3.wait_recv()
    for k in range(8):
        aug[k * 16 : (k + 1) * 16, :RANK] = gmat[k, :16]
    rows_i = lax.broadcasted_iota(jnp.int32, (RANK, RANK), 0)
    cols_i = lax.broadcasted_iota(jnp.int32, (RANK, RANK), 1)
    aug[:, RANK:] = jnp.where(rows_i == cols_i, 1.0, 0.0).astype(F32)
    sub = lax.broadcasted_iota(jnp.int32, (8, 128), 0)

    def spread_row(v, i):
        return jnp.broadcast_to(v[i : i + 1, :], (8, 128))

    def panel(k, _):
        base = pl.multiple_of(k * 16, 16)
        halves = (pl.ds(base, 8), pl.ds(base + 8, 8))
        rowp = [aug[at, :RANK] for at in halves]
        ext = [aug[at, RANK:] for at in halves]
        turned = [pltpu.roll(v, lax.rem(128 - base, 128), 1) for v in rowp]
        col = [[jnp.broadcast_to(v[:, j : j + 1], (8, 128)) for v in turned] for j in range(16)]
        diag = [jnp.ones((8, 128), F32)] * 2
        for j in range(16):
            top, i = j // 8, j % 8
            pivot = spread_row(col[j][top], i)
            inv = 1.0 / pivot
            low = [None, None]
            for h in range(top, 2):
                low[h] = col[j][h] * inv
            low[top] = jnp.where(sub > i, low[top], 0.0)
            pivots = [spread_row(col[m][top], i) for m in range(j + 1, 16)]
            row_r, row_e = spread_row(rowp[top], i), spread_row(ext[top], i)
            for h in range(top, 2):
                for m in range(j + 1, 16):
                    col[m][h] = col[m][h] - low[h] * pivots[m - j - 1]
                rowp[h] = rowp[h] - low[h] * row_r
                ext[h] = ext[h] - low[h] * row_e
            diag[top] = jnp.where(sub == i, pivot, diag[top])
        for h in (0, 1):
            inv = lax.rsqrt(diag[h])
            inv = inv * (1.5 - 0.5 * diag[h] * inv * inv)
            rowp[h] = rowp[h] * inv
            ext[h] = ext[h] * inv
            wbuf[halves[h], :] = ext[h]
        v1, v2, v3 = split3(jnp.concatenate(rowp, axis=0))
        e1, e2, e3 = split3(jnp.concatenate(ext, axis=0))
        left = jnp.concatenate([v1, v1, v2, v2, v1, v3], axis=0).T.astype(BF16)
        top = jnp.concatenate([v1, v2, v1, v2, v3, v1], axis=0)
        more = jnp.concatenate([e1, e2, e1, e2, e3, e1], axis=0)
        both = jnp.concatenate([top, more], axis=1).astype(BF16)
        aug[...] -= jnp.dot(left, both, preferred_element_type=F32)
        return 0

    lines, passed = [], []

    def spread(part):
        a0, a1, _ = order[part]
        for d in FAR:
            region = rs2.at[part, pl.ds(0, 4 if d else 3)]
            describe(region, region, a1s.at[part], a1r.at[part, d], sibling).wait_recv()
            here = gy.at[c, part, pl.ds(a0 * 16 + mod4(a1 - d) * 4, 4)]
            for e in (2, 1, 3):
                send(here, here, a2s.at[part, e - 1], a2r.at[part, e - 1], way(part, (e, 0, 0)))
            send(here, here, fs.at[part, 0], fr.at[part, 0], sibling)
        here = gy.at[c, part, pl.ds(a0 * 16, 16)]
        lines.append([describe(here, here, a2s.at[part, e], a2r.at[part, e], sibling) for e in range(3)])
        passed.append([describe(here, here, fs.at[part, 0], fr.at[part, 0], sibling)])

    lax.fori_loop(0, 3, panel, 0)
    spread(0)
    lax.fori_loop(3, 4, panel, 0)
    spread(1)
    lax.fori_loop(4, 5, panel, 0)
    spread(2)
    for group_of in s1:
        sent += group_of
    for copy in sent + gx + g2 + [g3] + list(core.values()):
        copy.wait_send()
    for part in range(3):
        region = rs2.at[part]
        for sems in (r2s, a1s):
            describe(region, region, sems.at[part], r2r.at[part], sibling).wait_send()

    lax.fori_loop(5, 8, panel, 0)

    w = wbuf[...]
    pb = jnp.zeros((ROWS, RANK), F32)
    p_again = pall[...].reshape(ROWS, RANK)
    for piece in split3(w)[::-1]:
        pb = pb + lax.dot_general(
            p_again, piece.astype(BF16), (((1,), (1,)), ((), ())), preferred_element_type=F32
        )
    basis_ref[...] = pb
    bmat[...] = (
        jnp.dot(pb, w, preferred_element_type=F32, precision=lax.Precision.HIGHEST) * 0.125
    ).astype(BF16)

    squares = jnp.sum(jnp.sum(gmat[:, 16:], axis=0))
    root_mean = jnp.sqrt(jnp.full((1, RANK), squares) / (8 * D * D) + 1e-06)
    w_ref[...] = wbuf[...] * (jnp.minimum(1.0, clip_ref[0, 0] / root_mean) * 0.125)

    for d in (1, 3, 2):
        for part in range(3):
            lines[part][d - 1].wait_recv()
            here = gy.at[c, part, pl.ds(mod4(order[part][0] - d) * 16, 16)]
            passed[part].append(send(here, here, fs.at[part, d], fr.at[part, d], sibling))
    for group_of in passed:
        for copy in group_of:
            copy.wait_recv()
    for group_of in lines + passed:
        for copy in group_of:
            copy.wait_send()


def update(merged, gy, bmat, basis, w_ref, new_out, basis_out, q_out, new, q_buf, sems):
    f = lax.axis_index("fsdp")
    x, y = f // 4, lax.rem(f, 4)

    def right(part, x2, y2):
        tiles = [gy[c2, part, tile_of(part, x2, y2, z2)] for c2 in (0, 1) for z2 in range(4)]
        return jnp.concatenate(tiles, axis=0)

    copies = [pltpu.make_async_copy(basis, basis_out, sems.at[CHUNKS])]
    copies[0].start()
    for j in range(CHUNKS):
        cols = pl.ds(j * 768, 768)
        places = [((2 * j + k) // 4, (2 * j + k) % 4) for k in (0, 1)]
        block = jnp.concatenate([right(part, x2, y2) for x2, y2 in places for part in range(3)], axis=1)
        low = jnp.dot(bmat[...], block, preferred_element_type=F32)
        new[:, cols] = (merged[:, cols].astype(F32) - low).astype(BF16)
        copies.append(pltpu.make_async_copy(new.at[:, cols], new_out.at[:, cols], sems.at[j]))
        copies[-1].start()
    block = jnp.concatenate([right(part, x, y) for part in range(3)], axis=1)
    value = jnp.zeros((RANK, ROWS), F32)
    for piece in split3(w_ref[...])[::-1]:
        value = value + jnp.dot(piece.astype(BF16), block, preferred_element_type=F32)
    q_buf[...] = value.T
    copies.append(pltpu.make_async_copy(q_buf, q_out, sems.at[CHUNKS + 1]))
    copies[-1].start()
    for copy in copies:
        copy.wait()


def body(grads, errors, q_start, clip_rms):
    dma = pltpu.SemaphoreType.DMA
    vmem = pltpu.VMEM
    hbm = pl.BlockSpec(memory_space=pltpu.HBM)
    inside = pl.BlockSpec(memory_space=pltpu.VMEM)
    merged, gy, bmat, basis, w = pl.pallas_call(
        exchange,
        out_shape=(
            vmem((ROWS, D), BF16),
            vmem((2, 3, 64, 16, 128), BF16),
            vmem((ROWS, RANK), BF16),
            vmem((ROWS, RANK), F32),
            vmem((RANK, RANK), F32),
        ),
        in_specs=[pl.BlockSpec(memory_space=pltpu.SMEM), hbm, hbm, hbm],
        out_specs=(inside,) * 5,
        scratch_shapes=[
            vmem((ROWS, D), BF16),
            vmem((HALF, RANK), F32),
            vmem((2, 4, 4, 256, RANK), BF16),
            vmem((ROWS, RANK), F32),
            vmem((8, 128), F32),
            vmem((HALF, RANK), F32),
            vmem((4, HALF, RANK), BF16),
            vmem((2, HALF, RANK), BF16),
            vmem((RANK, ROWS), BF16),
            vmem((2, 24, RANK), F32),
            vmem((15, 24, RANK), F32),
            vmem((3, 24, RANK), F32),
            vmem((8, 24, RANK), F32),
            vmem((RANK, 2 * RANK), F32),
            vmem((RANK, RANK), F32),
            vmem((2, 3, 64, 16, 128), BF16),
            vmem((3, 64, 16, 128), BF16),
            vmem((3, 64, 16, 128), BF16),
            vmem((3, 3, 16, 16, 128), BF16),
            vmem((3, 16, 16, 128), BF16),
            vmem((3, 15, 16, 128), BF16),
            dma((2, CHUNKS)),
            dma(()),
            dma((3,)),
            dma((3,)),
            dma((4, 3)),
            dma((3,)),
            dma((7,)),
            dma((7,)),
            dma(()),
            dma(()),
            dma((3,)),
            dma((3,)),
            dma(()),
            dma(()),
            dma((15,)),
            dma((15,)),
            dma((3,)),
            dma((3,)),
            dma((3,)),
            dma((3,)),
            dma((1,)),
            dma((1,)),
            dma((3, 4)),
            dma((3, 4)),
            dma((3, 3)),
            dma((3, 3)),
            dma((3, 3)),
            dma((3, 3)),
            dma((3,)),
            dma((3,)),
            dma((3,)),
            dma((3, 4)),
            dma((3, 4)),
            dma((3, 4)),
        ],
        compiler_params=pltpu.CompilerParams(
            collective_id=0, has_side_effects=True, vmem_limit_bytes=40 * 1024 * 1024
        ),
        name="exchange",
    )(clip_rms.reshape(1, 1), *[pltpu.with_memory_space_constraint(v, pltpu.HBM) for v in (grads[0], errors[0], q_start)])
    new_errors, basis, q_out = pl.pallas_call(
        update,
        out_shape=(
            jax.ShapeDtypeStruct((ROWS, D), BF16),
            jax.ShapeDtypeStruct((ROWS, RANK), F32),
            jax.ShapeDtypeStruct((ROWS, RANK), F32),
        ),
        in_specs=[inside] * 5,
        out_specs=(pl.BlockSpec(memory_space=pl.ANY),) * 3,
        scratch_shapes=[vmem((ROWS, D), BF16), vmem((ROWS, RANK), F32), dma((CHUNKS + 2,))],
        compiler_params=pltpu.CompilerParams(vmem_limit_bytes=24 * 1024 * 1024),
        name="update",
    )(*[pltpu.with_memory_space_constraint(v, pltpu.VMEM) for v in (merged, gy, bmat, basis, w)])
    return new_errors[None], basis, q_out


def solution(mesh):
    return jax.shard_map(
        body,
        mesh=mesh,
        in_specs=(P("replica", "fsdp", None), P("replica", "fsdp", None), P("fsdp", None), P()),
        out_specs=(P("replica", "fsdp", None), P("fsdp", None), P("fsdp", None)),
        check_vma=False,
    )
```

```python
import jax
import jax.numpy as jnp
from jax import lax
from jax.experimental import pallas as pl
from jax.experimental.pallas import tpu as pltpu
from jax.sharding import PartitionSpec as P

MESH = pl.DeviceIdType.MESH
F32 = jnp.float32
BF16 = jnp.bfloat16

ROWS = 384
D = 6144
RANK = 128
CHUNKS = 8
CHUNK = ROWS // CHUNKS
HALF = ROWS // 2
FAR = (2, 1, 3, 0)
PLANE = [(d, e) for d in FAR for e in FAR][:-1]


def mod4(v):
    return lax.rem(v + 4, 4)


def split3(v):
    a = v.astype(BF16).astype(F32)
    b = (v - a).astype(BF16).astype(F32)
    return a, b, (v - a - b).astype(BF16).astype(F32)


def tile_of(part, x, y, z):
    return (z * 16 + x * 4 + y, x * 16 + y * 4 + z, y * 16 + z * 4 + x)[part]


def exchange(
    clip_ref,
    grads,
    errors,
    q_ref,
    gbuf,
    gy,
    bmat,
    basis_ref,
    w_ref,
    ebuf,
    qin,
    qh,
    pacc,
    sq,
    phalf,
    pz,
    pall,
    pt,
    gsend,
    gxr,
    gyr,
    gmat,
    aug,
    wbuf,
    yl,
    yr,
    yc,
    rs1,
    t1,
    rs2,
    load_sem,
    qin_sem,
    q1s,
    q1r,
    q2s,
    q2r,
    q3s,
    q3r,
    p1s,
    p1r,
    p2s,
    p2r,
    p3s,
    p3r,
    gxs,
    gxq,
    gys,
    gyq,
    g2s,
    g2r,
    g3s,
    g3r,
    cs,
    cr,
    r1s,
    r1r,
    a2s,
    a2r,
    r2s,
    r2r,
    a1s,
    a1r,
    fs,
    fr,
):
    f = lax.axis_index("fsdp")
    r = lax.axis_index("replica")
    x, y, z, c = f // 4, lax.rem(f, 4), r // 2, lax.rem(r, 2)
    sibling = (f, z * 2 + 1 - c)

    xs = [mod4(x + d) * 4 for d in range(4)]
    ys = [mod4(y + d) for d in range(4)]
    zs = [mod4(z + d) * 2 + c for d in range(4)]

    def at_xy(dx, dy):
        return xs[dx] + ys[dy]

    def at_z(dz):
        return zs[dz]

    def describe(src, dst, ssem, rsem, device):
        return pltpu.make_async_remote_copy(
            src_ref=src, dst_ref=dst, send_sem=ssem, recv_sem=rsem, device_id=device, device_id_type=MESH
        )

    def send(src, dst, ssem, rsem, device):
        copy = describe(src, dst, ssem, rsem, device)
        copy.start()
        return copy

    sent = []

    qload = pltpu.make_async_copy(q_ref.at[pl.ds(pl.multiple_of(c * HALF, HALF), HALF)], qin, qin_sem)
    qload.start()

    barrier = pltpu.get_barrier_semaphore()
    peers = []
    for d in (2, 1, 3):
        peers += [(at_xy(d, 0), r), (at_xy(0, d), r)]
    peers.append(sibling)
    for d in (2, 1, 3):
        peers.append((f, at_z(d)))
    for device in peers:
        pl.semaphore_signal(barrier, inc=1, device_id=device, device_id_type=MESH)

    for k in range(CHUNKS):
        rows = pl.ds(k * CHUNK, CHUNK)
        pltpu.make_async_copy(grads.at[rows], gbuf.at[rows], load_sem.at[0, k]).start()
        pltpu.make_async_copy(errors.at[rows], ebuf.at[rows], load_sem.at[1, k]).start()

    s_me, t_me = jnp.where(c == 0, y, x), jnp.where(c == 0, x, y)
    qload.wait()
    filled = pl.ds(pl.multiple_of(c * 64, 64), HALF)
    for s in range(4):
        for t in range(4):
            qh[0, s, t, HALF:] = jnp.zeros((64, RANK), BF16)
            qh[1, s, t, :64] = jnp.zeros((64, RANK), BF16)
    qh[c, s_me, t_me, filled] = qin[...].astype(BF16)
    sq[...] = jnp.zeros_like(sq)
    pl.semaphore_wait(barrier, len(peers))

    def along_t(d):
        return (jnp.where(c == 0, at_xy(d, 0), at_xy(0, d)), r)

    def along_s(d):
        return (jnp.where(c == 0, at_xy(0, d), at_xy(d, 0)), r)

    own = qh.at[c, s_me, t_me, filled]
    q1 = [send(own, own, q1s.at[d - 1], q1r.at[d - 1], along_t(d)) for d in (1, 2, 3)]
    q2 = [send(own, own, q2s.at[0, d - 1], q2r.at[d - 1], along_s(d)) for d in (1, 2, 3)]
    q3 = [send(own, own, q3s.at[0], q3r.at[0], sibling)]

    def merge(k, _):
        rows = pl.ds(pl.multiple_of(k * CHUNK, CHUNK), CHUNK)
        pltpu.make_async_copy(grads.at[rows], gbuf.at[rows], load_sem.at[0, k]).wait()
        pltpu.make_async_copy(errors.at[rows], ebuf.at[rows], load_sem.at[1, k]).wait()

        def group(i, _):
            rows = pl.ds(pl.multiple_of(k * CHUNK + i * 16, 16), 16)
            total = jnp.zeros((16, 128), F32)
            for j in range(D // 768):
                cols = pl.ds(j * 768, 768)
                m = gbuf[rows, cols].astype(F32) + ebuf[rows, cols].astype(F32)
                gbuf[rows, cols] = m.astype(BF16)
                m2 = m * m
                for i2 in range(6):
                    total = total + m2[:, i2 * 128 : (i2 + 1) * 128]
            sq[...] += total[:8] + total[8:]
            return 0

        lax.fori_loop(0, CHUNK // 16, group, 0)
        return 0

    lax.fori_loop(0, 3, merge, 0)
    for d in (1, 3, 2):
        q1[d - 1].wait_recv()
        here = qh.at[c, s_me, mod4(t_me - d), filled]
        for e in (2, 1, 3):
            q2.append(send(here, here, q2s.at[d, e - 1], q2r.at[e - 1], along_s(e)))
        q3.append(send(here, here, q3s.at[d], q3r.at[d], sibling))
    lax.fori_loop(3, CHUNKS, merge, 0)
    def add_p(half, places, first=False):
        cols, right = [], []
        for s in places:
            right.append(qh[half, s].reshape(1024, RANK))
            for t in range(4):
                g = jnp.where(half == 0, t * 4 + s, s * 4 + t)
                cols.append(gbuf[:, pl.ds(pl.multiple_of(g * ROWS + half * 128, 128), 256)])
        term = jnp.dot(
            jnp.concatenate(cols, axis=1), jnp.concatenate(right, axis=0), preferred_element_type=F32
        )
        if first:
            pacc[...] = term
        else:
            pacc[...] += term

    add_p(c, [s_me], True)
    for copy in q3[:4]:
        copy.wait_recv()
    add_p(1 - c, [t_me])
    for d in (1, 3, 2):
        here = qh.at[c, mod4(s_me - d), :, filled]
        describe(here, here, q2s.at[0, 0], q2r.at[d - 1], sibling).wait_recv()
        q3.append(send(here, here, q3s.at[3 + d], q3r.at[3 + d], sibling))
    add_p(c, [mod4(s_me - d) for d in (1, 3, 2)])
    for copy in q3[4:]:
        copy.wait_recv()
    add_p(1 - c, [mod4(t_me - d) for d in (1, 3, 2)])
    sent += q1 + q2 + q3

    half_c = pl.ds(pl.multiple_of(c * HALF, HALF), HALF)
    other_half = pl.ds(pl.multiple_of((1 - c) * HALF, HALF), HALF)
    p1 = send(pacc.at[other_half], phalf, p1s, p1r, sibling)
    p1.wait_recv()
    pz[z] = (pacc[half_c, :] + phalf[...]).astype(BF16)
    p2 = [send(pz.at[z], pz.at[z], p2s.at[d - 1], p2r.at[d - 1], (f, at_z(d))) for d in (2, 1, 3)]
    for copy in p2:
        copy.wait_recv()
    total = pz[0].astype(F32)
    for k in range(1, 4):
        total = total + pz[k].astype(F32)
    pall[c] = total.astype(BF16)
    p3 = send(pall.at[c], pall.at[c], p3s, p3r, sibling)
    p3.wait_recv()
    sent += [p1, p3] + p2

    p_full = pall[...].reshape(ROWS, RANK)
    pt[...] = p_full.T

    slot = c * 4 + z
    my_rows = pl.ds(pl.multiple_of(slot * 16, 16), 16)
    gsend[0, :16] = jnp.dot(pt[my_rows, :], p_full, preferred_element_type=F32)
    gsend[0, 16:] = sq[...]
    gx = [
        send(gsend.at[0], gxr.at[k], gxs.at[k], gxq.at[k], (at_xy(dx, dy), r)) for k, (dx, dy) in enumerate(PLANE)
    ]

    core, s1 = {}, ([], [], [])
    order = ((z, x, y), (x, y, z), (y, z, x))

    def way(part, steps):
        dx, dy, dz = ((steps[1], steps[2], steps[0]), (steps[0], steps[1], steps[2]), (steps[2], steps[0], steps[1]))[
            part
        ]
        return (at_xy(dx, dy), at_z(dz))

    def multiply(part, places):
        cols = [
            gbuf[:, pl.ds(pl.multiple_of((x2 * 4 + y2) * ROWS + part * 128, 128), 128)] for x2, y2 in places
        ]
        block = jnp.dot(pt[...], jnp.concatenate(cols, axis=1), preferred_element_type=F32).astype(BF16)
        for k, (x2, y2) in enumerate(places):
            for c2 in (0, 1):
                for z2 in range(4):
                    at = c2 * 64 + z2 * 16
                    yl[c2, part, tile_of(part, x2, y2, z2)] = block[at : at + 16, k * 128 : (k + 1) * 128]

    def line(part, d):
        return pl.ds(pl.multiple_of(mod4(order[part][0] + d) * 16, 16), 16)

    def swap(part, d):
        at = line(part, d)
        core[part, d] = send(yl.at[1 - c, part, at], yr.at[part, at], cs.at[part, d], cr.at[part, d], sibling)

    def add_core(part, d):
        at = line(part, d)
        core[part, d].wait_recv()
        yc[part, at] = (yl[c, part, at].astype(F32) + yr[part, at].astype(F32)).astype(BF16)
        if d:
            s1[part].append(
                send(
                    yc.at[part, at],
                    rs1.at[part, d - 1],
                    r1s.at[part, d - 1],
                    r1r.at[part, d - 1],
                    way(part, (d, 0, 0)),
                )
            )

    def add_line(part):
        a0, a1, a2 = order[part]
        for copy in s1[part]:
            copy.wait_recv()
        value = yc[part, pl.ds(a0 * 16, 16)].astype(F32)
        for d in range(3):
            value = value + rs1[part, d].astype(F32)
        t1[part] = value.astype(BF16)
        return [
            send(
                t1.at[part, mod4(a1 + d) * 4 + mod4(a2 + e)],
                rs2.at[part, k],
                r2s.at[part],
                r2r.at[part],
                way(part, (0, d, e)),
            )
            for k, (d, e) in enumerate(PLANE)
        ]

    def add_plane(part):
        a0, a1, a2 = order[part]
        describe(rs2.at[part], rs2.at[part], r2s.at[part], r2r.at[part], sibling).wait_recv()
        value = t1[part, a1 * 4 + a2].astype(F32)
        for k in range(15):
            value = value + rs2[part, k].astype(F32)
        mine = a0 * 16 + a1 * 4 + a2
        gy[c, part, mine] = value.astype(BF16)
        here = gy.at[c, part, mine]
        for d, e in PLANE:
            send(here, here, a1s.at[part], a1r.at[part, d], way(part, (0, d, e)))

    for j in range(4):
        multiply(0, [(j, k) for k in range(4)])
    for d in FAR:
        swap(0, d)

    def begin(part, d):
        multiply(part, [(mod4(x + d), k) for k in range(4)] if part == 1 else [(k, mod4(y + d)) for k in range(4)])
        swap(part, d)

    for d in (2, 1, 3):
        begin(1, d)
        begin(2, d)
        add_core(0, d)
    for d in (2, 1, 3):
        add_core(1, d)
        add_core(2, d)
    begin(1, 0)
    begin(2, 0)
    for part in range(3):
        add_core(part, 0)

    add_line(0)
    for copy in gx:
        copy.wait_recv()
    gsum = gsend[0]
    for k in range(15):
        gsum = gsum + gxr[k]
    gmat[slot] = gsum
    g2 = [send(gmat.at[slot], gmat.at[slot], g2s.at[d - 1], g2r.at[d - 1], (f, at_z(d))) for d in (1, 2, 3)]
    add_line(1)
    add_line(2)
    for copy in g2:
        copy.wait_recv()
    side = gmat.at[pl.ds(c * 4, 4)]
    g3 = send(side, side, g3s.at[0], g3r.at[0], sibling)
    for part in range(3):
        add_plane(part)

    g3.wait_recv()
    for k in range(8):
        aug[k * 16 : (k + 1) * 16, :RANK] = gmat[k, :16]
    rows_i = lax.broadcasted_iota(jnp.int32, (RANK, RANK), 0)
    cols_i = lax.broadcasted_iota(jnp.int32, (RANK, RANK), 1)
    aug[:, RANK:] = jnp.where(rows_i == cols_i, 1.0, 0.0).astype(F32)
    sub = lax.broadcasted_iota(jnp.int32, (8, 128), 0)

    def spread_row(v, i):
        return jnp.broadcast_to(v[i : i + 1, :], (8, 128))

    def panel(k, _):
        base = pl.multiple_of(k * 16, 16)
        halves = (pl.ds(base, 8), pl.ds(base + 8, 8))
        rowp = [aug[at, :RANK] for at in halves]
        ext = [aug[at, RANK:] for at in halves]
        turned = [pltpu.roll(v, lax.rem(128 - base, 128), 1) for v in rowp]
        col = [[jnp.broadcast_to(v[:, j : j + 1], (8, 128)) for v in turned] for j in range(16)]
        diag = [jnp.ones((8, 128), F32)] * 2
        for j in range(16):
            top, i = j // 8, j % 8
            pivot = spread_row(col[j][top], i)
            inv = 1.0 / pivot
            low = [None, None]
            for h in range(top, 2):
                low[h] = col[j][h] * inv
            low[top] = jnp.where(sub > i, low[top], 0.0)
            pivots = [spread_row(col[m][top], i) for m in range(j + 1, 16)]
            row_r, row_e = spread_row(rowp[top], i), spread_row(ext[top], i)
            for h in range(top, 2):
                for m in range(j + 1, 16):
                    col[m][h] = col[m][h] - low[h] * pivots[m - j - 1]
                rowp[h] = rowp[h] - low[h] * row_r
                ext[h] = ext[h] - low[h] * row_e
            diag[top] = jnp.where(sub == i, pivot, diag[top])
        for h in (0, 1):
            inv = lax.rsqrt(diag[h])
            inv = inv * (1.5 - 0.5 * diag[h] * inv * inv)
            rowp[h] = rowp[h] * inv
            ext[h] = ext[h] * inv
            wbuf[halves[h], :] = ext[h]
        v1, v2, v3 = split3(jnp.concatenate(rowp, axis=0))
        e1, e2, e3 = split3(jnp.concatenate(ext, axis=0))
        left = jnp.concatenate([v1, v1, v2, v2, v1, v3], axis=0).T.astype(BF16)
        top = jnp.concatenate([v1, v2, v1, v2, v3, v1], axis=0)
        more = jnp.concatenate([e1, e2, e1, e2, e3, e1], axis=0)
        both = jnp.concatenate([top, more], axis=1).astype(BF16)
        aug[...] -= jnp.dot(left, both, preferred_element_type=F32)
        return 0

    lines, passed = [], []

    def spread(part):
        a0, a1, _ = order[part]
        for d in FAR:
            region = rs2.at[part, pl.ds(0, 4 if d else 3)]
            describe(region, region, a1s.at[part], a1r.at[part, d], sibling).wait_recv()
            here = gy.at[c, part, pl.ds(a0 * 16 + mod4(a1 - d) * 4, 4)]
            for e in (2, 1, 3):
                send(here, here, a2s.at[part, e - 1], a2r.at[part, e - 1], way(part, (e, 0, 0)))
            send(here, here, fs.at[part, 0], fr.at[part, 0], sibling)
        here = gy.at[c, part, pl.ds(a0 * 16, 16)]
        lines.append([describe(here, here, a2s.at[part, e], a2r.at[part, e], sibling) for e in range(3)])
        passed.append([describe(here, here, fs.at[part, 0], fr.at[part, 0], sibling)])

    lax.fori_loop(0, 3, panel, 0)
    spread(0)
    lax.fori_loop(3, 4, panel, 0)
    spread(1)
    lax.fori_loop(4, 5, panel, 0)
    spread(2)
    lax.fori_loop(5, 8, panel, 0)

    w = wbuf[...]
    pb = jnp.zeros((ROWS, RANK), F32)
    p_again = pall[...].reshape(ROWS, RANK)
    for piece in split3(w)[::-1]:
        pb = pb + lax.dot_general(
            p_again, piece.astype(BF16), (((1,), (1,)), ((), ())), preferred_element_type=F32
        )
    basis_ref[...] = pb
    bmat[...] = (
        jnp.dot(pb, w, preferred_element_type=F32, precision=lax.Precision.HIGHEST) * 0.125
    ).astype(BF16)

    for group_of in s1:
        sent += group_of
    for copy in sent + gx + g2 + [g3] + list(core.values()):
        copy.wait_send()
    for part in range(3):
        region = rs2.at[part]
        for sems in (r2s, a1s):
            describe(region, region, sems.at[part], r2r.at[part], sibling).wait_send()

    squares = jnp.sum(jnp.sum(gmat[:, 16:], axis=0))
    root_mean = jnp.sqrt(jnp.full((1, RANK), squares) / (8 * D * D) + 1e-06)
    w_ref[...] = wbuf[...] * (jnp.minimum(1.0, clip_ref[0, 0] / root_mean) * 0.125)

    for d in (1, 3, 2):
        for part in range(3):
            lines[part][d - 1].wait_recv()
            here = gy.at[c, part, pl.ds(mod4(order[part][0] - d) * 16, 16)]
            passed[part].append(send(here, here, fs.at[part, d], fr.at[part, d], sibling))
    for group_of in passed:
        for copy in group_of:
            copy.wait_recv()
    for group_of in lines + passed:
        for copy in group_of:
            copy.wait_send()


def update(merged, gy, bmat, basis, w_ref, new_out, basis_out, q_out, new, q_buf, sems):
    f = lax.axis_index("fsdp")
    x, y = f // 4, lax.rem(f, 4)

    def right(part, x2, y2):
        tiles = [gy[c2, part, tile_of(part, x2, y2, z2)] for c2 in (0, 1) for z2 in range(4)]
        return jnp.concatenate(tiles, axis=0)

    copies = [pltpu.make_async_copy(basis, basis_out, sems.at[CHUNKS])]
    copies[0].start()
    for j in range(CHUNKS):
        cols = pl.ds(j * 768, 768)
        places = [((2 * j + k) // 4, (2 * j + k) % 4) for k in (0, 1)]
        block = jnp.concatenate([right(part, x2, y2) for x2, y2 in places for part in range(3)], axis=1)
        low = jnp.dot(bmat[...], block, preferred_element_type=F32)
        new[:, cols] = (merged[:, cols].astype(F32) - low).astype(BF16)
        copies.append(pltpu.make_async_copy(new.at[:, cols], new_out.at[:, cols], sems.at[j]))
        copies[-1].start()
    block = jnp.concatenate([right(part, x, y) for part in range(3)], axis=1)
    value = jnp.zeros((RANK, ROWS), F32)
    for piece in split3(w_ref[...])[::-1]:
        value = value + jnp.dot(piece.astype(BF16), block, preferred_element_type=F32)
    q_buf[...] = value.T
    copies.append(pltpu.make_async_copy(q_buf, q_out, sems.at[CHUNKS + 1]))
    copies[-1].start()
    for copy in copies:
        copy.wait()


def body(grads, errors, q_start, clip_rms):
    dma = pltpu.SemaphoreType.DMA
    vmem = pltpu.VMEM
    hbm = pl.BlockSpec(memory_space=pltpu.HBM)
    inside = pl.BlockSpec(memory_space=pltpu.VMEM)
    merged, gy, bmat, basis, w = pl.pallas_call(
        exchange,
        out_shape=(
            vmem((ROWS, D), BF16),
            vmem((2, 3, 64, 16, 128), BF16),
            vmem((ROWS, RANK), BF16),
            vmem((ROWS, RANK), F32),
            vmem((RANK, RANK), F32),
        ),
        in_specs=[pl.BlockSpec(memory_space=pltpu.SMEM), hbm, hbm, hbm],
        out_specs=(inside,) * 5,
        scratch_shapes=[
            vmem((ROWS, D), BF16),
            vmem((HALF, RANK), F32),
            vmem((2, 4, 4, 256, RANK), BF16),
            vmem((ROWS, RANK), F32),
            vmem((8, 128), F32),
            vmem((HALF, RANK), F32),
            vmem((4, HALF, RANK), BF16),
            vmem((2, HALF, RANK), BF16),
            vmem((RANK, ROWS), BF16),
            vmem((2, 24, RANK), F32),
            vmem((15, 24, RANK), F32),
            vmem((3, 24, RANK), F32),
            vmem((8, 24, RANK), F32),
            vmem((RANK, 2 * RANK), F32),
            vmem((RANK, RANK), F32),
            vmem((2, 3, 64, 16, 128), BF16),
            vmem((3, 64, 16, 128), BF16),
            vmem((3, 64, 16, 128), BF16),
            vmem((3, 3, 16, 16, 128), BF16),
            vmem((3, 16, 16, 128), BF16),
            vmem((3, 15, 16, 128), BF16),
            dma((2, CHUNKS)),
            dma(()),
            dma((3,)),
            dma((3,)),
            dma((4, 3)),
            dma((3,)),
            dma((7,)),
            dma((7,)),
            dma(()),
            dma(()),
            dma((3,)),
            dma((3,)),
            dma(()),
            dma(()),
            dma((15,)),
            dma((15,)),
            dma((3,)),
            dma((3,)),
            dma((3,)),
            dma((3,)),
            dma((1,)),
            dma((1,)),
            dma((3, 4)),
            dma((3, 4)),
            dma((3, 3)),
            dma((3, 3)),
            dma((3, 3)),
            dma((3, 3)),
            dma((3,)),
            dma((3,)),
            dma((3,)),
            dma((3, 4)),
            dma((3, 4)),
            dma((3, 4)),
        ],
        compiler_params=pltpu.CompilerParams(
            collective_id=0, has_side_effects=True, vmem_limit_bytes=40 * 1024 * 1024
        ),
        name="exchange",
    )(clip_rms.reshape(1, 1), *[pltpu.with_memory_space_constraint(v, pltpu.HBM) for v in (grads[0], errors[0], q_start)])
    new_errors, basis, q_out = pl.pallas_call(
        update,
        out_shape=(
            jax.ShapeDtypeStruct((ROWS, D), BF16),
            jax.ShapeDtypeStruct((ROWS, RANK), F32),
            jax.ShapeDtypeStruct((ROWS, RANK), F32),
        ),
        in_specs=[inside] * 5,
        out_specs=(pl.BlockSpec(memory_space=pl.ANY),) * 3,
        scratch_shapes=[vmem((ROWS, D), BF16), vmem((ROWS, RANK), F32), dma((CHUNKS + 2,))],
        compiler_params=pltpu.CompilerParams(vmem_limit_bytes=24 * 1024 * 1024),
        name="update",
    )(*[pltpu.with_memory_space_constraint(v, pltpu.VMEM) for v in (merged, gy, bmat, basis, w)])
    return new_errors[None], basis, q_out


def solution(mesh):
    return jax.shard_map(
        body,
        mesh=mesh,
        in_specs=(P("replica", "fsdp", None), P("replica", "fsdp", None), P("fsdp", None), P()),
        out_specs=(P("replica", "fsdp", None), P("fsdp", None), P("fsdp", None)),
        check_vma=False,
    )
```

```python
import jax
import jax.numpy as jnp
from jax import lax
from jax.experimental import pallas as pl
from jax.experimental.pallas import tpu as pltpu
from jax.sharding import PartitionSpec as P

MESH = pl.DeviceIdType.MESH
F32 = jnp.float32
BF16 = jnp.bfloat16

ROWS = 384
D = 6144
RANK = 128
CHUNKS = 8
CHUNK = ROWS // CHUNKS
HALF = ROWS // 2
FAR = (2, 1, 3, 0)
PLANE = [(d, e) for d in FAR for e in FAR][:-1]


def mod4(v):
    return lax.rem(v + 4, 4)


def split3(v):
    a = v.astype(BF16).astype(F32)
    b = (v - a).astype(BF16).astype(F32)
    return a, b, (v - a - b).astype(BF16).astype(F32)


def tile_of(part, x, y, z):
    return (z * 16 + x * 4 + y, x * 16 + y * 4 + z, y * 16 + z * 4 + x)[part]


def exchange(
    clip_ref,
    grads,
    errors,
    q_ref,
    gbuf,
    gy,
    bmat,
    basis_ref,
    w_ref,
    ebuf,
    qin,
    qh,
    pacc,
    sq,
    phalf,
    pz,
    pall,
    pt,
    gsend,
    gxr,
    gyr,
    gmat,
    aug,
    wbuf,
    yl,
    yr,
    yc,
    rs1,
    t1,
    rs2,
    load_sem,
    qin_sem,
    q1s,
    q1r,
    q2s,
    q2r,
    q3s,
    q3r,
    p1s,
    p1r,
    p2s,
    p2r,
    p3s,
    p3r,
    gxs,
    gxq,
    gys,
    gyq,
    g2s,
    g2r,
    g3s,
    g3r,
    cs,
    cr,
    r1s,
    r1r,
    a2s,
    a2r,
    r2s,
    r2r,
    a1s,
    a1r,
    fs,
    fr,
):
    f = lax.axis_index("fsdp")
    r = lax.axis_index("replica")
    x, y, z, c = f // 4, lax.rem(f, 4), r // 2, lax.rem(r, 2)
    sibling = (f, z * 2 + 1 - c)

    xs = [mod4(x + d) * 4 for d in range(4)]
    ys = [mod4(y + d) for d in range(4)]
    zs = [mod4(z + d) * 2 + c for d in range(4)]

    def at_xy(dx, dy):
        return xs[dx] + ys[dy]

    def at_z(dz):
        return zs[dz]

    def describe(src, dst, ssem, rsem, device):
        return pltpu.make_async_remote_copy(
            src_ref=src, dst_ref=dst, send_sem=ssem, recv_sem=rsem, device_id=device, device_id_type=MESH
        )

    def send(src, dst, ssem, rsem, device):
        copy = describe(src, dst, ssem, rsem, device)
        copy.start()
        return copy

    sent = []

    qload = pltpu.make_async_copy(q_ref.at[pl.ds(pl.multiple_of(c * HALF, HALF), HALF)], qin, qin_sem)
    qload.start()

    barrier = pltpu.get_barrier_semaphore()
    peers = []
    for d in (2, 1, 3):
        peers += [(at_xy(d, 0), r), (at_xy(0, d), r)]
    peers.append(sibling)
    for d in (2, 1, 3):
        peers.append((f, at_z(d)))
    for device in peers:
        pl.semaphore_signal(barrier, inc=1, device_id=device, device_id_type=MESH)

    for k in range(CHUNKS):
        rows = pl.ds(k * CHUNK, CHUNK)
        pltpu.make_async_copy(grads.at[rows], gbuf.at[rows], load_sem.at[0, k]).start()
        pltpu.make_async_copy(errors.at[rows], ebuf.at[rows], load_sem.at[1, k]).start()

    s_me, t_me = jnp.where(c == 0, y, x), jnp.where(c == 0, x, y)
    qload.wait()
    filled = pl.ds(pl.multiple_of(c * 64, 64), HALF)
    for s in range(4):
        for t in range(4):
            qh[0, s, t, HALF:] = jnp.zeros((64, RANK), BF16)
            qh[1, s, t, :64] = jnp.zeros((64, RANK), BF16)
    qh[c, s_me, t_me, filled] = qin[...].astype(BF16)
    sq[...] = jnp.zeros_like(sq)
    pl.semaphore_wait(barrier, len(peers))

    def along_t(d):
        return (jnp.where(c == 0, at_xy(d, 0), at_xy(0, d)), r)

    def along_s(d):
        return (jnp.where(c == 0, at_xy(0, d), at_xy(d, 0)), r)

    own = qh.at[c, s_me, t_me, filled]
    q1 = [send(own, own, q1s.at[d - 1], q1r.at[d - 1], along_t(d)) for d in (1, 2, 3)]
    q2 = [send(own, own, q2s.at[0, d - 1], q2r.at[d - 1], along_s(d)) for d in (1, 2, 3)]
    q3 = [send(own, own, q3s.at[0], q3r.at[0], sibling)]

    def merge(k, _):
        rows = pl.ds(pl.multiple_of(k * CHUNK, CHUNK), CHUNK)
        pltpu.make_async_copy(grads.at[rows], gbuf.at[rows], load_sem.at[0, k]).wait()
        pltpu.make_async_copy(errors.at[rows], ebuf.at[rows], load_sem.at[1, k]).wait()

        def group(i, _):
            rows = pl.ds(pl.multiple_of(k * CHUNK + i * 16, 16), 16)
            total = jnp.zeros((16, 128), F32)
            for j in range(D // 768):
                cols = pl.ds(j * 768, 768)
                m = gbuf[rows, cols].astype(F32) + ebuf[rows, cols].astype(F32)
                gbuf[rows, cols] = m.astype(BF16)
                m2 = m * m
                for i2 in range(6):
                    total = total + m2[:, i2 * 128 : (i2 + 1) * 128]
            sq[...] += total[:8] + total[8:]
            return 0

        lax.fori_loop(0, CHUNK // 16, group, 0)
        return 0

    lax.fori_loop(0, 3, merge, 0)
    for d in (1, 3, 2):
        q1[d - 1].wait_recv()
        here = qh.at[c, s_me, mod4(t_me - d), filled]
        for e in (2, 1, 3):
            q2.append(send(here, here, q2s.at[d, e - 1], q2r.at[e - 1], along_s(e)))
        q3.append(send(here, here, q3s.at[d], q3r.at[d], sibling))
    lax.fori_loop(3, CHUNKS, merge, 0)
    def add_p(half, places, first=False):
        cols, right = [], []
        for s in places:
            right.append(qh[half, s].reshape(1024, RANK))
            for t in range(4):
                g = jnp.where(half == 0, t * 4 + s, s * 4 + t)
                cols.append(gbuf[:, pl.ds(pl.multiple_of(g * ROWS + half * 128, 128), 256)])
        term = jnp.dot(
            jnp.concatenate(cols, axis=1), jnp.concatenate(right, axis=0), preferred_element_type=F32
        )
        if first:
            pacc[...] = term
        else:
            pacc[...] += term

    add_p(c, [s_me], True)
    for copy in q3[:4]:
        copy.wait_recv()
    add_p(1 - c, [t_me])
    for d in (1, 3, 2):
        here = qh.at[c, mod4(s_me - d), :, filled]
        describe(here, here, q2s.at[0, 0], q2r.at[d - 1], sibling).wait_recv()
        q3.append(send(here, here, q3s.at[3 + d], q3r.at[3 + d], sibling))
    add_p(c, [mod4(s_me - d) for d in (1, 3, 2)])
    for copy in q3[4:]:
        copy.wait_recv()
    add_p(1 - c, [mod4(t_me - d) for d in (1, 3, 2)])
    sent += q1 + q2 + q3

    half_c = pl.ds(pl.multiple_of(c * HALF, HALF), HALF)
    other_half = pl.ds(pl.multiple_of((1 - c) * HALF, HALF), HALF)
    p1 = send(pacc.at[other_half], phalf, p1s, p1r, sibling)
    p1.wait_recv()
    pz[z] = (pacc[half_c, :] + phalf[...]).astype(BF16)
    p2 = [send(pz.at[z], pz.at[z], p2s.at[d - 1], p2r.at[d - 1], (f, at_z(d))) for d in (2, 1, 3)]
    for copy in p2:
        copy.wait_recv()
    total = pz[0].astype(F32)
    for k in range(1, 4):
        total = total + pz[k].astype(F32)
    pall[c] = total.astype(BF16)
    p3 = send(pall.at[c], pall.at[c], p3s, p3r, sibling)
    p3.wait_recv()
    sent += [p1, p3] + p2

    p_full = pall[...].reshape(ROWS, RANK)
    pt[...] = p_full.T

    slot = c * 4 + z
    my_rows = pl.ds(pl.multiple_of(slot * 16, 16), 16)
    gsend[0, :16] = jnp.dot(pt[my_rows, :], p_full, preferred_element_type=F32)
    gsend[0, 16:] = sq[...]
    gx = [
        send(gsend.at[0], gxr.at[k], gxs.at[k], gxq.at[k], (at_xy(dx, dy), r)) for k, (dx, dy) in enumerate(PLANE)
    ]

    core, s1 = {}, ([], [], [])
    order = ((z, x, y), (x, y, z), (y, z, x))

    def way(part, steps):
        dx, dy, dz = ((steps[1], steps[2], steps[0]), (steps[0], steps[1], steps[2]), (steps[2], steps[0], steps[1]))[
            part
        ]
        return (at_xy(dx, dy), at_z(dz))

    def multiply(part, places):
        cols = [
            gbuf[:, pl.ds(pl.multiple_of((x2 * 4 + y2) * ROWS + part * 128, 128), 128)] for x2, y2 in places
        ]
        block = jnp.dot(pt[...], jnp.concatenate(cols, axis=1), preferred_element_type=F32).astype(BF16)
        for k, (x2, y2) in enumerate(places):
            for c2 in (0, 1):
                for z2 in range(4):
                    at = c2 * 64 + z2 * 16
                    yl[c2, part, tile_of(part, x2, y2, z2)] = block[at : at + 16, k * 128 : (k + 1) * 128]

    def line(part, d):
        return pl.ds(pl.multiple_of(mod4(order[part][0] + d) * 16, 16), 16)

    def swap(part, d):
        at = line(part, d)
        core[part, d] = send(yl.at[1 - c, part, at], yr.at[part, at], cs.at[part, d], cr.at[part, d], sibling)

    def add_core(part, d):
        at = line(part, d)
        core[part, d].wait_recv()
        yc[part, at] = (yl[c, part, at].astype(F32) + yr[part, at].astype(F32)).astype(BF16)
        if d:
            s1[part].append(
                send(
                    yc.at[part, at],
                    rs1.at[part, d - 1],
                    r1s.at[part, d - 1],
                    r1r.at[part, d - 1],
                    way(part, (d, 0, 0)),
                )
            )

    def add_line(part):
        a0, a1, a2 = order[part]
        for copy in s1[part]:
            copy.wait_recv()
        value = yc[part, pl.ds(a0 * 16, 16)].astype(F32)
        for d in range(3):
            value = value + rs1[part, d].astype(F32)
        t1[part] = value.astype(BF16)
        return [
            send(
                t1.at[part, mod4(a1 + d) * 4 + mod4(a2 + e)],
                rs2.at[part, k],
                r2s.at[part],
                r2r.at[part],
                way(part, (0, d, e)),
            )
            for k, (d, e) in enumerate(PLANE)
        ]

    def add_plane(part):
        a0, a1, a2 = order[part]
        describe(rs2.at[part], rs2.at[part], r2s.at[part], r2r.at[part], sibling).wait_recv()
        value = t1[part, a1 * 4 + a2].astype(F32)
        for k in range(15):
            value = value + rs2[part, k].astype(F32)
        mine = a0 * 16 + a1 * 4 + a2
        gy[c, part, mine] = value.astype(BF16)
        here = gy.at[c, part, mine]
        for d, e in PLANE:
            send(here, here, a1s.at[part], a1r.at[part, d], way(part, (0, d, e)))

    for j in range(4):
        multiply(0, [(j, k) for k in range(4)])
    for d in FAR:
        swap(0, d)

    def begin(part, d):
        multiply(part, [(mod4(x + d), k) for k in range(4)] if part == 1 else [(k, mod4(y + d)) for k in range(4)])
        swap(part, d)

    for d in (2, 1, 3):
        begin(1, d)
        begin(2, d)
        add_core(0, d)
    for d in (2, 1, 3):
        add_core(1, d)
        add_core(2, d)
    begin(1, 0)
    begin(2, 0)
    for part in range(3):
        add_core(part, 0)

    add_line(0)
    add_line(1)
    add_line(2)
    for copy in gx:
        copy.wait_recv()
    gsum = gsend[0]
    for k in range(15):
        gsum = gsum + gxr[k]
    gmat[slot] = gsum
    g2 = [send(gmat.at[slot], gmat.at[slot], g2s.at[d - 1], g2r.at[d - 1], (f, at_z(d))) for d in (1, 2, 3)]
    add_plane(0)
    add_plane(1)
    for copy in g2:
        copy.wait_recv()
    side = gmat.at[pl.ds(c * 4, 4)]
    g3 = send(side, side, g3s.at[0], g3r.at[0], sibling)
    add_plane(2)

    g3.wait_recv()
    for k in range(8):
        aug[k * 16 : (k + 1) * 16, :RANK] = gmat[k, :16]
    rows_i = lax.broadcasted_iota(jnp.int32, (RANK, RANK), 0)
    cols_i = lax.broadcasted_iota(jnp.int32, (RANK, RANK), 1)
    aug[:, RANK:] = jnp.where(rows_i == cols_i, 1.0, 0.0).astype(F32)
    sub = lax.broadcasted_iota(jnp.int32, (8, 128), 0)

    def spread_row(v, i):
        return jnp.broadcast_to(v[i : i + 1, :], (8, 128))

    def panel(k, _):
        base = pl.multiple_of(k * 16, 16)
        halves = (pl.ds(base, 8), pl.ds(base + 8, 8))
        rowp = [aug[at, :RANK] for at in halves]
        ext = [aug[at, RANK:] for at in halves]
        turned = [pltpu.roll(v, lax.rem(128 - base, 128), 1) for v in rowp]
        col = [[jnp.broadcast_to(v[:, j : j + 1], (8, 128)) for v in turned] for j in range(16)]
        diag = [jnp.ones((8, 128), F32)] * 2
        for j in range(16):
            top, i = j // 8, j % 8
            pivot = spread_row(col[j][top], i)
            inv = 1.0 / pivot
            low = [None, None]
            for h in range(top, 2):
                low[h] = col[j][h] * inv
            low[top] = jnp.where(sub > i, low[top], 0.0)
            pivots = [spread_row(col[m][top], i) for m in range(j + 1, 16)]
            row_r, row_e = spread_row(rowp[top], i), spread_row(ext[top], i)
            for h in range(top, 2):
                for m in range(j + 1, 16):
                    col[m][h] = col[m][h] - low[h] * pivots[m - j - 1]
                rowp[h] = rowp[h] - low[h] * row_r
                ext[h] = ext[h] - low[h] * row_e
            diag[top] = jnp.where(sub == i, pivot, diag[top])
        for h in (0, 1):
            inv = lax.rsqrt(diag[h])
            inv = inv * (1.5 - 0.5 * diag[h] * inv * inv)
            rowp[h] = rowp[h] * inv
            ext[h] = ext[h] * inv
            wbuf[halves[h], :] = ext[h]
        v1, v2, v3 = split3(jnp.concatenate(rowp, axis=0))
        e1, e2, e3 = split3(jnp.concatenate(ext, axis=0))
        left = jnp.concatenate([v1, v1, v2, v2, v1, v3], axis=0).T.astype(BF16)
        top = jnp.concatenate([v1, v2, v1, v2, v3, v1], axis=0)
        more = jnp.concatenate([e1, e2, e1, e2, e3, e1], axis=0)
        both = jnp.concatenate([top, more], axis=1).astype(BF16)
        aug[...] -= jnp.dot(left, both, preferred_element_type=F32)
        return 0

    lines, passed = [], []

    def spread(part):
        a0, a1, _ = order[part]
        for d in FAR:
            region = rs2.at[part, pl.ds(0, 4 if d else 3)]
            describe(region, region, a1s.at[part], a1r.at[part, d], sibling).wait_recv()
            here = gy.at[c, part, pl.ds(a0 * 16 + mod4(a1 - d) * 4, 4)]
            for e in (2, 1, 3):
                send(here, here, a2s.at[part, e - 1], a2r.at[part, e - 1], way(part, (e, 0, 0)))
            send(here, here, fs.at[part, 0], fr.at[part, 0], sibling)
        here = gy.at[c, part, pl.ds(a0 * 16, 16)]
        lines.append([describe(here, here, a2s.at[part, e], a2r.at[part, e], sibling) for e in range(3)])
        passed.append([describe(here, here, fs.at[part, 0], fr.at[part, 0], sibling)])

    lax.fori_loop(0, 3, panel, 0)
    spread(0)
    lax.fori_loop(3, 4, panel, 0)
    spread(1)
    lax.fori_loop(4, 5, panel, 0)
    spread(2)
    lax.fori_loop(5, 8, panel, 0)

    w = wbuf[...]
    pb = jnp.zeros((ROWS, RANK), F32)
    p_again = pall[...].reshape(ROWS, RANK)
    for piece in split3(w)[::-1]:
        pb = pb + lax.dot_general(
            p_again, piece.astype(BF16), (((1,), (1,)), ((), ())), preferred_element_type=F32
        )
    basis_ref[...] = pb
    bmat[...] = (
        jnp.dot(pb, w, preferred_element_type=F32, precision=lax.Precision.HIGHEST) * 0.125
    ).astype(BF16)

    for group_of in s1:
        sent += group_of
    for copy in sent + gx + g2 + [g3] + list(core.values()):
        copy.wait_send()
    for part in range(3):
        region = rs2.at[part]
        for sems in (r2s, a1s):
            describe(region, region, sems.at[part], r2r.at[part], sibling).wait_send()

    squares = jnp.sum(jnp.sum(gmat[:, 16:], axis=0))
    root_mean = jnp.sqrt(jnp.full((1, RANK), squares) / (8 * D * D) + 1e-06)
    w_ref[...] = wbuf[...] * (jnp.minimum(1.0, clip_ref[0, 0] / root_mean) * 0.125)

    for d in (1, 3, 2):
        for part in range(3):
            lines[part][d - 1].wait_recv()
            here = gy.at[c, part, pl.ds(mod4(order[part][0] - d) * 16, 16)]
            passed[part].append(send(here, here, fs.at[part, d], fr.at[part, d], sibling))
    for group_of in passed:
        for copy in group_of:
            copy.wait_recv()
    for group_of in lines + passed:
        for copy in group_of:
            copy.wait_send()


def update(merged, gy, bmat, basis, w_ref, new_out, basis_out, q_out, new, q_buf, sems):
    f = lax.axis_index("fsdp")
    x, y = f // 4, lax.rem(f, 4)

    def right(part, x2, y2):
        tiles = [gy[c2, part, tile_of(part, x2, y2, z2)] for c2 in (0, 1) for z2 in range(4)]
        return jnp.concatenate(tiles, axis=0)

    copies = [pltpu.make_async_copy(basis, basis_out, sems.at[CHUNKS])]
    copies[0].start()
    for j in range(CHUNKS):
        cols = pl.ds(j * 768, 768)
        places = [((2 * j + k) // 4, (2 * j + k) % 4) for k in (0, 1)]
        block = jnp.concatenate([right(part, x2, y2) for x2, y2 in places for part in range(3)], axis=1)
        low = jnp.dot(bmat[...], block, preferred_element_type=F32)
        new[:, cols] = (merged[:, cols].astype(F32) - low).astype(BF16)
        copies.append(pltpu.make_async_copy(new.at[:, cols], new_out.at[:, cols], sems.at[j]))
        copies[-1].start()
    block = jnp.concatenate([right(part, x, y) for part in range(3)], axis=1)
    value = jnp.zeros((RANK, ROWS), F32)
    for piece in split3(w_ref[...])[::-1]:
        value = value + jnp.dot(piece.astype(BF16), block, preferred_element_type=F32)
    q_buf[...] = value.T
    copies.append(pltpu.make_async_copy(q_buf, q_out, sems.at[CHUNKS + 1]))
    copies[-1].start()
    for copy in copies:
        copy.wait()


def body(grads, errors, q_start, clip_rms):
    dma = pltpu.SemaphoreType.DMA
    vmem = pltpu.VMEM
    hbm = pl.BlockSpec(memory_space=pltpu.HBM)
    inside = pl.BlockSpec(memory_space=pltpu.VMEM)
    merged, gy, bmat, basis, w = pl.pallas_call(
        exchange,
        out_shape=(
            vmem((ROWS, D), BF16),
            vmem((2, 3, 64, 16, 128), BF16),
            vmem((ROWS, RANK), BF16),
            vmem((ROWS, RANK), F32),
            vmem((RANK, RANK), F32),
        ),
        in_specs=[pl.BlockSpec(memory_space=pltpu.SMEM), hbm, hbm, hbm],
        out_specs=(inside,) * 5,
        scratch_shapes=[
            vmem((ROWS, D), BF16),
            vmem((HALF, RANK), F32),
            vmem((2, 4, 4, 256, RANK), BF16),
            vmem((ROWS, RANK), F32),
            vmem((8, 128), F32),
            vmem((HALF, RANK), F32),
            vmem((4, HALF, RANK), BF16),
            vmem((2, HALF, RANK), BF16),
            vmem((RANK, ROWS), BF16),
            vmem((2, 24, RANK), F32),
            vmem((15, 24, RANK), F32),
            vmem((3, 24, RANK), F32),
            vmem((8, 24, RANK), F32),
            vmem((RANK, 2 * RANK), F32),
            vmem((RANK, RANK), F32),
            vmem((2, 3, 64, 16, 128), BF16),
            vmem((3, 64, 16, 128), BF16),
            vmem((3, 64, 16, 128), BF16),
            vmem((3, 3, 16, 16, 128), BF16),
            vmem((3, 16, 16, 128), BF16),
            vmem((3, 15, 16, 128), BF16),
            dma((2, CHUNKS)),
            dma(()),
            dma((3,)),
            dma((3,)),
            dma((4, 3)),
            dma((3,)),
            dma((7,)),
            dma((7,)),
            dma(()),
            dma(()),
            dma((3,)),
            dma((3,)),
            dma(()),
            dma(()),
            dma((15,)),
            dma((15,)),
            dma((3,)),
            dma((3,)),
            dma((3,)),
            dma((3,)),
            dma((1,)),
            dma((1,)),
            dma((3, 4)),
            dma((3, 4)),
            dma((3, 3)),
            dma((3, 3)),
            dma((3, 3)),
            dma((3, 3)),
            dma((3,)),
            dma((3,)),
            dma((3,)),
            dma((3, 4)),
            dma((3, 4)),
            dma((3, 4)),
        ],
        compiler_params=pltpu.CompilerParams(
            collective_id=0, has_side_effects=True, vmem_limit_bytes=40 * 1024 * 1024
        ),
        name="exchange",
    )(clip_rms.reshape(1, 1), *[pltpu.with_memory_space_constraint(v, pltpu.HBM) for v in (grads[0], errors[0], q_start)])
    new_errors, basis, q_out = pl.pallas_call(
        update,
        out_shape=(
            jax.ShapeDtypeStruct((ROWS, D), BF16),
            jax.ShapeDtypeStruct((ROWS, RANK), F32),
            jax.ShapeDtypeStruct((ROWS, RANK), F32),
        ),
        in_specs=[inside] * 5,
        out_specs=(pl.BlockSpec(memory_space=pl.ANY),) * 3,
        scratch_shapes=[vmem((ROWS, D), BF16), vmem((ROWS, RANK), F32), dma((CHUNKS + 2,))],
        compiler_params=pltpu.CompilerParams(vmem_limit_bytes=24 * 1024 * 1024),
        name="update",
    )(*[pltpu.with_memory_space_constraint(v, pltpu.VMEM) for v in (merged, gy, bmat, basis, w)])
    return new_errors[None], basis, q_out


def solution(mesh):
    return jax.shard_map(
        body,
        mesh=mesh,
        in_specs=(P("replica", "fsdp", None), P("replica", "fsdp", None), P("fsdp", None), P()),
        out_specs=(P("replica", "fsdp", None), P("fsdp", None), P("fsdp", None)),
        check_vma=False,
    )
```
